32 devices in a mesh: dp: 16 (over z, x, core), tensor: 2 (over y).
Axes of the slice: x: 2, y: 2, z: 4, core: 2. Of those that a mesh axis runs over, the one named last changes fastest.
Arguments:
- tokens: bfloat16 [32768, 512], P(('dp', 'tensor')), may hold values from -6 to 6
- segments: int32 [64, 512], P('dp'), may hold values from 0 to 7, never falling along the last dimension, each value on 1 to 256 neighbouring positions
- positions: bfloat16 [512, 512], replicated, may hold values from -3 to 3
- heads_weight: bfloat16 [512, 3, 512], P(None, None, 'tensor'), may hold values from -0.25 to 0.25
- merge_weight: bfloat16 [512, 512], P('tensor'), may hold values from -1 to 1
- merge_bias: bfloat16 [512], replicated, may hold values from -1.5 to 1.5
- first_gain: bfloat16 [512], replicated, may hold values from 0.5 to 1.5
- first_shift: bfloat16 [512], replicated, may hold values from -1.5 to 1.5
- up_weight: bfloat16 [512, 2048], P(None, 'tensor'), may hold values from -0.25 to 0.25
- up_bias: bfloat16 [2048], P('tensor'), may hold values from -2.5 to 2.5
- down_weight: bfloat16 [2048, 512], P('tensor'), may hold values from -0.1875 to 0.1875
- down_bias: bfloat16 [512], replicated, may hold values from -1.5 to 1.5
- second_gain: bfloat16 [512], replicated, may hold values from 0.5 to 1.5
- second_shift: bfloat16 [512], replicated, may hold values from -1.5 to 1.5
- cotangent: bfloat16 [32768, 512], P(('dp', 'tensor')), may hold values from -6 to 6
Outputs:
- layer_out: bfloat16 [32768, 512], P(('dp', 'tensor'))
- tokens_grad: float32 [32768, 512], P(('dp', 'tensor'))
- positions_grad: float32 [512, 512], replicated
- heads_weight_grad: float32 [512, 3, 512], P(None, None, 'tensor')
- merge_weight_grad: float32 [512, 512], P('tensor')
- merge_bias_grad: float32 [512], replicated
- first_gain_grad: float32 [512], replicated
- first_shift_grad: float32 [512], replicated
- up_weight_grad: float32 [512, 2048], P(None, 'tensor')
- up_bias_grad: float32 [2048], P('tensor')
- down_weight_grad: float32 [2048, 512], P('tensor')
- down_bias_grad: float32 [512], replicated
- second_gain_grad: float32 [512], replicated
- second_shift_grad: float32 [512], replicated
The draws below stay inside these ranges and needn't reach their ends.
Inputs may be any that keep to these rules, and one draw needn't show every extreme that they name: `segments`: along a window the numbers never fall; no document has more than 256 characters, and in every window one has exactly that many.
All inputs are finite; a program needn't handle non-finite values.
Results may differ from the reference program's by a relative error of at most 0.013.
The reference program's roundings to bfloat16 on the way count: a program that leaves them out, or rounds other values in their place, can miss the bound.
Values may be sent and summed in bfloat16 or wider, within the bound.
A program may use at most 128 MiB of HBM per device.

```python
import math
import jax
import jax.numpy as jnp
import numpy as np
from jax import lax

D = 512
HEADS = 8
FF = 2048
WLEN = 512
DOCS = 8
MOST_DOC = 256
WINDOWS = 64
TOKENS = 32768


def block_scale(own_key, dims, shards, low, top_value):
    def one(dim, shards_of):
        draws = jax.random.uniform(jax.random.fold_in(jax.random.fold_in(own_key, 6), dim), (shards_of,), jnp.float32, low / len(shards), top_value / len(shards))
        return jnp.repeat(jnp.exp(draws), dims[dim] // shards_of).reshape((-1,) + (1,) * (len(dims) - dim - 1))

    level = one(*shards[0])
    for cut in shards[1:]:
        level = level * one(*cut)
    return level


def length_profile(number_of, total, most, lean):
    weights = [(1 << 20) // math.isqrt(rank ** lean) + 1 for rank in range(2, number_of + 1)]
    surplus, counts = total - most - (number_of - 1), [1] * (number_of - 1)
    while surplus > 0:
        movable = [i for i in range(number_of - 1) if counts[i] < most]
        mass, left = sum([weights[i] for i in movable]), surplus
        for i in movable:
            addition = min(most - counts[i], max(1, left * weights[i] // mass), surplus)
            counts[i] = counts[i] + addition
            surplus = surplus - addition
    return np.array([most] + counts)


def ragged(stream_key, amount, total, most, skew):
    if amount == 2:
        one = jax.random.randint(stream_key, (), max(1, total - most), min(most, total - 1) + 1)
        return jnp.stack([one, total - one])
    lengths = jnp.asarray(length_profile(amount, total, most, skew), jnp.int32)
    couples = (amount - 1) // 2
    giver, sink = lengths[1:1 + 2 * couples:2], lengths[2:2 + 2 * couples:2]
    margin = jnp.minimum(giver - 1, most - sink)
    passed = jax.random.randint(jax.random.fold_in(stream_key, 1), (couples,), 0, 1 << 20) % (margin + 1)
    lengths = lengths.at[1:1 + 2 * couples:2].set(giver - passed).at[2:2 + 2 * couples:2].set(sink + passed)
    return lengths[jax.random.permutation(jax.random.fold_in(stream_key, 2), amount)]


def normal_values(own_key, dims, scale, bound, cuts=(), held_as=jnp.bfloat16):
    entries = jax.random.normal(own_key, dims, jnp.float32) * scale
    if len(cuts) > 0:
        entries = block_scale(own_key, dims, cuts, -0.22, 0.18) * entries
    return jnp.clip(entries, min=-bound, max=bound).astype(held_as)


def setup_inputs(seed: int = 0) -> dict:
    streams_of = jax.random.split(jax.random.key(seed), 16)
    tokens = normal_values(streams_of[0], (TOKENS, D), 1.0, 6.0, ((0, 32),))
    segments = jax.vmap(lambda own: jnp.searchsorted(jnp.cumsum(ragged(own, DOCS, WLEN, MOST_DOC, 3)), jnp.arange(WLEN), side="right"))(jax.random.split(streams_of[1], WINDOWS)).reshape((WINDOWS, WLEN)).astype(jnp.int32)
    positions = normal_values(streams_of[2], (WLEN, D), 0.5, 3.0)
    heads_weight = normal_values(streams_of[3], (D, 3, D), D ** -0.5, 0.25, ((2, 2),))
    merge_weight = normal_values(streams_of[4], (D, D), (D // 16) ** -0.5, 1.0, ((0, 2),))
    merge_bias = normal_values(streams_of[5], (D,), 0.3, 1.5)
    first_gain = jnp.clip(1.0 + 0.1 * jax.random.normal(streams_of[6], (D,), jnp.float32), 0.5, 1.5).astype(jnp.bfloat16)
    first_shift = normal_values(streams_of[7], (D,), 0.3, 1.5)
    up_weight = normal_values(streams_of[8], (D, FF), D ** -0.5, 0.25, ((1, 2),))
    up_bias = normal_values(streams_of[9], (FF,), 0.5, 2.5, ((0, 2),))
    down_weight = normal_values(streams_of[10], (FF, D), (FF // 2) ** -0.5, 0.1875, ((0, 2),))
    down_bias = normal_values(streams_of[11], (D,), 0.3, 1.5)
    second_gain = jnp.clip(1.0 + 0.1 * jax.random.normal(streams_of[12], (D,), jnp.float32), 0.5, 1.5).astype(jnp.bfloat16)
    second_shift = normal_values(streams_of[13], (D,), 0.3, 1.5)
    cotangent = normal_values(streams_of[14], (TOKENS, D), 1.0, 6.0, ((0, 32),))
    return dict(tokens=tokens, segments=segments, positions=positions, heads_weight=heads_weight, merge_weight=merge_weight, merge_bias=merge_bias, first_gain=first_gain, first_shift=first_shift, up_weight=up_weight, up_bias=up_bias, down_weight=down_weight, down_bias=down_bias, second_gain=second_gain, second_shift=second_shift, cotangent=cotangent)


@jax.custom_vjp
def low(v):
    return lax.optimization_barrier(v.astype(jnp.bfloat16)).astype(jnp.float32)

@jax.custom_vjp
def low_back(v):
    return v

def low_keep(v):
    return (low(v), None)

def low_pass(kept, grad):
    return (grad,)

def back_keep(v):
    return (v, None)

def back_low(kept, grad):
    return (low(grad),)
low.defvjp(low_keep, low_pass)
low_back.defvjp(back_keep, back_low)

def layer_norm(value, gain, shift):
    center = lax.optimization_barrier(jnp.mean(value, -1, keepdims=True))
    centred = value - center
    spread = lax.optimization_barrier(jnp.mean(centred * centred, -1, keepdims=True))
    return centred * lax.rsqrt(spread + 1e-05) * gain + shift

def forward(tokens, segments, positions, heads_weight, merge_weight, merge_bias, first_gain, first_shift, up_weight, up_bias, down_weight, down_bias, second_gain, second_shift):
    highest = lax.Precision.HIGHEST
    groups = tokens.shape[0]
    head_size = D // HEADS
    scale = head_size ** (-0.5)
    start_sum = tokens + positions[None]
    attn_in = low(start_sum)
    triple = jnp.einsum('gtd,dcf->gtcf', attn_in, heads_weight, precision=highest)
    triple = low_back(low(triple))
    query = triple[:, :, 0].reshape(groups, WLEN, HEADS, head_size)
    keys_all = triple[:, :, 1].reshape(groups, WLEN, HEADS, head_size)
    values_all = triple[:, :, 2].reshape(groups, WLEN, HEADS, head_size)

    def attend(items):
        win_query, win_keys, win_values, win_segs = items
        raw = jnp.einsum('thd,shd->hts', win_query, win_keys, precision=highest) * scale
        raw = low_back(raw)
        places = jnp.arange(WLEN)
        allowed = (win_segs[:, None] == win_segs[None, :]) & (places[None, :] <= places[:, None])
        scores = jnp.where(allowed[None], raw, -1000000000.0)
        probs = jax.nn.softmax(scores, axis=-1)
        return jnp.einsum('hts,shd->thd', low(probs), win_values, precision=highest)
    mixed = lax.map(jax.checkpoint(attend), (query, keys_all, values_all, segments))
    mixed = low_back(low(mixed.reshape(groups, WLEN, D)))
    attn_out = low_back(jnp.einsum('gtc,cd->gtd', mixed, merge_weight, precision=highest))
    first_sum = start_sum + attn_out + merge_bias
    normed = layer_norm(first_sum, first_gain, first_shift)
    lifted = low(normed)
    pre_act = low_back(jnp.einsum('gtd,df->gtf', lifted, up_weight, precision=highest) + up_bias)
    hidden = low(jax.nn.gelu(pre_act))
    branch = low_back(jnp.einsum('gtf,fd->gtd', hidden, down_weight, precision=highest))
    second_sum = normed + branch + down_bias
    return layer_norm(second_sum, second_gain, second_shift)

def reference(tokens, segments, positions, heads_weight, merge_weight, merge_bias, first_gain, first_shift, up_weight, up_bias, down_weight, down_bias, second_gain, second_shift, cotangent):
    group = math.gcd(WINDOWS, 8)
    steps_count = WINDOWS // group
    params = tuple((item.astype(jnp.float32) for item in (positions, heads_weight, merge_weight, merge_bias, first_gain, first_shift, up_weight, up_bias, down_weight, down_bias, second_gain, second_shift)))
    inputs = tokens.astype(jnp.float32).reshape(steps_count, group, WLEN, D)
    seg_groups = segments.reshape(steps_count, group, WLEN)
    cot_groups = cotangent.astype(jnp.float32).reshape(steps_count, group, WLEN, D)

    def step(totals, items):
        block_in, block_seg, block_cot = items

        def apply(values, *weights):
            return forward(values, block_seg, *weights)
        result, pullback = jax.vjp(apply, block_in, *params)
        grads = pullback(block_cot)
        totals = tuple((total + grad for total, grad in zip(totals, grads[1:])))
        return (totals, (result.astype(jnp.bfloat16), grads[0]))
    init = tuple((jnp.zeros_like(item) for item in params))
    totals, (outputs, in_grads) = lax.scan(step, init, (inputs, seg_groups, cot_groups))
    return (outputs.reshape(TOKENS, D), in_grads.reshape(TOKENS, D), totals[0], totals[1], totals[2], totals[3], totals[4], totals[5], totals[6], totals[7], totals[8], totals[9], totals[10], totals[11])
```

```python
import functools
import jax
import jax.numpy as jnp
from jax import lax
from jax.experimental import pallas as pl
from jax.experimental.pallas import tpu as pltpu
from jax.sharding import PartitionSpec as P

F32, BF16 = jnp.float32, jnp.bfloat16
HEAD = 64
ROWS = 256
NEG = -1000000000.0
GELU_A = 0.7978845608028654
GELU_B = GELU_A * 0.044715


def nn(a, b):
    return lax.dot_general(a, b, (((1,), (0,)), ((), ())), preferred_element_type=F32)


def nt(a, b):
    return lax.dot_general(a, b, (((1,), (1,)), ((), ())), preferred_element_type=F32)


def loop(count, body):
    lax.fori_loop(0, count, lambda i, c: (body(i), c)[1], 0)


def at(i, size):
    return pl.ds(pl.multiple_of(i * size, size), size)


def mean(v):
    return jnp.sum(v, -1, keepdims=True) * (1.0 / v.shape[-1])


def kernel(
    tok, seg, pos, cot, whp, wm, wu, wd, vec,
    out, tg, gd, gu, gm, gh, pg_out, vg,
    ai, ait, trip, bias, probs, mix, mixt, n1, r1, nb, nbt, hid, gp, gs, bg, bgt, mg, dtrip, acc,
):
    R, D = tok.shape
    T = pos.shape[0]
    W = R // T
    FH = wu.shape[2]
    C = 128
    tiles = R // ROWS
    per = T // ROWS
    lane = lax.broadcasted_iota(jnp.int32, (1, C), 1)
    t_id = lax.axis_index("tensor")

    def qkv(j):
        rows = at(j, ROWS)
        x = tok[rows, :].astype(F32) + pos[at(lax.rem(j, per), ROWS), :].astype(F32)
        xb = x.astype(BF16)
        ai[rows, :] = xb
        ait[:, rows] = xb.T

    loop(tiles, qkv)

    def qkv_half(h):
        def body(j):
            rows = at(j, ROWS)
            xb = ai[rows, :]
            for p in range(2):
                y = nn(xb, whp[h, p]).astype(BF16)
                trip[2 * h + p, rows, 0:C] = y[:, 0:C] * 0.125
                trip[2 * h + p, rows, C:] = y[:, C:]

        loop(tiles, body)

    for w in range(W):
        row = seg[pl.ds(t_id * W + w, 1), :].astype(F32)
        wide = jnp.broadcast_to(row, (128, T))
        col = wide.T
        for tb in range(per):
            nk = (tb + 1) * ROWS
            for c2 in range(ROWS // 128):
                lo = tb * ROWS + c2 * 128
                s_id = lax.broadcasted_iota(jnp.int32, (nk, 128), 0)
                l_id = lax.broadcasted_iota(jnp.int32, (nk, 128), 1) + lo
                ok = (col[:nk] == row[:, lo : lo + 128]) & (s_id <= l_id)
                bias[w, :nk, lo : lo + 128] = jnp.where(ok, 0.0, NEG)

    def attend(p, w):
        rows = at(w, T)
        cols = at(p, C)
        q = trip[p, rows, 0:C]
        k = trip[p, rows, C : 2 * C]
        vt = trip[p, rows, 2 * C :].T
        for tb in range(per):
            nk = (tb + 1) * ROWS
            ts = slice(tb * ROWS, (tb + 1) * ROWS)
            parts = []
            for a in range(2):
                qa = jnp.where((lane < HEAD) == (a == 0), q[ts], jnp.zeros((), BF16))
                s = nt(k[:nk], qa) + bias[w, :nk, ts]
                e = jnp.exp(s - jnp.max(s, 0, keepdims=True))
                pt = (e * (1.0 / jnp.sum(e, 0, keepdims=True))).astype(BF16)
                probs[w, 2 * p + a, :nk, ts] = pt
                parts.append(nn(vt[a * HEAD : (a + 1) * HEAD, :nk], pt))
            m = jnp.concatenate(parts, 0).astype(BF16)
            lanes = pl.ds(pl.multiple_of(w * T + tb * ROWS, ROWS), ROWS)
            mixt[cols, lanes] = m
            mix[lanes, cols] = m.T

    def attend_half(h):
        loop(2 * W, lambda i: attend(2 * h + i // W, lax.rem(i, W)))

    for h in range(2):
        qkv_half(h)
        attend_half(h)

    mb, g1, s1, db, g2, s2 = [vec[0, i : i + 1, :] for i in range(6)]
    acc[...] = jnp.zeros_like(acc)

    def rowsum(i, v):
        acc[pl.ds(8 * i, 8), :] += jnp.sum(v.reshape(-1, 8, v.shape[-1]), 0)

    def merge(j):
        rows = at(j, ROWS)
        x = tok[rows, :].astype(F32) + pos[at(lax.rem(j, per), ROWS), :].astype(F32)
        f = x + nn(mix[rows, :], wm[...]) + mb
        z = f - mean(f)
        r = lax.rsqrt(mean(z * z) + 1e-5)
        n = z * r
        n1[rows, :] = n
        r1[rows, :] = jnp.broadcast_to(r, (ROWS, 128))
        y = (n * g1 + s1).astype(BF16)
        nb[rows, :] = y
        nbt[:, rows] = y.T

    loop(tiles, merge)

    def up(h):
        def body(j):
            rows = at(j, ROWS)
            x = nb[rows, :]
            for c in range(FH // D):
                cs = slice(c * D, (c + 1) * D)
                v = nn(x, wu[h, :, cs]) + vec[h, 6 + c : 7 + c, :]
                v2 = v * v
                th = jnp.tanh(v * (GELU_A + GELU_B * v2))
                half = 0.5 + 0.5 * th
                hv = v * half
                hid[h, rows, cs] = hv.astype(BF16)
                gp[h, rows, cs] = (half + hv * (1.0 - th) * (GELU_A + 3.0 * GELU_B * v2)).astype(BF16)

        loop(tiles, body)

    up(0)
    up(1)

    def down(j):
        rows = at(j, ROWS)
        n = n1[rows, :] * g1 + s1
        f = n + (nn(hid[0, rows, :], wd[0]) + nn(hid[1, rows, :], wd[1])) + db
        z = f - mean(f)
        r = lax.rsqrt(mean(z * z) + 1e-5)
        n2 = z * r
        out[rows, :] = (n2 * g2 + s2).astype(BF16)
        g = cot[rows, :].astype(F32)
        e = g * g2
        d = r * (e - mean(e) - n2 * mean(e * n2))
        gs[rows, :] = d
        b = d.astype(BF16)
        bg[rows, :] = b
        bgt[:, rows] = b.T
        rowsum(0, g * n2)
        rowsum(1, g)
        rowsum(2, d)

    loop(tiles, down)

    for h in (1, 0):
        def body(c, h=h):
            gd[h, :, at(c, D)] = nn(bgt[...], hid[h, :, at(c, D)]).astype(BF16)

        loop(FH // D, body)

    def hidden_back(j):
        rows = at(j, ROWS)
        b = bg[rows, :]
        for h in range(2):
            for c in range(FH // D):
                cs = slice(c * D, (c + 1) * D)
                v = nt(b, wd[h, cs, :]) * gp[h, rows, cs].astype(F32)
                vb = v.astype(BF16)
                hid[h, rows, cs] = vb
                rowsum(3 + 2 * h + c, vb.astype(F32))

    loop(tiles, hidden_back)
    for h in (1, 0):
        def body(c, h=h):
            gu[h, :, at(c, D)] = nn(nbt[...], hid[h, :, at(c, D)]).astype(BF16)

        loop(FH // D, body)

    def first_back(j):
        rows = at(j, ROWS)
        g = gs[rows, :] + (nt(hid[0, rows, :], wu[0]) + nt(hid[1, rows, :], wu[1]))
        n = n1[rows, :]
        e = g * g1
        d = r1[rows, 0:1] * (e - mean(e) - n * mean(e * n))
        gs[rows, :] = d
        b = d.astype(BF16)
        bg[rows, :] = b
        mg[rows, :] = nt(b, wm[...]).astype(BF16)
        rowsum(7, g * n)
        rowsum(8, g)
        rowsum(9, d)

    loop(tiles, first_back)
    gm[...] = nn(mixt[...], bg[...]).astype(BF16)

    def attend_back(p, w):
        rows = at(w, T)
        cols = at(p, C)
        q = trip[p, rows, 0:C]
        k = trip[p, rows, C : 2 * C]
        v = trip[p, rows, 2 * C :]
        do = mg[rows, cols]
        kt = k.T
        prod = do.T.astype(F32) * mixt[cols, rows].astype(F32)
        dk, dv = None, None
        dq = []
        for tb in reversed(range(per)):
            nk = (tb + 1) * ROWS
            ts = slice(tb * ROWS, (tb + 1) * ROWS)
            pts, dss, qas, dos, dqs = [], [], [], [], []
            for a in range(2):
                mine = (lane < HEAD) == (a == 0)
                doa = jnp.where(mine, do[ts], jnp.zeros((), BF16))
                qa = jnp.where(mine, q[ts], jnp.zeros((), BF16))
                inner = jnp.sum(prod[a * HEAD : (a + 1) * HEAD, ts], 0, keepdims=True)
                pt = probs[w, 2 * p + a, :nk, ts]
                ds = (pt.astype(F32) * (nt(v[:nk], doa) - inner)).astype(BF16)
                dqs.append(nn(kt[a * HEAD : (a + 1) * HEAD, :nk], ds))
                pts.append(pt)
                dss.append(ds)
                qas.append(qa)
                dos.append(doa)
            dkb = nn(jnp.concatenate(dss, 1), jnp.concatenate(qas, 0))
            dvb = nn(jnp.concatenate(pts, 1), jnp.concatenate(dos, 0))
            if dk is None:
                dk, dv = dkb, dvb
            else:
                dk = jnp.concatenate([dk[:nk] + dkb, dk[nk:]], 0)
                dv = jnp.concatenate([dv[:nk] + dvb, dv[nk:]], 0)
            lanes = pl.ds(pl.multiple_of(w * T + tb * ROWS, ROWS), ROWS)
            dtrip[p, lanes, 0:C] = (jnp.concatenate(dqs, 0) * 0.125).astype(BF16).T
        dtrip[p, rows, C : 2 * C] = dk.astype(BF16)
        dtrip[p, rows, 2 * C :] = dv.astype(BF16)

    for i in range(2):
        for h in (1, 0):
            loop(W, lambda w: attend_back(2 * h + i, w))
            gh[h, i] = nn(ait[...], dtrip[2 * h + i]).astype(BF16)

    def last(j):
        total = jnp.zeros((ROWS, D), F32)
        for w in range(W):
            rows = pl.ds(pl.multiple_of(w * T + j * ROWS, ROWS), ROWS)
            g = gs[rows, :]
            for p in range(4):
                g += nt(dtrip[p, rows, :], whp[p // 2, p % 2])
            tg[rows, :] = g
            total += g
        pg_out[at(j, ROWS), :] = total.astype(BF16)

    loop(per, last)
    for i in range(10):
        vg[i : i + 1, :] = jnp.sum(acc[8 * i : 8 * i + 8, :], 0, keepdims=True)


def scratch(R, D, T, FH):
    W = R // T
    V = pltpu.VMEM
    return [
        V((R, D), BF16), V((D, R), BF16), V((4, R, 384), BF16), V((W, T, T), F32), V((W, 8, T, T), BF16),
        V((R, D), BF16), V((D, R), BF16), V((R, D), F32), V((R, 128), F32), V((R, D), BF16), V((D, R), BF16),
        V((2, R, FH), BF16), V((2, R, FH), BF16), V((R, D), F32), V((R, D), BF16), V((D, R), BF16),
        V((R, D), BF16), V((4, R, 384), BF16), V((80, D), F32),
    ]


def call(tok, seg, pos, cot, whp, wm, wu, wd, vec):
    R, D = tok.shape
    T = pos.shape[0]
    FH = wu.shape[2]
    S = jax.ShapeDtypeStruct
    vm = pl.BlockSpec(memory_space=pltpu.VMEM)
    outs = [
        S((R, D), BF16), S((R, D), F32), S((2, D, FH), BF16), S((2, D, FH), BF16), S((D, D), BF16),
        S((2, 2, D, 384), BF16), S((T, D), BF16), S((16, D), F32),
    ]
    return pl.pallas_call(
        kernel,
        out_shape=outs,
        in_specs=[vm] * 9,
        out_specs=[vm] * len(outs),
        scratch_shapes=scratch(R, D, T, FH),
        compiler_params=pltpu.CompilerParams(vmem_limit_bytes=63 * 2**20),
    )(tok, seg, pos, cot, whp, wm, wu, wd, vec)


def per_device(tok, seg, pos, hw, mw, mb, g1, s1, uw, ub, dw, db, g2, s2, cot):
    D = tok.shape[1]
    half = hw.shape[2]
    whp = hw.reshape(D, 3, 2, 128).transpose(2, 0, 1, 3).reshape(2, D, 384)
    vec = jnp.concatenate([v.astype(F32) for v in (mb, g1, s1, db, g2, s2, ub)]).reshape(8, D)
    swap = lambda v: jnp.stack([v, lax.ppermute(v, "tensor", [(0, 1), (1, 0)])])
    whp, wm, wu, wd, vec = swap(whp), swap(mw).reshape(2 * half, D), swap(uw), swap(dw), swap(vec)
    out, tg, gd, gu, gm, gh, pg, vg = call(tok, seg, pos, cot, whp, wm, wu, wd, vec)
    gm = gm.reshape(2, half, D)
    pick = lambda v: lax.psum(v[0] + lax.ppermute(v[1], "tensor", [(0, 1), (1, 0)]), "dp").astype(F32)
    gd, gu, gm, gh = pick(gd), pick(gu), pick(gm), pick(gh)
    vg_own = lax.psum(vg, "dp")
    rest = lax.psum(vg, ("dp", "tensor"))
    ubg = lax.psum(vg[3:5] + lax.ppermute(vg[5:7], "tensor", [(0, 1), (1, 0)]), "dp").reshape(-1)
    pg = lax.psum(pg.astype(F32), ("dp", "tensor"))
    hg = gh.reshape(2, D, 3, 128).transpose(1, 2, 0, 3).reshape(D, 3, half)
    return (out, tg, pg, hg, gm, rest[9], rest[7], rest[8], gu, ubg, gd.T, rest[2], rest[0], rest[1])


def solution(mesh):
    rows = P(("dp", "tensor"), None)
    ins = (rows, P("dp", None), P(), P(None, None, "tensor"), P("tensor", None), P(), P(), P(), P(None, "tensor"), P("tensor"),
           P("tensor", None), P(), P(), P(), rows)
    outs = (rows, rows, P(), P(None, None, "tensor"), P("tensor", None), P(), P(), P(), P(None, "tensor"), P("tensor"),
            P("tensor", None), P(), P(), P())
    return jax.shard_map(per_device, mesh=mesh, in_specs=ins, out_specs=outs, check_vma=False)
```

```python
import functools
import jax
import jax.numpy as jnp
from jax import lax
from jax.experimental import pallas as pl
from jax.experimental.pallas import tpu as pltpu
from jax.sharding import PartitionSpec as P

F32, BF16 = jnp.float32, jnp.bfloat16
MESH = pl.DeviceIdType.MESH
VMEM_LIMIT = 64 * 2**20 - 2**18
HEAD = 64
ROWS = 256
NEG = -1000000000.0
GELU_A = 0.7978845608028654
GELU_B = GELU_A * 0.044715


def nn(a, b):
    return lax.dot_general(a, b, (((1,), (0,)), ((), ())), preferred_element_type=F32)


def nt(a, b):
    return lax.dot_general(a, b, (((1,), (1,)), ((), ())), preferred_element_type=F32)


def loop(count, body):
    lax.fori_loop(0, count, lambda i, c: (body(i), c)[1], 0)


def at(i, size):
    return pl.ds(pl.multiple_of(i * size, size), size)


def mean(v):
    return jnp.sum(v, -1, keepdims=True) * (1.0 / v.shape[-1])


class Net:
    def __init__(self, send_sem, recv_sem, dp):
        self.send_sem, self.recv_sem, self.sent, self.count = send_sem, recv_sem, [], 0
        i = lax.axis_index("dp")
        self.t = lax.axis_index("tensor")
        self.c = lax.rem(i, 2)
        self.x = lax.rem(i // 2, 2)
        self.z = lax.rem(i // 4, 4)
        self.core = {"dp": i + 1 - 2 * self.c}
        self.xdev = {"dp": i + 2 - 4 * self.x}
        self.ydev = {"tensor": 1 - self.t}
        self.zto = [lax.rem(self.z + s, 4) for s in range(1, 4)]
        self.zdev = [{"dp": i + 4 * (j - self.z)} for j in self.zto]
        self.extra = []
        step = 16
        while step < dp:
            bit = lax.rem(i // step, 2)
            self.extra.append({"dp": i + step * (1 - 2 * bit)})
            step *= 2

    def everyone(self):
        return [self.core, self.xdev, self.ydev] + self.zdev + self.extra

    def greet(self):
        barrier = pltpu.get_barrier_semaphore()
        for device in self.everyone():
            pl.semaphore_signal(barrier, inc=1, device_id=device, device_id_type=MESH)
        pl.semaphore_wait(barrier, len(self.everyone()))

    def send(self, src, dst, device):
        k = self.count
        self.count += 1
        copy = pltpu.make_async_remote_copy(
            src_ref=src, dst_ref=dst, send_sem=self.send_sem.at[k], recv_sem=self.recv_sem.at[k],
            device_id=device, device_id_type=MESH,
        )
        copy.start()
        self.sent.append(copy)
        return copy

    def finish(self):
        for copy in self.sent:
            copy.wait_send()


def tri(tb):
    return slice(tb * (tb + 1) // 2 * ROWS, (tb + 1) * (tb + 2) // 2 * ROWS)


def part(base, size):
    return pl.ds(pl.multiple_of(base, size), size)


def fetch_direct(net, own, oth):
    half = own.shape[0] // 2
    r = part(net.c * half, half)
    y = net.send(own.at[r], oth.at[r], net.ydev)
    yield
    y.wait_recv()
    c = net.send(oth.at[r], oth.at[r], net.core)
    yield
    c.wait_recv()
    yield


def fetch_shared(net, own, oth):
    q = own.shape[0] // 4
    a = part((2 * net.c + net.x) * q, q)
    b = part((2 * net.c + 1 - net.x) * q, q)
    y = net.send(own.at[a], oth.at[a], net.ydev)
    yield
    y.wait_recv()
    x = net.send(oth.at[a], oth.at[a], net.xdev)
    c0 = net.send(oth.at[a], oth.at[a], net.core)
    yield
    x.wait_recv()
    c1 = net.send(oth.at[b], oth.at[b], net.core)
    yield
    c0.wait_recv()
    c1.wait_recv()
    yield


def add(ref, at_rows, others, to=None):
    total = ref[at_rows, :].astype(F32)
    for other in others:
        total = total + other.astype(F32)
    (ref if to is None else to)[at_rows, :] = total.astype(BF16)


def reduce(net, own, oth, rc, yr, xr, zr, er, fin, fin_oth=None):
    rows = own.shape[0]
    hr, qr, sr = rows // 2, rows // 4, rows // 16
    mine = part(net.c * hr, hr)
    c1 = net.send(oth.at[part((1 - net.c) * hr, hr)], rc.at[1], net.core)
    c0 = net.send(own.at[part((1 - net.c) * hr, hr)], rc.at[0], net.core)
    yield
    c1.wait_recv()
    add(oth, mine, [rc[1]])
    y = net.send(oth.at[mine], yr, net.ydev)
    yield
    c0.wait_recv()
    y.wait_recv()
    add(own, mine, [rc[0], yr[...]])
    x = net.send(own.at[part(net.c * hr + (1 - net.x) * qr, qr)], xr, net.xdev)
    yield
    x.wait_recv()
    base = net.c * hr + net.x * qr
    add(own, part(base, qr), [xr[...]])
    zs = [net.send(own.at[part(base + j * sr, sr)], zr.at[s], net.zdev[s]) for s, j in enumerate(net.zto)]
    yield
    for z in zs:
        z.wait_recv()
    shard = part(base + net.z * sr, sr)
    add(own, shard, [zr[0], zr[1], zr[2]], fin)
    for b, device in enumerate(net.extra):
        e = net.send(fin.at[shard], er.at[b], device)
        yield
        e.wait_recv()
        e.wait_send()
        net.sent = [o for o in net.sent if o is not e]
        add(fin, shard, [er[b]])
    zs = [net.send(fin.at[shard], fin.at[shard], device) for device in net.zdev]
    yield
    for z in zs:
        z.wait_recv()
    quarter = part(base, qr)
    x = net.send(fin.at[quarter], fin.at[quarter], net.xdev)
    yield
    x.wait_recv()
    c = net.send(fin.at[mine], fin.at[mine], net.core)
    if fin_oth is not None:
        y = net.send(fin.at[mine], fin.at[mine], net.ydev)
        yield
        y.wait_recv()
        c1 = net.send(fin_oth.at[mine], fin_oth.at[mine], net.core)
        yield
        c1.wait_recv()
    else:
        yield
    c.wait_recv()


def reduce_vectors(net, vs, vr, vz):
    c = net.send(vs.at[0], vr.at[0], net.core)
    yield
    c.wait_recv()
    vs[1] = vs[0] + vr[0]
    x = net.send(vs.at[1], vr.at[1], net.xdev)
    yield
    x.wait_recv()
    vs[2] = vs[1] + vr[1]
    vz[net.z] = vs[2]
    zs = [net.send(vs.at[2], vz.at[net.z], device) for device in net.zdev]
    yield
    for z in zs:
        z.wait_recv()
    vs[3] = (vz[0] + vz[1]) + (vz[2] + vz[3])
    k = 3
    for b, device in enumerate(net.extra):
        e = net.send(vs.at[k], vr.at[3 + b], device)
        yield
        e.wait_recv()
        vs[k + 1] = vs[k] + vr[3 + b]
        k += 1
    y = net.send(vs.at[k], vr.at[2], net.ydev)
    yield
    y.wait_recv()
    vs[k + 1] = vs[k] + vr[2]
    vs[k + 1, 3:5, :] = vs[k, 3:5, :] + vr[2, 5:7, :]


def kernel(
    dp,
    tok_h, seg, pos_h, cot_h, hw, mw, uw, dw, vec0,
    out_h, tg_h, fd_h, fu_h, fm_h, fh_h, fp_h, vg_h,
    tok, pos, cot, whp, wm, wu, wd, vec,
    ai, ait, trip, bias, probs, mix, mixt, n1, r1, nbt, hid, gp, gs, bg, bgt, dtrip, acc,
    gd, gu, gm, gh, gpos, rc, yr, xr, zr, er, rcm, yrm, xrm, zrm, erm, rch, yrh, xrh, zrh, erh,
    fd, fu, fm, fh, fp, vs, vr, vz,
    send_sem, recv_sem, local_sem,
):
    R, D = tok.shape
    T = pos.shape[0]
    W = R // T
    FH = wu.shape[2]
    C = 128
    tiles = R // ROWS
    per = T // ROWS
    lane = lax.broadcasted_iota(jnp.int32, (1, C), 1)
    nb, mg = ai, mix
    net = Net(send_sem, recv_sem, dp)
    t_id = net.t
    local = []

    def move(src, dst):
        copy = pltpu.make_async_copy(src, dst, local_sem.at[len(local)])
        copy.start()
        local.append(copy)
        return copy

    heads_in = [
        move(hw.at[c, :, p * C : (p + 1) * C], whp.at[0, p, :, c * C : (c + 1) * C]) for p in range(2) for c in range(3)
    ]
    tok_in, pos_in = move(tok_h, tok), move(pos_h, pos)
    merge_in = move(mw, wm.at[0 : D // 2])
    up_in, down_in = move(uw, wu.at[0]), move(dw, wd.at[0])
    cot_in = move(cot_h, cot)
    net.greet()
    vec[0] = vec0[...]
    vec_y = net.send(vec0, vec.at[1], net.ydev)
    for copy in heads_in:
        copy.wait()
    get_h = [fetch_direct(net, whp.at[0, p], whp.at[1, p]) for p in range(2)]
    get_m = fetch_direct(net, wm.at[0 : D // 2], wm.at[D // 2 :])
    get_u = fetch_shared(net, wu.at[0], wu.at[1])
    get_d = fetch_shared(net, wd.at[0], wd.at[1])
    next(get_h[0])
    next(get_h[1])
    tok_in.wait()
    pos_in.wait()

    def enter(j):
        rows = at(j, ROWS)
        x = tok[rows, :].astype(F32) + pos[at(lax.rem(j, per), ROWS), :].astype(F32)
        xb = x.astype(BF16)
        ai[rows, :] = xb
        ait[:, rows] = xb.T

    loop(tiles, enter)

    def qkv(h, p):
        def body(j):
            rows = at(j, ROWS)
            xb = ai[rows, :]
            y = nn(xb, whp[h, p]).astype(BF16)
            trip[2 * h + p, rows, 0:C] = y[:, 0:C] * 0.125
            trip[2 * h + p, rows, C:] = y[:, C:]

        loop(tiles, body)

    for w in range(W):
        row = seg[pl.ds(t_id * W + w, 1), :].astype(F32)
        wide = jnp.broadcast_to(row, (128, T))
        col = wide.T
        for tb in range(per):
            nk = (tb + 1) * ROWS
            for c2 in range(ROWS // 128):
                lo = tb * ROWS + c2 * 128
                s_id = lax.broadcasted_iota(jnp.int32, (nk, 128), 0)
                l_id = lax.broadcasted_iota(jnp.int32, (nk, 128), 1) + lo
                ok = (col[:nk] == row[:, lo : lo + 128]) & (s_id <= l_id)
                bias[w, tri(tb), c2 * 128 : c2 * 128 + 128] = jnp.where(ok, 0.0, NEG)

    def attend(p, w):
        rows = at(w, T)
        cols = at(p, C)
        q = trip[p, rows, 0:C]
        k = trip[p, rows, C : 2 * C]
        vt = trip[p, rows, 2 * C :].T
        for tb in range(per):
            nk = (tb + 1) * ROWS
            ts = slice(tb * ROWS, (tb + 1) * ROWS)
            parts = []
            for a in range(2):
                qa = jnp.where((lane < HEAD) == (a == 0), q[ts], jnp.zeros((), BF16))
                s = nt(k[:nk], qa) + bias[w, tri(tb), :]
                e = jnp.exp(s - jnp.max(s, 0, keepdims=True))
                pt = (e * (1.0 / jnp.sum(e, 0, keepdims=True))).astype(BF16)
                probs[w, 2 * p + a, tri(tb), :] = pt
                parts.append(nn(vt[a * HEAD : (a + 1) * HEAD, :nk], pt))
            m = jnp.concatenate(parts, 0).astype(BF16)
            lanes = pl.ds(pl.multiple_of(w * T + tb * ROWS, ROWS), ROWS)
            mixt[cols, lanes] = m
            mix[lanes, cols] = m.T

    qkv(0, 0)
    loop(W, lambda w: attend(0, w))
    next(get_h[0])
    merge_in.wait()
    next(get_m)
    up_in.wait()
    next(get_u)
    qkv(0, 1)
    loop(W, lambda w: attend(1, w))
    next(get_h[0])
    next(get_h[1])
    down_in.wait()
    next(get_d)
    qkv(1, 0)
    loop(W, lambda w: attend(2, w))
    next(get_m)
    next(get_u)
    next(get_h[1])
    qkv(1, 1)
    loop(W, lambda w: attend(3, w))
    next(get_m)
    next(get_u)
    next(get_d)

    mb, g1, s1, db, g2, s2 = [vec[0, i : i + 1, :] for i in range(6)]
    acc[...] = jnp.zeros_like(acc)

    def rowsum(i, v):
        acc[pl.ds(8 * i, 8), :] += jnp.sum(v.reshape(-1, 8, v.shape[-1]), 0)

    def merge(j):
        rows = at(j, ROWS)
        x = tok[rows, :].astype(F32) + pos[at(lax.rem(j, per), ROWS), :].astype(F32)
        f = x + nn(mix[rows, :], wm[...]) + mb
        z = f - mean(f)
        r = lax.rsqrt(mean(z * z) + 1e-5)
        n = z * r
        n1[rows, :] = n
        r1[rows, :] = jnp.broadcast_to(r, (ROWS, 128))
        y = (n * g1 + s1).astype(BF16)
        nb[rows, :] = y
        nbt[:, rows] = y.T

    loop(tiles, merge)

    def up(h):
        def body(j):
            rows = at(j, ROWS)
            x = nb[rows, :]
            for c in range(FH // D):
                cs = slice(c * D, (c + 1) * D)
                v = nn(x, wu[h, :, cs]) + vec[h, 6 + c : 7 + c, :]
                v2 = v * v
                th = jnp.tanh(v * (GELU_A + GELU_B * v2))
                half = 0.5 + 0.5 * th
                hv = v * half
                hid[h, rows, cs] = hv.astype(BF16)
                gp[h, rows, cs] = (half + hv * (1.0 - th) * (GELU_A + 3.0 * GELU_B * v2)).astype(BF16)

        loop(tiles, body)

    up(0)
    next(get_u)
    next(get_d)
    vec_y.wait_recv()
    up(1)
    next(get_d)
    cot_in.wait()

    def down(j):
        rows = at(j, ROWS)
        n = n1[rows, :] * g1 + s1
        f = n + (nn(hid[0, rows, :], wd[0]) + nn(hid[1, rows, :], wd[1])) + db
        z = f - mean(f)
        r = lax.rsqrt(mean(z * z) + 1e-5)
        n2 = z * r
        g = cot[rows, :].astype(F32)
        cot[rows, :] = (n2 * g2 + s2).astype(BF16)
        e = g * g2
        d = r * (e - mean(e) - n2 * mean(e * n2))
        gs[rows, :] = d
        b = d.astype(BF16)
        bg[rows, :] = b
        bgt[:, rows] = b.T
        rowsum(0, g * n2)
        rowsum(1, g)
        rowsum(2, d)

    loop(tiles, down)

    move(cot, out_h)

    def pieces(g, f, k):
        return [
            reduce(net, g.at[c, 0], g.at[c, 1], rc.at[k + c], yr.at[k + c], xr.at[k + c], zr.at[k + c], er.at[k + c], f.at[c])
            for c in range(FH // D)
        ]

    red_d, red_u = pieces(gd, fd, 0), pieces(gu, fu, FH // D)
    red_m = reduce(net, gm.at[0], gm.at[1], rcm.at[0], yrm.at[0], xrm.at[0], zrm.at[0], erm.at[0], fm)
    red_h = [reduce(net, gh.at[0, i], gh.at[1, i], rch.at[i], yrh.at[i], xrh.at[i], zrh.at[i], erh.at[i], fh.at[i]) for i in range(2)]
    red_p = reduce(
        net, gpos.at[t_id], gpos.at[1 - t_id], rcm.at[1], yrm.at[1], xrm.at[1], zrm.at[1], erm.at[1], fp.at[t_id], fp.at[1 - t_id]
    )
    red_v = reduce_vectors(net, vs, vr, vz)

    def run(*queue):
        for g in queue:
            next(g, None)

    for c in range(FH // D):
        for h in (1, 0):
            gd[c, h] = nn(bgt[...], hid[h, :, c * D : (c + 1) * D]).astype(BF16)
        run(red_d[c])

    def hidden_back(j):
        rows = at(j, ROWS)
        b = bg[rows, :]
        for h in range(2):
            for c in range(FH // D):
                cs = slice(c * D, (c + 1) * D)
                v = nt(b, wd[h, cs, :]) * gp[h, rows, cs].astype(F32)
                vb = v.astype(BF16)
                hid[h, rows, cs] = vb
                rowsum(3 + 2 * h + c, vb.astype(F32))

    run(red_d[0])
    loop(tiles // 2, hidden_back)
    run(red_d[1])
    loop(tiles // 2, lambda j: hidden_back(j + tiles // 2))
    for c in range(FH // D):
        for h in (1, 0):
            gu[c, h] = nn(nbt[...], hid[h, :, c * D : (c + 1) * D]).astype(BF16)
        run(red_u[c])

    def first_back(j):
        rows = at(j, ROWS)
        g = gs[rows, :] + (nt(hid[0, rows, :], wu[0]) + nt(hid[1, rows, :], wu[1]))
        n = n1[rows, :]
        e = g * g1
        d = r1[rows, 0:1] * (e - mean(e) - n * mean(e * n))
        gs[rows, :] = d
        b = d.astype(BF16)
        bg[rows, :] = b
        mg[rows, :] = nt(b, wm[...]).astype(BF16)
        rowsum(7, g * n)
        rowsum(8, g)
        rowsum(9, d)

    loop(tiles // 2, first_back)
    run(red_u[0], red_d[0])
    loop(tiles // 2, lambda j: first_back(j + tiles // 2))
    run(red_u[1])
    for h in (1, 0):
        gm[h] = nn(mixt[h * (D // 2) : (h + 1) * (D // 2), :], bg[...]).astype(BF16)
    run(red_m, red_d[1], red_d[0])
    vs[0] = jnp.zeros(vs.shape[1:], F32)
    for i in range(10):
        vs[0, i : i + 1, :] = jnp.sum(acc[8 * i : 8 * i + 8, :], 0, keepdims=True)
    run(red_v)

    def attend_back(p, w):
        rows = at(w, T)
        cols = at(p, C)
        q = trip[p, rows, 0:C]
        k = trip[p, rows, C : 2 * C]
        v = trip[p, rows, 2 * C :]
        do = mg[rows, cols]
        kt = k.T
        prod = do.T.astype(F32) * mixt[cols, rows].astype(F32)
        dk, dv = None, None
        dq = []
        for tb in reversed(range(per)):
            nk = (tb + 1) * ROWS
            ts = slice(tb * ROWS, (tb + 1) * ROWS)
            pts, dss, qas, dos, dqs = [], [], [], [], []
            for a in range(2):
                mine = (lane < HEAD) == (a == 0)
                doa = jnp.where(mine, do[ts], jnp.zeros((), BF16))
                qa = jnp.where(mine, q[ts], jnp.zeros((), BF16))
                inner = jnp.sum(prod[a * HEAD : (a + 1) * HEAD, ts], 0, keepdims=True)
                pt = probs[w, 2 * p + a, tri(tb), :]
                ds = (pt.astype(F32) * (nt(v[:nk], doa) - inner)).astype(BF16)
                dqs.append(nn(kt[a * HEAD : (a + 1) * HEAD, :nk], ds))
                pts.append(pt)
                dss.append(ds)
                qas.append(qa)
                dos.append(doa)
            dkb = nn(jnp.concatenate(dss, 1), jnp.concatenate(qas, 0))
            dvb = nn(jnp.concatenate(pts, 1), jnp.concatenate(dos, 0))
            if dk is None:
                dk, dv = dkb, dvb
            else:
                dk = jnp.concatenate([dk[:nk] + dkb, dk[nk:]], 0)
                dv = jnp.concatenate([dv[:nk] + dvb, dv[nk:]], 0)
            lanes = pl.ds(pl.multiple_of(w * T + tb * ROWS, ROWS), ROWS)
            dtrip[p, lanes, 0:C] = (jnp.concatenate(dqs, 0) * 0.125).astype(BF16).T
        dtrip[p, rows, C : 2 * C] = dk.astype(BF16)
        dtrip[p, rows, 2 * C :] = dv.astype(BF16)

    def back_pair(h, i):
        loop(W, lambda w: attend_back(2 * h + i, w))
        gh[h, i] = nn(ait[...], dtrip[2 * h + i]).astype(BF16)

    back_pair(1, 0)
    run(red_m, red_v, red_u[0], red_d[0], red_d[1])
    back_pair(0, 0)
    run(red_h[0], red_v, red_u[1], red_d[0], red_d[1])
    back_pair(1, 1)
    run(red_h[0], red_v, red_m, red_u[0], red_d[0], red_d[1])
    back_pair(0, 1)
    run(red_h[1], red_v, red_m, red_u[0], red_u[1], red_d[0], red_d[1])

    def last(j):
        total = jnp.zeros((ROWS, D), F32)
        for w in range(W):
            rows = pl.ds(pl.multiple_of(w * T + j * ROWS, ROWS), ROWS)
            g = gs[rows, :]
            for p in range(4):
                g += nt(dtrip[p, rows, :], whp[p // 2, p % 2])
            gs[rows, :] = g
            total += g
        gpos[j] = total.astype(BF16)

    loop(per, last)
    move(gs, tg_h)
    run(red_p)
    queue = [red_h[0], red_h[1], red_p, red_m, red_v, red_d[0], red_d[1], red_u[0], red_u[1]]
    done = [(fh.at[0], fh_h.at[0]), (fh.at[1], fh_h.at[1]), (fp, fp_h), (fm, fm_h), (vs.at[vs.shape[0] - 1], vg_h)]
    done += [(fd.at[c], fd_h.at[c]) for c in range(2)] + [(fu.at[c], fu_h.at[c]) for c in range(2)]
    while queue:
        for k in reversed(range(len(queue))):
            try:
                next(queue[k])
            except StopIteration:
                move(*done[k])
                del queue[k], done[k]
    net.finish()
    for copy in local[len(heads_in) + 6 :]:
        copy.wait()


def scratch(R, D, T, FH, dp):
    W = R // T
    V = pltpu.VMEM
    area = tri(T // ROWS - 1).stop
    X = max(1, (dp // 16).bit_length() - 1)
    NC, DH = FH // D, D // 2
    sems = 160 + 40 * X
    assert NC == 2
    return [
        V((R, D), BF16), V((T, D), BF16), V((R, D), BF16), V((2, 2, D, 384), BF16), V((D, D), BF16), V((2, D, FH), BF16),
        V((2, FH, D), BF16), V((2, 8, D), F32),
        V((R, D), BF16), V((D, R), BF16), V((4, R, 384), BF16), V((W, area, ROWS), F32), V((W, 8, area, ROWS), BF16),
        V((R, D), BF16), V((D, R), BF16), V((R, D), F32), V((R, 128), F32), V((D, R), BF16),
        V((2, R, FH), BF16), V((2, R, FH), BF16), V((R, D), F32), V((R, D), BF16), V((D, R), BF16),
        V((4, R, 384), BF16), V((80, D), F32),
        V((NC, 2, D, D), BF16), V((NC, 2, D, D), BF16), V((2, DH, D), BF16), V((2, 2, D, 384), BF16), V((2, T // 2, D), BF16),
        V((4, 2, DH, D), BF16), V((4, DH, D), BF16), V((4, DH // 2, D), BF16), V((4, 3, D // 16, D), BF16), V((4, X, D // 16, D), BF16),
        V((2, 2, DH // 2, D), BF16), V((2, DH // 2, D), BF16), V((2, DH // 4, D), BF16), V((2, 3, DH // 16, D), BF16),
        V((2, X, DH // 16, D), BF16),
        V((2, 2, DH, 384), BF16), V((2, DH, 384), BF16), V((2, DH // 2, 384), BF16), V((2, 3, D // 16, 384), BF16),
        V((2, X, D // 16, 384), BF16),
        V((NC, D, D), BF16), V((NC, D, D), BF16), V((DH, D), BF16), V((2, D, 384), BF16), V((2, T // 2, D), BF16),
        V((5 + (dp // 16).bit_length() - 1, 16, D), F32), V((3 + X, 16, D), F32), V((4, 16, D), F32),
        pltpu.SemaphoreType.DMA((sems,)), pltpu.SemaphoreType.DMA((sems,)), pltpu.SemaphoreType.DMA((32,)),
    ]


def call(dp, tok, seg, pos, cot, hw, mw, uw, dw, vec):
    R, D = tok.shape
    T = pos.shape[0]
    FH = uw.shape[1]
    S = jax.ShapeDtypeStruct
    vm = pl.BlockSpec(memory_space=pltpu.VMEM)
    hb = pl.BlockSpec(memory_space=pl.ANY)
    outs = [
        S((R, D), BF16), S((R, D), F32), S((2, D, D), BF16), S((2, D, D), BF16), S((D // 2, D), BF16),
        S((2, D, 384), BF16), S((2, T // 2, D), BF16), S((16, D), F32),
    ]
    return pl.pallas_call(
        functools.partial(kernel, dp),
        out_shape=outs,
        in_specs=[hb, vm, hb, hb, hb, hb, hb, hb, vm],
        out_specs=[hb] * len(outs),
        scratch_shapes=scratch(R, D, T, FH, dp),
        compiler_params=pltpu.CompilerParams(vmem_limit_bytes=VMEM_LIMIT, collective_id=1, has_side_effects=True),
    )(tok, seg, pos, cot, hw, mw, uw, dw, vec)


def per_device(dp, tok, seg, pos, hw, mw, mb, g1, s1, uw, ub, dw, db, g2, s2, cot):
    D = tok.shape[1]
    T = pos.shape[0]
    vec = jnp.concatenate([v.astype(F32) for v in (mb, g1, s1, db, g2, s2, ub)]).reshape(8, D)
    out, tg, gd, gu, gm, gh, pg, v = call(dp, tok, seg, pos, cot, hw.transpose(1, 0, 2), mw, uw, dw, vec)
    gd = gd.transpose(0, 2, 1).reshape(-1, D).astype(F32)
    gu = gu.transpose(1, 0, 2).reshape(D, -1).astype(F32)
    gh = gh.reshape(2, D, 3, 128).transpose(1, 2, 0, 3).reshape(D, 3, -1).astype(F32)
    pg = pg.reshape(T, D).astype(F32)
    return (out, tg, pg, gh, gm.astype(F32), v[9], v[7], v[8], gu, v[3:5].reshape(-1), gd, v[2], v[0], v[1])


def solution(mesh):
    rows = P(("dp", "tensor"), None)
    ins = (rows, P("dp", None), P(), P(None, None, "tensor"), P("tensor", None), P(), P(), P(), P(None, "tensor"), P("tensor"),
           P("tensor", None), P(), P(), P(), rows)
    outs = (rows, rows, P(), P(None, None, "tensor"), P("tensor", None), P(), P(), P(), P(None, "tensor"), P("tensor"),
            P("tensor", None), P(), P(), P())
    return jax.shard_map(
        functools.partial(per_device, mesh.shape["dp"]), mesh=mesh, in_specs=ins, out_specs=outs, check_vma=False
    )
```

```python
import functools
import jax
import jax.numpy as jnp
from jax import lax
from jax.experimental import pallas as pl
from jax.experimental.pallas import tpu as pltpu
from jax.sharding import PartitionSpec as P

F32, BF16 = jnp.float32, jnp.bfloat16
MESH = pl.DeviceIdType.MESH
FETCH = (("g0", "x"), ("g1", "x"), ("wm", "z"), ("wu0", "z"), ("wu1", "x"), ("wd0", "x"), ("wd1", "y"))
PIECES = (
    ("d0a", "d0", 0, 512, 0, 256, "yxz"),
    ("d0b", "d0", 0, 512, 256, 512, "yxz"),
    ("d1a", "d1", 0, 512, 0, 256, "xzy"),
    ("d1b", "d1", 0, 512, 256, 512, "xzy"),
    ("u0a", "u0", 0, 512, 0, 256, "yxz"),
    ("u0b", "u0", 0, 512, 256, 512, "yxz"),
    ("u1", "u1", 0, 512, 0, 512, "xyz"),
    ("m", "m", 0, 256, 0, 512, "xyz"),
    ("h0a", "h0", 0, 256, 0, 384, "xyz"),
    ("h0b", "h0", 256, 512, 0, 384, "xyz"),
    ("h1a", "h1", 0, 256, 0, 384, "yxz"),
    ("h1b", "h1", 256, 512, 0, 384, "yxz"),
    ("p", "p", 0, 256, 0, 512, "pz"),
)
ORDER = (
    "g0", "wu0", "g1", "wm", "wu1", "enter", "qkv0", "att0", "wd0", "qkv1", "wd1", "g0", "att1", "wu0", "g1", "g0", "wm", "g0",
    "qkv2", "att2", "wu0", "wu1", "g1", "wu0", "wm", "g1", "qkv3", "att3", "wm", "wd0", "merge", "wu1", "up0", "wu1", "wd1",
    "wd0", "up1", "wd1", "wd0", "down", "gd1", "d1a", "d1b", "gd0", "d0a", "d0b", "d1a", "d1b", "hb0", "d0a", "d0b", "hb1", "gu0",
    "u0a", "u0b", "d1a", "gu1", "u1", "d0a", "u0a", "u0b", "fb0", "d1b", "d0b", "u1", "fb1", "d0a", "d1a", "ab0", "u0a", "d0b",
    "ab3", "u0b", "d1b", "d1a", "gm", "m", "gh0", "d0a", "ab2", "d0b", "m", "d1b", "u1", "ab1", "u0a", "d1a", "gh3", "d0a", "u0b",
    "last", "p", "d0b", "m", "u1", "d1b", "gh1", "h1a", "h1b", "d1a", "p", "u0a", "gh2", "h0a", "h0b", "d0a", "u0b", "h1a", "d0b",
    "h1b", "d1a", "m", "h0a", "h0b", "vec", "v", "d0a", "d0b", "d1b", "u1", "v", "d1b", "u0a", "p", "u0b", "h1a", "h0a", "m",
    "h1b", "h0b", "v", "u1", "h0a", "u0a", "p", "h0b", "u0a", "u0b", "m", "h1a", "v", "u0b", "h1b", "h0a", "p", "v", "h0b", "u1",
    "h1a", "m", "u1", "h1b", "m", "h0a", "h0b", "p", "h1a", "h1b", "h0a", "p", "h0b", "h0a", "h1a", "h0b", "h1b", "h1a", "h1b",
)
VMEM_LIMIT = 64 * 2**20 - 2**18
HEAD = 64
ROWS = 256
NEG = -1000000000.0
GELU_A = 0.7978845608028654
GELU_B = GELU_A * 0.044715


def nn(a, b):
    return lax.dot_general(a, b, (((1,), (0,)), ((), ())), preferred_element_type=F32)


def nt(a, b):
    return lax.dot_general(a, b, (((1,), (1,)), ((), ())), preferred_element_type=F32)


def loop(count, body):
    lax.fori_loop(0, count, lambda i, c: (body(i), c)[1], 0)


def at(i, size):
    return pl.ds(pl.multiple_of(i * size, size), size)


def mean(v):
    return jnp.sum(v, -1, keepdims=True) * (1.0 / v.shape[-1])


class Net:
    def __init__(self, send_sem, recv_sem, dp):
        self.send_sem, self.recv_sem, self.sent, self.count = send_sem, recv_sem, [], 0
        i = lax.axis_index("dp")
        self.t = lax.axis_index("tensor")
        self.c = lax.rem(i, 2)
        self.x = lax.rem(i // 2, 2)
        self.z = lax.rem(i // 4, 4)
        self.core = {"dp": i + 1 - 2 * self.c}
        self.xdev = {"dp": i + 2 - 4 * self.x}
        self.ydev = {"tensor": 1 - self.t}
        self.zto = [lax.rem(self.z + s, 4) for s in range(1, 4)]
        self.zdev = [{"dp": i + 4 * (j - self.z)} for j in self.zto]
        self.zpair = {"dp": i + 4 * (1 - 2 * lax.rem(self.z, 2))}
        self.e = lax.rem(i // 2, 8)
        self.eto = [lax.rem(self.e + s, 8) for s in range(1, 8)]
        self.edev = [{"dp": i + 2 * (j - self.e)} for j in self.eto]
        self.xydev = {"dp": i + 2 - 4 * self.x, "tensor": 1 - self.t}
        self.extra = []
        step = 16
        while step < dp:
            bit = lax.rem(i // step, 2)
            self.extra.append({"dp": i + step * (1 - 2 * bit)})
            step *= 2

    def everyone(self):
        more = ([self.xydev] if any("p" in o for *_, o in PIECES) else []) + (self.edev if any("8" in o for *_, o in PIECES) else [self.xdev] + self.zdev)
        return [self.core, self.ydev] + more + self.extra

    def greet(self):
        barrier = pltpu.get_barrier_semaphore()
        for device in self.everyone():
            pl.semaphore_signal(barrier, inc=1, device_id=device, device_id_type=MESH)
        pl.semaphore_wait(barrier, len(self.everyone()))

    def send(self, src, dst, device):
        k = self.count
        self.count += 1
        copy = pltpu.make_async_remote_copy(
            src_ref=src, dst_ref=dst, send_sem=self.send_sem.at[k], recv_sem=self.recv_sem.at[k],
            device_id=device, device_id_type=MESH,
        )
        copy.start()
        self.sent.append(copy)
        return copy

    def finish(self):
        for copy in self.sent:
            copy.wait_send()


def tri(tb):
    return slice(tb * (tb + 1) // 2 * ROWS, (tb + 1) * (tb + 2) // 2 * ROWS)


def part(base, size):
    return pl.ds(pl.multiple_of(base, size), size)


def fetch_direct(net, ready, own, oth):
    half = own.shape[0] // 2
    r = part(net.c * half, half)
    ready.wait()
    y = net.send(own.at[r], oth.at[r], net.ydev)
    yield
    y.wait_recv()
    c = net.send(oth.at[r], oth.at[r], net.core)
    yield
    c.wait_recv()


def fetch_shared(net, ready, own, oth, along):
    q = own.shape[0] // 4
    bit, device = (net.x, net.xdev) if along == "x" else (lax.rem(net.z, 2), net.zpair)
    a = part((2 * net.c + bit) * q, q)
    b = part((2 * net.c + 1 - bit) * q, q)
    ready.wait()
    y = net.send(own.at[a], oth.at[a], net.ydev)
    yield
    y.wait_recv()
    x = net.send(oth.at[a], oth.at[a], device)
    c0 = net.send(oth.at[a], oth.at[a], net.core)
    yield
    x.wait_recv()
    c1 = net.send(oth.at[b], oth.at[b], net.core)
    yield
    c0.wait_recv()
    c1.wait_recv()


class Ready:
    def __init__(self, *copies):
        self.copies = list(copies)

    def wait(self):
        for copy in self.copies:
            copy.wait()
        self.copies = []


def recv_rows(rows, order, extra):
    size, halves, total = rows // 2, 2, rows
    for stage in order:
        if stage == "y":
            total, halves = total + size, 1
        elif stage == "x":
            size //= 2
            total += size * halves
        elif stage == "z":
            size //= 4
            total += 3 * size * halves
        elif stage == "8":
            size //= 8
            total += 7 * size * halves
        elif stage == "p":
            size //= 2
            total, halves = total + 3 * size, 1
    return total + extra * size


def reduce(net, g, own, buf, fin, order):
    rows = g.shape[1]
    oth = 1 - own
    used = [0]
    pending = {0: [], 1: []}

    def take(k):
        used[0] += k
        return buf.at[used[0] - k : used[0]]

    def post(h, base, size, device):
        dst = take(size)
        pending[h is oth].append((net.send(g.at[h, part(base, size)], dst, device), dst))

    def settle(h, base, size, to=None):
        here = part(base, size)
        total = g[h, here, :].astype(F32)
        for copy, dst in pending[h is oth]:
            copy.wait_recv()
            total = total + dst[...].astype(F32)
        pending[h is oth] = []
        if to is None:
            g[h, here, :] = total.astype(BF16)
        else:
            to[here, :] = total.astype(BF16)

    size = rows // 2
    base = net.c * size
    halves = [oth, own]
    for h in halves:
        post(h, (1 - net.c) * size, size, net.core)
    yield
    history = []
    for stage in order:
        history.append((stage, base, size))
        if stage == "y":
            settle(oth, base, size)
            dst = take(size)
            pending[False].append((net.send(g.at[oth, part(base, size)], dst, net.ydev), dst))
            halves = [own]
        elif stage == "p":
            settle(oth, base, size)
            settle(own, base, size)
            size //= 2
            near, far = base + net.x * size, base + (1 - net.x) * size
            for h, start, device in ((oth, far, net.xydev), (oth, near, net.ydev), (own, far, net.xdev)):
                dst = take(size)
                pending[False].append((net.send(g.at[h, part(start, size)], dst, device), dst))
            base, halves = near, [own]
        else:
            for h in halves:
                settle(h, base, size)
            count, to, devices, place = {"x": (2, [1 - net.x], [net.xdev], net.x), "z": (4, net.zto, net.zdev, net.z),
                                         "8": (8, net.eto, net.edev, net.e)}[stage]
            size //= count
            for h in halves:
                for j, device in zip(to, devices):
                    post(h, base + j * size, size, device)
            base = base + place * size
        yield
    last = fin.at[own] if len(fin.shape) == 3 else fin
    settle(own, base, size, last)
    here = part(base, size)
    for device in net.extra:
        dst = take(size)
        copy = net.send(last.at[here], dst, device)
        yield
        copy.wait_recv()
        copy.wait_send()
        net.sent = [o for o in net.sent if o is not copy]
        last[here, :] = (last[here, :].astype(F32) + dst[...].astype(F32)).astype(BF16)
    whole = [last]
    for stage, base, size in reversed(history):
        if stage == "y":
            continue
        devices = {"x": [net.xdev], "z": net.zdev, "8": net.edev, "p": [net.xydev, net.ydev, net.xdev]}[stage]
        copies = [net.send(last.at[here], last.at[here], device) for device in devices]
        yield
        for copy in copies:
            copy.wait_recv()
        here = part(base, size)
        if stage == "p":
            whole = [fin.at[own], fin.at[oth]]
    copies = [net.send(f.at[here], f.at[here], net.core) for f in whole]
    yield
    for copy in copies:
        copy.wait_recv()


def reduce_vectors(net, vs, vr, vz):
    c = net.send(vs.at[0], vr.at[0], net.core)
    yield
    c.wait_recv()
    vs[1] = vs[0] + vr[0]
    x = net.send(vs.at[1], vr.at[1], net.xdev)
    yield
    x.wait_recv()
    vs[2] = vs[1] + vr[1]
    vz[net.z] = vs[2]
    zs = [net.send(vs.at[2], vz.at[net.z], device) for device in net.zdev]
    yield
    for z in zs:
        z.wait_recv()
    vs[3] = (vz[0] + vz[1]) + (vz[2] + vz[3])
    k = 3
    for b, device in enumerate(net.extra):
        e = net.send(vs.at[k], vr.at[3 + b], device)
        yield
        e.wait_recv()
        vs[k + 1] = vs[k] + vr[3 + b]
        k += 1
    y = net.send(vs.at[k], vr.at[2], net.ydev)
    yield
    y.wait_recv()
    vs[k + 1] = vs[k] + vr[2]
    vs[k + 1, 3:5, :] = vs[k, 3:5, :] + vr[2, 5:7, :]


REACH = 256


def span(j):
    return max(0, (j + 1) * 128 - REACH - 128), (j + 1) * 128


def strip(j):
    start = sum(span(i)[1] - span(i)[0] for i in range(j))
    return slice(start, start + span(j)[1] - span(j)[0])


def kernel(
    dp,
    tok_h, seg, pos_h, cot_h, hw, mw, uw, dw, v0, v1, v2, v3, v4, v5, v6,
    out_h, tg_h, fd_h, fu_h, fm_h, fh_h, fp_h, vg_h,
    tok, pos, cot, whp, wm, wu, wd, vec,
    ai, ait, trip, bias, probs, mix, mixt, n1, r1, nbt, hid, gp, gs, bg, bgt, dtrip, acc,
    gd, gu, gm, gh, gpos, fd, fu, fm, fh, fp, vs, vr, vz,
    send_sem, recv_sem, local_sem, *bufs,
):
    R, D = tok.shape
    T = pos.shape[0]
    W = R // T
    FH = wu.shape[2]
    C = 128
    tiles = R // ROWS
    per = T // ROWS
    lane = lax.broadcasted_iota(jnp.int32, (1, C), 1)
    nb, mg = ai, mix
    net = Net(send_sem, recv_sem, dp)
    t_id = net.t
    local = []

    def move(src, dst):
        copy = pltpu.make_async_copy(src, dst, local_sem.at[len(local)])
        copy.start()
        local.append(copy)
        return copy

    heads_in = [
        Ready(*[move(hw.at[c, :, p * C : (p + 1) * C], whp.at[0, p, :, c * C : (c + 1) * C]) for c in range(3)])
        for p in range(2)
    ]
    rows_in = Ready(move(tok_h, tok), move(pos_h, pos))
    merge_in, up_in, down_in = Ready(move(mw, wm.at[0 : D // 2])), Ready(move(uw, wu.at[0])), Ready(move(dw, wd.at[0]))
    cot_in = Ready(move(cot_h, cot))
    inward = len(local)
    net.greet()
    for k, v in enumerate((v0, v1, v2, v3, v4, v5)):
        vec[0, k : k + 1, :] = v[...].astype(F32).reshape(1, D)
    for k in range(FH // D):
        vec[0, 6 + k : 7 + k, :] = v6[k * D : (k + 1) * D].astype(F32).reshape(1, D)
    mb, g1, s1, db, g2, s2 = [vec[0, i : i + 1, :] for i in range(6)]
    vec_y = net.send(vec.at[0], vec.at[1], net.ydev)

    steps = {}
    halves = {"g0": (heads_in[0], whp.at[0, 0], whp.at[1, 0]), "g1": (heads_in[1], whp.at[0, 1], whp.at[1, 1])}
    halves["wm"] = (merge_in, wm.at[0 : D // 2], wm.at[D // 2 :])
    for k in range(2):
        r = slice(k * D // 2, (k + 1) * D // 2)
        halves[f"wu{k}"] = (up_in, wu.at[0, r], wu.at[1, r])
        r = slice(k * FH // 2, (k + 1) * FH // 2)
        halves[f"wd{k}"] = (down_in, wd.at[0, r], wd.at[1, r])
    for name, way in FETCH:
        steps[name] = fetch_direct(net, *halves[name]) if way == "y" else fetch_shared(net, *halves[name], way)
    whole = {"m": (gm, fm, fm_h), "p": (gpos, fp, fp_h)}
    for k in range(2):
        whole[f"d{k}"] = (gd.at[k], fd.at[k], fd_h.at[k])
        whole[f"u{k}"] = (gu.at[k], fu.at[k], fu_h.at[k])
        whole[f"h{k}"] = (gh.at[k], fh.at[k], fh_h.at[k])
    ends = {"v": (vs.at[vs.shape[0] - 1], vg_h)}
    for (name, key, r0, r1_, c0, c1, order), buf in zip(PIECES, bufs):
        g, f, f_h = whole[key]
        if key != "p":
            g, f, f_h = g.at[:, r0:r1_, c0:c1], f.at[r0:r1_, c0:c1], f_h.at[r0:r1_, c0:c1]
        steps[name] = reduce(net, g, t_id if key == "p" else 0, buf, f, order)
        ends[name] = (f, f_h)
    steps["v"] = reduce_vectors(net, vs, vr, vz)
    def enter(j):
        rows = at(j, ROWS)
        x = tok[rows, :].astype(F32) + pos[at(lax.rem(j, per), ROWS), :].astype(F32)
        xb = x.astype(BF16)
        ai[rows, :] = xb
        ait[:, rows] = xb.T

    def seg_enter():
        rows_in.wait()
        loop(tiles, enter)
        masks()

    def qkv(h, p):
        every = [slice(j * ROWS, (j + 1) * ROWS) for j in range(tiles)]
        ys = [nn(ai[rows, :], whp[h, p]).astype(BF16) for rows in every]
        for rows, y in zip(every, ys):
            trip[2 * h + p, rows, 0:C] = y[:, 0:C] * 0.125
            trip[2 * h + p, rows, C:] = y[:, C:]

    def masks():
        for w in range(W):
            row = seg[pl.ds(t_id * W + w, 1), :].astype(F32)
            col = jnp.broadcast_to(row, (C, T)).T
            for j in range(T // C):
                lo, hi = span(j)
                s_id = lax.broadcasted_iota(jnp.int32, (hi - lo, C), 0) + lo
                l_id = lax.broadcasted_iota(jnp.int32, (hi - lo, C), 1) + j * C
                ok = (col[lo:hi] == row[:, j * C : (j + 1) * C]) & (s_id <= l_id)
                bias[w, strip(j), :] = jnp.where(ok, 0.0, NEG)

    def attend(p, ws):
        zero = jnp.zeros((), BF16)
        first = lane < HEAD
        strips = range(T // C)
        cols = at(p, C)
        ss, bs, vts, ms, pts = {}, {}, {}, {}, {}
        for w in ws:
            rows = at(w, T)
            q = trip[p, rows, 0:C]
            k = trip[p, rows, C : 2 * C]
            for j in strips:
                lo, hi = span(j)
                qj = q[j * C : (j + 1) * C]
                ss[w, j] = nt(k[lo:hi], jnp.concatenate([jnp.where(first, qj, zero), jnp.where(first, zero, qj)], 0))
                bs[w, j] = bias[w, strip(j), :]
            vts[w] = trip[p, rows, 2 * C :].T
        for w in ws:
            for j in strips:
                halves = []
                for a in range(2):
                    v = ss[w, j][:, a * C : (a + 1) * C] + bs[w, j]
                    e = jnp.exp(v - jnp.max(v, 0, keepdims=True))
                    halves.append((e * (1.0 / jnp.sum(e, 0, keepdims=True))).astype(BF16))
                pts[w, j] = jnp.concatenate(halves, 1)
            for j in strips:
                lo, hi = span(j)
                m = nn(vts[w][:, lo:hi], pts[w, j])
                ms[w, j] = jnp.concatenate([m[:HEAD, :C], m[HEAD:, C:]], 0).astype(BF16)
        for w in ws:
            rows = at(w, T)
            for j in strips:
                probs[w, p, strip(j), :] = pts[w, j]
            m = jnp.concatenate([ms[w, j] for j in strips], 1)
            mixt[cols, rows] = m
            mix[rows, cols] = m.T

    def rowsum(i, v):
        acc[pl.ds(8 * i, 8), :] += jnp.sum(v.reshape(-1, 8, v.shape[-1]), 0)

    def merge(jj):
        both = [at(2 * jj + i, ROWS) for i in range(2)]
        xs = [
            tok[rows, :].astype(F32) + pos[at(lax.rem(2 * jj + i, per), ROWS), :].astype(F32) + mb for i, rows in enumerate(both)
        ]
        fs = [x + nn(mix[rows, :], wm[...]) for x, rows in zip(xs, both)]
        zs = [f - mean(f) for f in fs]
        rs = [lax.rsqrt(mean(z * z) + 1e-5) for z in zs]
        ns = [z * r for z, r in zip(zs, rs)]
        ys = [(n * g1 + s1).astype(BF16) for n in ns]
        for rows, n, r, y in zip(both, ns, rs, ys):
            n1[rows, :] = n
            r1[rows, :] = jnp.broadcast_to(r, (ROWS, 128))
            nb[rows, :] = y
            nbt[:, rows] = y.T

    def up(h):
        def body(j):
            rows = at(j, ROWS)
            x = nb[rows, :]
            chunks = [slice(c * D // 2, (c + 1) * D // 2) for c in range(2 * FH // D)]
            vs = [nn(x, wu[h, :, cs]) + vec[h, 6 + cs.start // D : 7 + cs.start // D, cs.start % D : cs.start % D + D // 2] for cs in chunks]
            hs, ps = [], []
            for v in vs:
                v2 = v * v
                th = jnp.tanh(v * (GELU_A + GELU_B * v2))
                half = 0.5 + 0.5 * th
                hv = v * half
                hs.append(hv.astype(BF16))
                ps.append((half + hv * (1.0 - th) * (GELU_A + 3.0 * GELU_B * v2)).astype(BF16))
            for cs, hv, pv in zip(chunks, hs, ps):
                hid[h, rows, cs] = hv
                gp[h, rows, cs] = pv

        loop(tiles, body)

    def down(jj):
        both = [at(2 * jj + i, ROWS) for i in range(2)]
        gvs = [cot[rows, :] for rows in both]
        fs = [n1[rows, :] * g1 + (s1 + db) + (nn(hid[0, rows, :], wd[0]) + nn(hid[1, rows, :], wd[1])) for rows in both]
        todo = []
        for rows, f, g in zip(both, fs, gvs):
            z = f - mean(f)
            r = lax.rsqrt(mean(z * z) + 1e-5)
            n2 = z * r
            g = g.astype(F32)
            e = g * g2
            d = r * (e - mean(e) - n2 * mean(e * n2))
            todo.append((rows, (n2 * g2 + s2).astype(BF16), d, d.astype(BF16), g * n2, g))
        for rows, o, d, b, _, _ in todo:
            cot[rows, :] = o
            gs[rows, :] = d
            bg[rows, :] = b
            bgt[:, rows] = b.T
        for _, _, d, _, gn, g in todo:
            rowsum(0, gn)
            rowsum(1, g)
            rowsum(2, d)

    def seg_down():
        cot_in.wait()
        loop(tiles // 2, down)
        move(cot, out_h)

    def grad_down(c):
        for h in (1, 0):
            gd[c, h] = nn(bgt[...], hid[h, :, c * D : (c + 1) * D]).astype(BF16)

    def hidden_back(j):
        rows = at(j, ROWS)
        b = bg[rows, :]
        todo = [(h, c) for h in range(2) for c in range(FH // D)]
        dh = {k: nt(b, wd[k[0], k[1] * D : (k[1] + 1) * D, :]) for k in todo}
        vb = {(h, c): (dh[h, c] * gp[h, rows, c * D : (c + 1) * D].astype(F32)).astype(BF16) for h, c in todo}
        for h, c in todo:
            hid[h, rows, c * D : (c + 1) * D] = vb[h, c]
        for h, c in todo:
            rowsum(3 + 2 * h + c, vb[h, c].astype(F32))

    def grad_up(c):
        for h in (1, 0):
            gu[c, h] = nn(nbt[...], hid[h, :, c * D : (c + 1) * D]).astype(BF16)

    def first_back(jj):
        both = [at(2 * jj + i, ROWS) for i in range(2)]
        gg = [gs[rows, :] + (nt(hid[0, rows, :], wu[0]) + nt(hid[1, rows, :], wu[1])) for rows in both]
        nns = [n1[rows, :] for rows in both]
        rr = [r1[rows, 0:1] for rows in both]
        ds = []
        for g, n, r in zip(gg, nns, rr):
            e = g * g1
            ds.append(r * (e - mean(e) - n * mean(e * n)))
        bs = [d.astype(BF16) for d in ds]
        ms = [nt(b, wm[...]).astype(BF16) for b in bs]
        for rows, d, b, m in zip(both, ds, bs, ms):
            gs[rows, :] = d
            bg[rows, :] = b
            mg[rows, :] = m
        for g, n, d in zip(gg, nns, ds):
            rowsum(7, g * n)
            rowsum(8, g)
            rowsum(9, d)

    def grad_merge():
        for h in (1, 0):
            gm[h] = nn(mixt[h * (D // 2) : (h + 1) * (D // 2), :], bg[...]).astype(BF16)

    def vectors():
        vs[0] = jnp.zeros(vs.shape[1:], F32)
        for i in range(10):
            vs[0, i : i + 1, :] = jnp.sum(acc[8 * i : 8 * i + 8, :], 0, keepdims=True)

    def attend_back(p, ws):
        zero = jnp.zeros((), BF16)
        first = lane < HEAD
        strips = range(T // C)
        cols = at(p, C)
        both = lambda x: jnp.concatenate([jnp.where(first, x, zero), jnp.where(first, zero, x)], 0)
        cut = lambda x, j, s: x[s * C - span(j)[0] : (s + 1) * C - span(j)[0], :]
        users = [[j for j in strips if span(j)[0] <= s * C < span(j)[1]] for s in strips]
        dps, pts, dds, dvs, kts, qqs, prods, dss, dks, ms = [{} for _ in range(10)]
        for w in ws:
            rows = at(w, T)
            v = trip[p, rows, 2 * C :]
            do = mg[rows, cols]
            q = trip[p, rows, 0:C]
            for j in strips:
                dds[w, j] = both(do[j * C : (j + 1) * C])
                dps[w, j] = nt(v[span(j)[0] : span(j)[1]], dds[w, j])
                pts[w, j] = probs[w, p, strip(j), :]
                qqs[w, j] = both(q[j * C : (j + 1) * C])
            prods[w] = do.T.astype(F32) * mixt[cols, rows].astype(F32)
            kts[w] = trip[p, rows, C : 2 * C].T
        for w in ws:
            for s in strips:
                js = users[s]
                dvs[w, s] = nn(jnp.concatenate([cut(pts[w, j], j, s) for j in js], 1), jnp.concatenate([dds[w, j] for j in js], 0))
            for j in strips:
                ts = slice(j * C, (j + 1) * C)
                ds = []
                for a in range(2):
                    cs = slice(a * C, (a + 1) * C)
                    inner = jnp.sum(prods[w][a * HEAD : (a + 1) * HEAD, ts], 0, keepdims=True)
                    ds.append((pts[w, j][:, cs].astype(F32) * (dps[w, j][:, cs] - inner)).astype(BF16))
                dss[w, j] = jnp.concatenate(ds, 1)
            for j in strips:
                m = nn(kts[w][:, span(j)[0] : span(j)[1]], dss[w, j])
                ms[w, j] = (jnp.concatenate([m[:HEAD, :C], m[HEAD:, C:]], 0) * 0.125).astype(BF16)
            for s in strips:
                js = users[s]
                dks[w, s] = nn(jnp.concatenate([cut(dss[w, j], j, s) for j in js], 1), jnp.concatenate([qqs[w, j] for j in js], 0))
        for w in ws:
            rows = at(w, T)
            dtrip[p, rows, 0:C] = jnp.concatenate([ms[w, j] for j in strips], 1).T
            for s in strips:
                lanes = pl.ds(pl.multiple_of(w * T + s * C, C), C)
                dtrip[p, lanes, C : 2 * C] = dks[w, s].astype(BF16)
                dtrip[p, lanes, 2 * C :] = dvs[w, s].astype(BF16)

    def last(j):
        total = jnp.zeros((ROWS, D), F32)
        for w in range(W):
            rows = pl.ds(pl.multiple_of(w * T + j * ROWS, ROWS), ROWS)
            g = gs[rows, :]
            for p in range(4):
                g += nt(dtrip[p, rows, :], whp[p // 2, p % 2])
            gs[rows, :] = g
            total += g
        gpos[j] = total.astype(BF16)

    def seg_last():
        loop(per, last)
        move(gs, tg_h)

    assert tiles == 4

    def half(body, k):
        loop(tiles // 2, lambda j: body(j + k * (tiles // 2)))

    def seg_up1():
        vec_y.wait_recv()
        up(1)

    acc[...] = jnp.zeros_like(acc)
    work = {"enter": seg_enter, "merge": lambda: loop(tiles // 2, merge), "up0": lambda: up(0), "up1": seg_up1, "down": seg_down}
    work.update({"gm": grad_merge, "vec": vectors, "last": seg_last})
    for p in range(4):
        work[f"qkv{p}"] = lambda p=p: qkv(p // 2, p % 2)
        work[f"att{p}"] = lambda p=p: attend(p, range(W))
        work[f"ab{p}"] = lambda p=p: attend_back(p, range(W))
        work[f"gh{p}"] = lambda p=p: gh.__setitem__((p % 2, p // 2), nn(ait[...], dtrip[p]).astype(BF16))
    for k in range(2):
        work[f"gd{k}"] = lambda k=k: grad_down(k)
        work[f"gu{k}"] = lambda k=k: grad_up(k)
        work[f"hb{k}"] = lambda k=k: half(hidden_back, k)
        work[f"fb{k}"] = lambda k=k: first_back(k)
    for name in ORDER:
        if name in work:
            work[name]()
            continue
        try:
            next(steps[name])
        except StopIteration:
            del steps[name]
            if name in ends:
                move(*ends[name])
    for name in list(steps):
        for _ in steps[name]:
            pass
        if name in ends:
            move(*ends[name])
    net.finish()
    for copy in local[inward:]:
        copy.wait()


def scratch(R, D, T, FH, dp):
    W = R // T
    V = pltpu.VMEM
    area = strip(T // 128 - 1).stop
    X = max(1, (dp // 16).bit_length() - 1)
    NC, DH = FH // D, D // 2
    sems = 240 + 40 * X
    assert NC == 2
    return [
        V((R, D), BF16), V((T, D), BF16), V((R, D), BF16), V((2, 2, D, 384), BF16), V((D, D), BF16), V((2, D, FH), BF16),
        V((2, FH, D), BF16), V((2, 8, D), F32),
        V((R, D), BF16), V((D, R), BF16), V((4, R, 384), BF16), V((W, area, 128), F32), V((W, 4, area, 256), BF16),
        V((R, D), BF16), V((D, R), BF16), V((R, D), F32), V((R, 128), F32), V((D, R), BF16),
        V((2, R, FH), BF16), V((2, R, FH), BF16), V((R, D), F32), V((R, D), BF16), V((D, R), BF16),
        V((4, R, 384), BF16), V((80, D), F32),
        V((NC, 2, D, D), BF16), V((NC, 2, D, D), BF16), V((2, DH, D), BF16), V((2, 2, D, 384), BF16), V((2, T // 2, D), BF16),
        V((NC, D, D), BF16), V((NC, D, D), BF16), V((DH, D), BF16), V((2, D, 384), BF16), V((2, T // 2, D), BF16),
        V((5 + (dp // 16).bit_length() - 1, 16, D), F32), V((3 + X, 16, D), F32), V((4, 16, D), F32),
        pltpu.SemaphoreType.DMA((sems,)), pltpu.SemaphoreType.DMA((sems,)), pltpu.SemaphoreType.DMA((40,)),
    ] + [V((recv_rows(b - a, order, (dp // 16).bit_length() - 1), d - c), BF16) for _, _, a, b, c, d, order in PIECES]


def call(dp, tok, seg, pos, cot, hw, mw, uw, dw, *vecs):
    R, D = tok.shape
    T = pos.shape[0]
    FH = uw.shape[1]
    S = jax.ShapeDtypeStruct
    vm = pl.BlockSpec(memory_space=pltpu.VMEM)
    hb = pl.BlockSpec(memory_space=pl.ANY)
    outs = [
        S((R, D), BF16), S((R, D), F32), S((2, D, D), BF16), S((2, D, D), BF16), S((D // 2, D), BF16),
        S((2, D, 384), BF16), S((2, T // 2, D), BF16), S((16, D), F32),
    ]
    return pl.pallas_call(
        functools.partial(kernel, dp),
        out_shape=outs,
        in_specs=[hb, vm, hb, hb, hb, hb, hb, hb] + [vm] * 7,
        out_specs=[hb] * len(outs),
        scratch_shapes=scratch(R, D, T, FH, dp),
        compiler_params=pltpu.CompilerParams(vmem_limit_bytes=VMEM_LIMIT, collective_id=1, has_side_effects=True),
    )(tok, seg, pos, cot, hw, mw, uw, dw, *vecs)


def widen(out_h, tg_h, fd_h, fu_h, fm_h, fh_h, fp_h, v, out, tg, pg_o, hg_o, gm_o, gu_o, gd_o, mb, g1, s1, ub, db, g2, s2,
          fd, fu, fm, fh, fp, tgv, outv, pg, hg, gm, gu, gd, sem, osem):
    D = fm.shape[1]
    pairs = [(fd_h, fd), (fu_h, fu), (fh_h, fh), (fm_h, fm), (fp_h, fp), (tg_h, tgv), (out_h, outv)]
    ins = [pltpu.make_async_copy(a, b, sem.at[k]) for k, (a, b) in enumerate(pairs)]
    for copy in ins:
        copy.start()
    outs = []

    def leave(src, dst):
        copy = pltpu.make_async_copy(src, dst, osem.at[len(outs)])
        copy.start()
        outs.append(copy)

    for row, o in ((9, mb), (7, g1), (8, s1), (2, db), (0, g2), (1, s2)):
        o[...] = v[row, :]
    for k in range(2):
        ub[k * D : (k + 1) * D] = v[3 + k, :]
    ins[0].wait()
    for c in range(2):
        for r in range(2):
            rows = slice(c * D + r * (D // 2), c * D + (r + 1) * (D // 2))
            gd[rows, :] = fd[c, :, r * (D // 2) : (r + 1) * (D // 2)].T.astype(F32)
        leave(gd.at[c * D : (c + 1) * D], gd_o.at[c * D : (c + 1) * D])
    ins[1].wait()
    for r in range(2):
        rows = slice(r * (D // 2), (r + 1) * (D // 2))
        for c in range(2):
            gu[rows, c * D : (c + 1) * D] = fu[c, rows, :].astype(F32)
        leave(gu.at[rows], gu_o.at[rows])
    ins[2].wait()
    for k in range(3):
        for p in range(2):
            hg[k, :, p * 128 : (p + 1) * 128] = fh[p, :, k * 128 : (k + 1) * 128].astype(F32)
        leave(hg.at[k], hg_o.at[k])
    ins[3].wait()
    gm[...] = fm[...].astype(F32)
    leave(gm, gm_o)
    ins[4].wait()
    for k in range(2):
        rows = slice(k * (D // 2), (k + 1) * (D // 2))
        pg[rows, :] = fp[k].astype(F32)
    leave(pg, pg_o)
    ins[5].wait()
    leave(tgv, tg)
    ins[6].wait()
    leave(outv, out)
    for copy in outs:
        copy.wait()


def finish(out, tg, fd, fu, fm, fh, fp, v):
    D = fm.shape[1]
    half = fm.shape[0]
    S, V = jax.ShapeDtypeStruct, pltpu.VMEM
    shapes = [(2 * half, D), (3, D, half), (half, D), (D, 2 * D), (2 * D, D)]
    hb = pl.BlockSpec(memory_space=pl.ANY)
    vm = pl.BlockSpec(memory_space=pltpu.VMEM)
    return pl.pallas_call(
        widen,
        out_shape=[S(out.shape, BF16), S(tg.shape, F32)] + [S(v, F32) for v in shapes]
        + [S((n,), F32) for n in (D, D, D, 2 * D, D, D, D)],
        in_specs=[hb] * 7 + [vm],
        out_specs=[hb] * 7 + [vm] * 7,
        scratch_shapes=[V(v.shape, BF16) for v in (fd, fu, fm, fh, fp)] + [V(tg.shape, F32), V(out.shape, BF16)] + [V(v, F32) for v in shapes]
        + [pltpu.SemaphoreType.DMA((7,)), pltpu.SemaphoreType.DMA((16,))],
        compiler_params=pltpu.CompilerParams(vmem_limit_bytes=VMEM_LIMIT),
    )(out, tg, fd, fu, fm, fh, fp, v)


def per_device(dp, tok, seg, pos, hw, mw, mb, g1, s1, uw, ub, dw, db, g2, s2, cot):
    out, tg, fd, fu, fm, fh, fp, v = call(dp, tok, seg, pos, cot, hw.transpose(1, 0, 2), mw, uw, dw, mb, g1, s1, db, g2, s2, ub)
    out, tg, pg, gh, gm, gu, gd, *vs = finish(out, tg, fd, fu, fm, fh, fp, v)
    mb, g1, s1, ub, db, g2, s2 = vs
    return (out, tg, pg, gh.transpose(1, 0, 2), gm, mb, g1, s1, gu, ub, gd, db, g2, s2)


def solution(mesh):
    rows = P(("dp", "tensor"), None)
    ins = (rows, P("dp", None), P(), P(None, None, "tensor"), P("tensor", None), P(), P(), P(), P(None, "tensor"), P("tensor"),
           P("tensor", None), P(), P(), P(), rows)
    outs = (rows, rows, P(), P(None, None, "tensor"), P("tensor", None), P(), P(), P(), P(None, "tensor"), P("tensor"),
            P("tensor", None), P(), P(), P())
    return jax.shard_map(
        functools.partial(per_device, mesh.shape["dp"]), mesh=mesh, in_specs=ins, out_specs=outs, check_vma=False
    )
```

```python
import functools
import jax
import jax.numpy as jnp
from jax import lax
from jax.experimental import pallas as pl
from jax.experimental.pallas import tpu as pltpu
from jax.sharding import PartitionSpec as P

F32, BF16 = jnp.float32, jnp.bfloat16
MESH = pl.DeviceIdType.MESH
FETCH = (
    ("wm", "wm", 0, 256, "x"),
    ("g0", "g0", 0, 512, "e"),
    ("wd", "wd", 0, 1024, "e"),
    ("g1", "g1", 0, 512, "e"),
    ("wu0", "wu", 0, 256, "x"),
    ("wu1", "wu", 256, 512, "y"),
)
PIECES = (
    ("d0", "d0", 0, 512, 0, 256, "xaby"),
    ("u0", "u0", 0, 512, 0, 256, "yxz"),
    ("d1", "d0", 0, 512, 256, 512, "xaby"),
    ("u1", "u0", 0, 512, 256, 512, "xyab"),
    ("d2", "d1", 0, 512, 0, 256, "xyz"),
    ("u2", "u1", 0, 512, 0, 256, "xyab"),
    ("d3", "d1", 0, 512, 256, 512, "yxz"),
    ("u3", "u1", 0, 512, 256, 512, "ayxb"),
    ("m", "m", 0, 256, 0, 512, "ayxb"),
    ("p", "p", 0, 256, 0, 512, "pz"),
    ("h0a", "h0", 0, 256, 0, 384, "xyab"),
    ("h0b", "h0", 256, 512, 0, 384, "yabx"),
    ("h1a", "h1", 0, 256, 0, 384, "yzx"),
    ("h1b", "h1", 256, 512, 0, 384, "xyz"),
)
ORDER = (
    "g0", "g1", "enter", "wm", "wd", "qkv0", "att0", "g0", "qkv1", "wu0", "g1", "att1", "wu1", "wm", "g0", "g1", "wd", "wm", "g0",
    "wm", "g1", "wu0", "g0", "qkv2", "att2", "g1", "qkv3", "wd", "att3", "merge", "wu0", "up0", "wu1", "wd", "wu0", "wu1", "up1",
    "wd", "down", "gd2", "d2", "gd3", "d3", "gd1", "d1", "d2", "gd0", "d0", "d3", "hb0", "d1", "d0", "hb1", "fb0", "d2", "d3",
    "gu3", "u3", "gu1", "u1", "d1", "gu2", "u2", "u3", "gu0", "u0", "u1", "d2", "d0", "u2", "fb1", "u0", "d3", "d1", "gm", "m",
    "ab0", "u3", "u1", "m", "ab2", "d2", "d0", "gh0", "u0", "u2", "gh2", "h0a", "h0b", "d3", "u3", "d1", "ab1", "h0a", "u1",
    "h0b", "m", "u0", "u2", "ab3", "d1", "u3", "d2", "d0", "last", "p", "u1", "d3", "h0a", "h0b", "u2", "u0", "m", "d1", "d0",
    "d2", "p", "u3", "gh3", "gh1", "h1a", "h1b", "d2", "h0a", "d3", "h0b", "u1", "vec", "v", "h1a", "h1b", "m", "d3", "u2", "d1",
    "u0", "h0a", "d0", "u3", "v", "p", "h0b", "u1", "h1a", "h1b", "m", "d0", "u2", "d1", "h0a", "u1", "d1", "p", "u0", "h1b",
    "u3", "h0b", "u0", "v", "h1a", "u2", "d0", "m", "h0a", "d0", "u1", "h0b", "h1a", "p", "u3", "h1b", "u1", "u2", "h0a", "v",
    "m", "u3", "h1a", "u2", "h0b", "h1b", "m", "p", "v", "h0a", "m", "p", "h0a", "h1a", "h0b", "h1b", "h1a", "h0b", "h1b",
)
VMEM_LIMIT = 64 * 2**20 - 2**18
POOL = 32
HEAD = 64
ROWS = 256
NEG = -1000000000.0
GELU_A = 0.7978845608028654
GELU_B = GELU_A * 0.044715


def nn(a, b):
    return lax.dot_general(a, b, (((1,), (0,)), ((), ())), preferred_element_type=F32)


def nt(a, b):
    return lax.dot_general(a, b, (((1,), (1,)), ((), ())), preferred_element_type=F32)


def loop(count, body):
    lax.fori_loop(0, count, lambda i, c: (body(i), c)[1], 0)


def at(i, size):
    return pl.ds(pl.multiple_of(i * size, size), size)


def mean(v):
    return jnp.sum(v, -1, keepdims=True) * (1.0 / v.shape[-1])


class Net:
    def __init__(self, send_sem, recv_sem, dp):
        self.send_sem, self.recv_sem, self.slots, self.count = send_sem, recv_sem, [None] * POOL, 0
        i = lax.axis_index("dp")
        self.t = lax.axis_index("tensor")
        self.c = lax.rem(i, 2)
        self.x = lax.rem(i // 2, 2)
        self.z = lax.rem(i // 4, 4)
        self.core = {"dp": i + 1 - 2 * self.c}
        self.xdev = {"dp": i + 2 - 4 * self.x}
        self.ydev = {"tensor": 1 - self.t}
        self.zto = [lax.rem(self.z + s, 4) for s in range(1, 4)]
        self.zdev = [{"dp": i + 4 * (j - self.z)} for j in self.zto]
        self.zpair = {"dp": i + 4 * (1 - 2 * lax.rem(self.z, 2))}
        self.zfar = {"dp": i + 4 * (3 - 2 * self.z)}
        self.zb = self.z // 2
        self.za = lax.rem(self.z, 2) + self.zb - 2 * lax.rem(self.z, 2) * self.zb
        self.e = lax.rem(i // 2, 8)
        self.eto = [lax.rem(self.e + s, 8) for s in range(1, 8)]
        self.edev = [{"dp": i + 2 * (j - self.e)} for j in self.eto]
        self.xydev = {"dp": i + 2 - 4 * self.x, "tensor": 1 - self.t}
        self.extra = []
        step = 16
        while step < dp:
            bit = lax.rem(i // step, 2)
            self.extra.append({"dp": i + step * (1 - 2 * bit)})
            step *= 2

    def everyone(self):
        more = ([self.xydev] if any("p" in o or "q" in o for *_, o in PIECES) else []) + (self.edev if any("8" in o for *_, o in PIECES) else [self.xdev] + self.zdev)
        return [self.core, self.ydev] + more + self.extra

    def greet(self):
        barrier = pltpu.get_barrier_semaphore()
        for device in self.everyone():
            pl.semaphore_signal(barrier, inc=1, device_id=device, device_id_type=MESH)
        pl.semaphore_wait(barrier, len(self.everyone()))

    def send(self, src, dst, device):
        k = self.count
        self.count += 1
        slot = k % POOL
        if self.slots[slot] is not None:
            self.slots[slot].wait_send()
        copy = pltpu.make_async_remote_copy(
            src_ref=src, dst_ref=dst, send_sem=self.send_sem.at[slot], recv_sem=self.recv_sem.at[k],
            device_id=device, device_id_type=MESH,
        )
        copy.start()
        self.slots[slot] = copy
        return copy

    def sent(self, copy):
        for slot, other in enumerate(self.slots):
            if other is copy:
                copy.wait_send()
                self.slots[slot] = None

    def finish(self):
        for copy in self.slots:
            if copy is not None:
                copy.wait_send()


def tri(tb):
    return slice(tb * (tb + 1) // 2 * ROWS, (tb + 1) * (tb + 2) // 2 * ROWS)


def part(base, size):
    return pl.ds(pl.multiple_of(base, size), size)


def fetch_direct(net, push, oth):
    half = oth.shape[0] // 2
    r = part(net.c * half, half)
    ys = push(r)
    yield
    for y in ys:
        y.wait_recv()
    c = net.send(oth.at[r], oth.at[r], net.core)
    yield
    c.wait_recv()


def fetch_shared(net, push, oth, along):
    q = oth.shape[0] // 4
    bit, device = (net.x, net.xdev) if along == "x" else (lax.rem(net.z, 2), net.zpair)
    a = part((2 * net.c + bit) * q, q)
    b = part((2 * net.c + 1 - bit) * q, q)
    ys = push(a)
    yield
    for y in ys:
        y.wait_recv()
    x = net.send(oth.at[a], oth.at[a], device)
    c0 = net.send(oth.at[a], oth.at[a], net.core)
    yield
    x.wait_recv()
    c1 = net.send(oth.at[b], oth.at[b], net.core)
    yield
    c0.wait_recv()
    c1.wait_recv()


def fetch_plane(net, push, oth):
    q = oth.shape[0] // 8
    z = lax.rem(net.z, 2)
    start = lambda x, z: (4 * net.c + 2 * x + z) * q
    mine, by_x, by_z = start(net.x, z), start(1 - net.x, z), start(net.x, 1 - z)
    ys = push(part(mine, q))
    yield
    for y in ys:
        y.wait_recv()
    again = lambda base, size, device: net.send(oth.at[part(base, size)], oth.at[part(base, size)], device)
    x1, z1 = again(mine, q, net.xdev), again(mine, q, net.zpair)
    cores = [again(mine, q, net.core)]
    yield
    x1.wait_recv()
    z1.wait_recv()
    z2 = again(by_x, q // 2, net.zpair)
    x2 = again(by_z + q // 2, q // 2, net.xdev)
    cores += [again(by_x, q, net.core), again(by_z, q, net.core)]
    yield
    x2.wait_recv()
    z2.wait_recv()
    cores.append(again(start(1 - net.x, 1 - z), q, net.core))
    yield
    for core in cores:
        core.wait_recv()


class Ready:
    def __init__(self, *copies):
        self.copies = list(copies)

    def wait(self):
        for copy in self.copies:
            copy.wait()
        self.copies = []


def needs(rows, order, extra):
    size, halves, both, one = rows // 2, 2, rows // 2, 0
    copies = 2 + extra
    for stage in order:
        count = {"x": 2, "a": 2, "b": 2, "z": 4, "8": 8}.get(stage, 1)
        if stage in "pq":
            size, halves = size // 2, 1
            one += 3 * size
            copies += 6 if stage == "p" else 4
            copies += stage == "p"
        elif stage == "y":
            halves = 1
            one += size
            copies += 1
        else:
            size //= count
            if halves == 2:
                both += (count - 1) * size
            else:
                one += (count - 1) * size
            copies += 2 * (count - 1)
    return both, one + extra * size, copies


class Arrival:
    def __init__(self, copy):
        self.copy, self.open = copy, True

    def wait(self):
        if self.open:
            self.copy.wait_recv()
        self.open = False


def reduce(net, g, own, buf_both, buf_one, fin, order):
    rows = g.shape[1]
    oth = 1 - own
    used = {2: 0, 1: 0}
    pending = {0: [], 1: []}

    def take(k, halves=1):
        used[halves] += k
        rows = slice(used[halves] - k, used[halves])
        return buf_both.at[:, rows] if halves == 2 else buf_one.at[rows]

    def post_both(base, size, device):
        dst = take(size, 2)
        arrival = Arrival(net.send(g.at[:, part(base, size)], dst, device))
        for h in (own, oth):
            pending[h is oth].append((arrival, dst.at[h]))

    def post(h, base, size, device):
        dst = take(size)
        pending[False].append((Arrival(net.send(g.at[h, part(base, size)], dst, device)), dst))

    def settle(h, base, size, to=None):
        here = part(base, size)
        total = g[h, here, :].astype(F32)
        for arrival, dst in pending[h is oth]:
            arrival.wait()
            total = total + dst[...].astype(F32)
        pending[h is oth] = []
        if to is None:
            g[h, here, :] = total.astype(BF16)
        else:
            to[here, :] = total.astype(BF16)

    size = rows // 2
    base = net.c * size
    both = True
    post_both((1 - net.c) * size, size, net.core)
    yield
    history = []
    for stage in order:
        history.append((stage, base, size))
        if both:
            settle(oth, base, size)
        if stage == "y":
            post(oth, base, size, net.ydev)
            both = False
        elif stage in "pq":
            settle(own, base, size)
            size //= 2
            near, far = base + net.x * size, base + (1 - net.x) * size
            post(oth, far, size, net.xydev)
            post(oth, near, size, net.ydev)
            post(own, far, size, net.xdev)
            base, both = near, False
        else:
            settle(own, base, size)
            count, to, devices, place = {"x": (2, [1 - net.x], [net.xdev], net.x), "z": (4, net.zto, net.zdev, net.z),
                                         "a": (2, [1 - net.za], [net.zpair], net.za), "b": (2, [1 - net.zb], [net.zfar], net.zb),
                                         "8": (8, net.eto, net.edev, net.e)}[stage]
            size //= count
            for j, device in zip(to, devices):
                if both:
                    post_both(base + j * size, size, device)
                else:
                    post(own, base + j * size, size, device)
            base = base + place * size
        yield
    last = fin.at[own] if len(fin.shape) == 3 else fin
    settle(own, base, size, last)
    here = part(base, size)
    for device in net.extra:
        dst = take(size)
        copy = net.send(last.at[here], dst, device)
        yield
        copy.wait_recv()
        net.sent(copy)
        last[here, :] = (last[here, :].astype(F32) + dst[...].astype(F32)).astype(BF16)
    whole = [last]
    for stage, base, size in reversed(history):
        if stage == "y":
            continue
        devices = {"x": [net.xdev], "z": net.zdev, "a": [net.zpair], "b": [net.zfar], "8": net.edev, "q": [net.xdev],
                   "p": [net.xydev, net.ydev, net.xdev]}[stage]
        copies = [net.send(last.at[here], last.at[here], device) for device in devices]
        yield
        for copy in copies:
            copy.wait_recv()
        here = part(base, size)
        if stage == "p":
            whole = [fin.at[own], fin.at[oth]]
    copies = [net.send(f.at[here], f.at[here], net.core) for f in whole]
    yield
    for copy in copies:
        copy.wait_recv()


def reduce_vectors(net, vs, vr, vz):
    c = net.send(vs.at[0], vr.at[0], net.core)
    yield
    c.wait_recv()
    vs[1] = vs[0] + vr[0]
    x = net.send(vs.at[1], vr.at[1], net.xdev)
    yield
    x.wait_recv()
    vs[2] = vs[1] + vr[1]
    vz[net.z] = vs[2]
    zs = [net.send(vs.at[2], vz.at[net.z], device) for device in net.zdev]
    yield
    for z in zs:
        z.wait_recv()
    vs[3] = (vz[0] + vz[1]) + (vz[2] + vz[3])
    k = 3
    for b, device in enumerate(net.extra):
        e = net.send(vs.at[k], vr.at[3 + b], device)
        yield
        e.wait_recv()
        vs[k + 1] = vs[k] + vr[3 + b]
        k += 1
    y = net.send(vs.at[k], vr.at[2], net.ydev)
    yield
    y.wait_recv()
    vs[k + 1] = vs[k] + vr[2]
    vs[k + 1, 3:5, :] = vs[k, 3:5, :] + vr[2, 5:7, :]


REACH = 256


def span(j):
    return max(0, (j + 1) * 128 - REACH - 128), (j + 1) * 128


def strip(j):
    start = sum(span(i)[1] - span(i)[0] for i in range(j))
    return slice(start, start + span(j)[1] - span(j)[0])


def kernel(
    dp,
    tok_h, seg, pos_h, cot_h, hw, mw, uw, dw, v0, v1, v2, v3, v4, v5, v6,
    out_h, tg_h, fd_h, fu_h, fm_h, fh_h, fp_h, vg_h,
    tok, pos, cot, whp, wm, wu, wd, vec,
    ai, ait, trip, bias, probs, mix, mixt, n1, r1, nbt, hid, gp, gs, bg, bgt, dtrip, acc,
    gd, gu, gm, gh, gpos, fd, fu, fm, fh, fp, vs, vr, vz,
    send_sem, recv_sem, local_sem, *bufs,
):
    R, D = tok.shape
    T = pos.shape[0]
    W = R // T
    FH = wu.shape[2]
    C = 128
    tiles = R // ROWS
    per = T // ROWS
    lane = lax.broadcasted_iota(jnp.int32, (1, C), 1)
    nb, mg = ai, mix
    net = Net(send_sem, recv_sem, dp)
    t_id = net.t
    local = []

    def move(src, dst):
        copy = pltpu.make_async_copy(src, dst, local_sem.at[len(local)])
        copy.start()
        local.append(copy)
        return copy

    heads_in = [
        Ready(*[move(hw.at[c, :, p * C : (p + 1) * C], whp.at[0, p, :, c * C : (c + 1) * C]) for c in range(3)])
        for p in range(2)
    ]
    rows_in = Ready(move(tok_h, tok), move(pos_h, pos))
    merge_in, up_in, down_in = Ready(move(mw, wm.at[0 : D // 2])), Ready(move(uw, wu.at[0])), Ready(move(dw, wd.at[0]))
    cot_in = Ready(move(cot_h, cot))
    inward = len(local)
    net.greet()
    for k, v in enumerate((v0, v1, v2, v3, v4, v5)):
        vec[0, k : k + 1, :] = v[...].astype(F32).reshape(1, D)
    for k in range(FH // D):
        vec[0, 6 + k : 7 + k, :] = v6[k * D : (k + 1) * D].astype(F32).reshape(1, D)
    mb, g1, s1, db, g2, s2 = [vec[0, i : i + 1, :] for i in range(6)]
    vec_y = net.send(vec.at[0], vec.at[1], net.ydev)

    def head_push(p):
        def push(r):
            return [
                net.send(hw.at[c, r, p * C : (p + 1) * C], whp.at[1, p, r, c * C : (c + 1) * C], net.ydev) for c in range(3)
            ]

        return push

    def row_push(own, oth, r0):
        def push(r):
            r = pl.ds(pl.multiple_of(r.start + r0, 16), r.size)
            return [net.send(own.at[r], oth.at[r], net.ydev)]

        return push

    steps = {}
    half = D // 2
    weights = {"wm": (mw, wm.at[half : 2 * half]), "wu": (uw, wu.at[1]), "wd": (dw, wd.at[1])}
    for name, key, r0, r1_, way in FETCH:
        if key in weights:
            own, oth = weights[key]
            push, oth = row_push(own, oth, r0), oth.at[r0:r1_]
        else:
            push, oth = head_push(int(key[1])), whp.at[1, int(key[1])]
        if way == "y":
            steps[name] = fetch_direct(net, push, oth)
        elif way == "e":
            steps[name] = fetch_plane(net, push, oth)
        else:
            steps[name] = fetch_shared(net, push, oth, way)
    whole = {"m": (gm, fm, fm_h), "p": (gpos, fp, fp_h)}
    for k in range(2):
        whole[f"d{k}"] = (gd.at[k], fd.at[k], fd_h.at[k])
        whole[f"u{k}"] = (gu.at[k], fu.at[k], fu_h.at[k])
        whole[f"h{k}"] = (gh.at[k], fh.at[k], fh_h.at[k])
    ends = {"v": (vs.at[vs.shape[0] - 1], vg_h)}
    for (name, key, r0, r1_, c0, c1, order), buf_both, buf_one in zip(PIECES, bufs[::2], bufs[1::2]):
        g, f, f_h = whole[key]
        if key != "p":
            g, f, f_h = g.at[:, r0:r1_, c0:c1], f.at[r0:r1_, c0:c1], f_h.at[r0:r1_, c0:c1]
        steps[name] = reduce(net, g, t_id if key == "p" else 0, buf_both, buf_one, f, order)
        ends[name] = (f, f_h)
    steps["v"] = reduce_vectors(net, vs, vr, vz)
    def enter(j):
        rows = at(j, ROWS)
        x = tok[rows, :].astype(F32) + pos[at(lax.rem(j, per), ROWS), :].astype(F32)
        xb = x.astype(BF16)
        ai[rows, :] = xb
        ait[:, rows] = xb.T

    def seg_enter():
        rows_in.wait()
        loop(tiles, enter)
        masks()

    def qkv(h, p):
        every = [slice(j * ROWS, (j + 1) * ROWS) for j in range(tiles)]
        ys = [nn(ai[rows, :], whp[h, p]).astype(BF16) for rows in every]
        for rows, y in zip(every, ys):
            trip[2 * h + p, rows, 0:C] = y[:, 0:C] * 0.125
            trip[2 * h + p, rows, C:] = y[:, C:]

    def masks():
        for w in range(W):
            row = seg[pl.ds(t_id * W + w, 1), :].astype(F32)
            col = jnp.broadcast_to(row, (C, T)).T
            for j in range(T // C):
                lo, hi = span(j)
                s_id = lax.broadcasted_iota(jnp.int32, (hi - lo, C), 0) + lo
                l_id = lax.broadcasted_iota(jnp.int32, (hi - lo, C), 1) + j * C
                ok = (col[lo:hi] == row[:, j * C : (j + 1) * C]) & (s_id <= l_id)
                bias[w, strip(j), :] = jnp.where(ok, 0.0, NEG)

    def attend(p, ws):
        zero = jnp.zeros((), BF16)
        first = lane < HEAD
        strips = range(T // C)
        cols = at(p, C)
        ss, bs, vts, ms, pts = {}, {}, {}, {}, {}
        for w in ws:
            rows = at(w, T)
            q = trip[p, rows, 0:C]
            k = trip[p, rows, C : 2 * C]
            for j in strips:
                lo, hi = span(j)
                qj = q[j * C : (j + 1) * C]
                ss[w, j] = nt(k[lo:hi], jnp.concatenate([jnp.where(first, qj, zero), jnp.where(first, zero, qj)], 0))
                bs[w, j] = bias[w, strip(j), :]
            vts[w] = trip[p, rows, 2 * C :].T
        for w in ws:
            for j in strips:
                halves = []
                for a in range(2):
                    v = ss[w, j][:, a * C : (a + 1) * C] + bs[w, j]
                    e = jnp.exp(v - jnp.max(v, 0, keepdims=True))
                    halves.append((e * (1.0 / jnp.sum(e, 0, keepdims=True))).astype(BF16))
                pts[w, j] = jnp.concatenate(halves, 1)
            for j in strips:
                lo, hi = span(j)
                m = nn(vts[w][:, lo:hi], pts[w, j])
                ms[w, j] = jnp.concatenate([m[:HEAD, :C], m[HEAD:, C:]], 0).astype(BF16)
        for w in ws:
            rows = at(w, T)
            for j in strips:
                probs[w, p, strip(j), :] = pts[w, j]
            m = jnp.concatenate([ms[w, j] for j in strips], 1)
            mixt[cols, rows] = m
            mix[rows, cols] = m.T

    def rowsum(i, v):
        acc[pl.ds(8 * i, 8), :] += jnp.sum(v.reshape(-1, 8, v.shape[-1]), 0)

    def merge(jj):
        both = [at(2 * jj + i, ROWS) for i in range(2)]
        xs = [
            tok[rows, :].astype(F32) + pos[at(lax.rem(2 * jj + i, per), ROWS), :].astype(F32) + mb for i, rows in enumerate(both)
        ]
        fs = [x + nn(mix[rows, :], wm[...]) for x, rows in zip(xs, both)]
        zs = [f - mean(f) for f in fs]
        rs = [lax.rsqrt(mean(z * z) + 1e-5) for z in zs]
        ns = [z * r for z, r in zip(zs, rs)]
        ys = [(n * g1 + s1).astype(BF16) for n in ns]
        for rows, n, r, y in zip(both, ns, rs, ys):
            n1[rows, :] = n
            r1[rows, :] = jnp.broadcast_to(r, (ROWS, 128))
            nb[rows, :] = y
            nbt[:, rows] = y.T

    def up(h):
        def body(j):
            rows = at(j, ROWS)
            x = nb[rows, :]
            chunks = [slice(c * D // 2, (c + 1) * D // 2) for c in range(2 * FH // D)]
            vs = [nn(x, wu[h, :, cs]) + vec[h, 6 + cs.start // D : 7 + cs.start // D, cs.start % D : cs.start % D + D // 2] for cs in chunks]
            hs, ps = [], []
            for v in vs:
                v2 = v * v
                th = jnp.tanh(v * (GELU_A + GELU_B * v2))
                half = 0.5 + 0.5 * th
                hv = v * half
                hs.append(hv.astype(BF16))
                ps.append((half + hv * (1.0 - th) * (GELU_A + 3.0 * GELU_B * v2)).astype(BF16))
            for cs, hv, pv in zip(chunks, hs, ps):
                hid[h, rows, cs] = hv
                gp[h, rows, cs] = pv

        loop(tiles, body)

    def down(jj):
        both = [at(2 * jj + i, ROWS) for i in range(2)]
        gvs = [cot[rows, :] for rows in both]
        fs = [n1[rows, :] * g1 + (s1 + db) + (nn(hid[0, rows, :], wd[0]) + nn(hid[1, rows, :], wd[1])) for rows in both]
        todo = []
        for rows, f, g in zip(both, fs, gvs):
            z = f - mean(f)
            r = lax.rsqrt(mean(z * z) + 1e-5)
            n2 = z * r
            g = g.astype(F32)
            e = g * g2
            d = r * (e - mean(e) - n2 * mean(e * n2))
            todo.append((rows, (n2 * g2 + s2).astype(BF16), d, d.astype(BF16), g * n2, g))
        for rows, o, d, b, _, _ in todo:
            cot[rows, :] = o
            gs[rows, :] = d
            bg[rows, :] = b
            bgt[:, rows] = b.T
        for _, _, d, _, gn, g in todo:
            rowsum(0, gn)
            rowsum(1, g)
            rowsum(2, d)

    def seg_down():
        cot_in.wait()
        down_in.wait()
        loop(tiles // 2, down)
        move(cot, out_h)

    def quarter(grad, left, k):
        n = FH // 4
        cols = slice(k * n, (k + 1) * n)
        ys = [nn(left[...], hid[h, :, cols]).astype(BF16) for h in (1, 0)]
        for h, y in zip((1, 0), ys):
            grad[k // 2, h, :, (k % 2) * n : (k % 2 + 1) * n] = y

    def hidden_back(j):
        rows = at(j, ROWS)
        b = bg[rows, :]
        todo = [(h, c) for h in range(2) for c in range(FH // D)]
        dh = {k: nt(b, wd[k[0], k[1] * D : (k[1] + 1) * D, :]) for k in todo}
        vb = {(h, c): (dh[h, c] * gp[h, rows, c * D : (c + 1) * D].astype(F32)).astype(BF16) for h, c in todo}
        for h, c in todo:
            hid[h, rows, c * D : (c + 1) * D] = vb[h, c]
        for h, c in todo:
            rowsum(3 + 2 * h + c, vb[h, c].astype(F32))

    def first_back(jj):
        both = [at(2 * jj + i, ROWS) for i in range(2)]
        gg = [gs[rows, :] + (nt(hid[0, rows, :], wu[0]) + nt(hid[1, rows, :], wu[1])) for rows in both]
        nns = [n1[rows, :] for rows in both]
        rr = [r1[rows, 0:1] for rows in both]
        ds = []
        for g, n, r in zip(gg, nns, rr):
            e = g * g1
            ds.append(r * (e - mean(e) - n * mean(e * n)))
        bs = [d.astype(BF16) for d in ds]
        ms = [nt(b, wm[...]).astype(BF16) for b in bs]
        for rows, d, b, m in zip(both, ds, bs, ms):
            gs[rows, :] = d
            bg[rows, :] = b
            mg[rows, :] = m
        for g, n, d in zip(gg, nns, ds):
            rowsum(7, g * n)
            rowsum(8, g)
            rowsum(9, d)

    def grad_merge():
        for h in (1, 0):
            gm[h] = nn(mixt[h * (D // 2) : (h + 1) * (D // 2), :], bg[...]).astype(BF16)

    def vectors():
        vs[0] = jnp.zeros(vs.shape[1:], F32)
        for i in range(10):
            vs[0, i : i + 1, :] = jnp.sum(acc[8 * i : 8 * i + 8, :], 0, keepdims=True)

    def attend_back(p, ws):
        zero = jnp.zeros((), BF16)
        first = lane < HEAD
        strips = range(T // C)
        cols = at(p, C)
        both = lambda x: jnp.concatenate([jnp.where(first, x, zero), jnp.where(first, zero, x)], 0)
        cut = lambda x, j, s: x[s * C - span(j)[0] : (s + 1) * C - span(j)[0], :]
        users = [[j for j in strips if span(j)[0] <= s * C < span(j)[1]] for s in strips]
        dps, pts, dds, dvs, kts, qqs, prods, dss, dks, ms = [{} for _ in range(10)]
        for w in ws:
            rows = at(w, T)
            v = trip[p, rows, 2 * C :]
            do = mg[rows, cols]
            q = trip[p, rows, 0:C]
            for j in strips:
                dds[w, j] = both(do[j * C : (j + 1) * C])
                dps[w, j] = nt(v[span(j)[0] : span(j)[1]], dds[w, j])
                pts[w, j] = probs[w, p, strip(j), :]
                qqs[w, j] = both(q[j * C : (j + 1) * C])
            prods[w] = do.T.astype(F32) * mixt[cols, rows].astype(F32)
            kts[w] = trip[p, rows, C : 2 * C].T
        for w in ws:
            for s in strips:
                js = users[s]
                dvs[w, s] = nn(jnp.concatenate([cut(pts[w, j], j, s) for j in js], 1), jnp.concatenate([dds[w, j] for j in js], 0))
            for j in strips:
                ts = slice(j * C, (j + 1) * C)
                ds = []
                for a in range(2):
                    cs = slice(a * C, (a + 1) * C)
                    inner = jnp.sum(prods[w][a * HEAD : (a + 1) * HEAD, ts], 0, keepdims=True)
                    ds.append((pts[w, j][:, cs].astype(F32) * (dps[w, j][:, cs] - inner)).astype(BF16))
                dss[w, j] = jnp.concatenate(ds, 1)
            for j in strips:
                m = nn(kts[w][:, span(j)[0] : span(j)[1]], dss[w, j])
                ms[w, j] = (jnp.concatenate([m[:HEAD, :C], m[HEAD:, C:]], 0) * 0.125).astype(BF16)
            for s in strips:
                js = users[s]
                dks[w, s] = nn(jnp.concatenate([cut(dss[w, j], j, s) for j in js], 1), jnp.concatenate([qqs[w, j] for j in js], 0))
        for w in ws:
            rows = at(w, T)
            dtrip[p, rows, 0:C] = jnp.concatenate([ms[w, j] for j in strips], 1).T
            for s in strips:
                lanes = pl.ds(pl.multiple_of(w * T + s * C, C), C)
                dtrip[p, lanes, C : 2 * C] = dks[w, s].astype(BF16)
                dtrip[p, lanes, 2 * C :] = dvs[w, s].astype(BF16)

    def last(j):
        total = jnp.zeros((ROWS, D), F32)
        for w in range(W):
            rows = pl.ds(pl.multiple_of(w * T + j * ROWS, ROWS), ROWS)
            g = gs[rows, :]
            for p in range(4):
                g += nt(dtrip[p, rows, :], whp[p // 2, p % 2])
            gs[rows, :] = g
            total += g
        gpos[j] = total.astype(BF16)

    def seg_last():
        loop(per, last)
        move(gs, tg_h)

    assert tiles == 4

    def half(body, k):
        loop(tiles // 2, lambda j: body(j + k * (tiles // 2)))

    def seg_up1():
        vec_y.wait_recv()
        up(1)

    acc[...] = jnp.zeros_like(acc)
    work = {"enter": seg_enter, "merge": lambda: (merge_in.wait(), loop(tiles // 2, merge)), "up0": lambda: (up_in.wait(), up(0)), "up1": seg_up1, "down": seg_down}
    work.update({"gm": grad_merge, "vec": vectors, "last": seg_last})
    for p in range(4):
        work[f"gd{p}"] = lambda p=p: quarter(gd, bgt, p)
        work[f"gu{p}"] = lambda p=p: quarter(gu, nbt, p)
        work[f"qkv{p}"] = lambda p=p: (heads_in[p % 2].wait(), qkv(p // 2, p % 2))
        work[f"att{p}"] = lambda p=p: attend(p, range(W))
        work[f"ab{p}"] = lambda p=p: attend_back(p, range(W))
        work[f"gh{p}"] = lambda p=p: gh.__setitem__((p % 2, p // 2), nn(ait[...], dtrip[p]).astype(BF16))
    for k in range(2):
        work[f"hb{k}"] = lambda k=k: half(hidden_back, k)
        work[f"fb{k}"] = lambda k=k: first_back(k)
    for name in ORDER:
        if name in work:
            work[name]()
            continue
        try:
            next(steps[name])
        except StopIteration:
            del steps[name]
            if name in ends:
                move(*ends[name])
    for name in list(steps):
        for _ in steps[name]:
            pass
        if name in ends:
            move(*ends[name])
    assert net.count <= recv_sem.shape[0], net.count
    net.finish()
    for copy in local[inward:]:
        copy.wait()


def scratch(R, D, T, FH, dp):
    W = R // T
    V = pltpu.VMEM
    area = strip(T // 128 - 1).stop
    X = max(1, (dp // 16).bit_length() - 1)
    NC, DH = FH // D, D // 2
    extra = (dp // 16).bit_length() - 1
    bufs, copies = [], 7 + extra
    for _, _, a, b, c, d, order in PIECES:
        both, one, more = needs(b - a, order, extra)
        bufs += [V((2, both, d - c), BF16), V((max(one, 16), d - c), BF16)]
        copies += more
    for _, key, _, _, way in FETCH:
        copies += (3 if key[0] == "g" else 1) + {"y": 1, "x": 3, "z": 3, "e": 8}[way]
    assert NC == 2
    return [
        V((R, D), BF16), V((T, D), BF16), V((R, D), BF16), V((2, 2, D, 384), BF16), V((D, D), BF16), V((2, D, FH), BF16),
        V((2, FH, D), BF16), V((2, 8, D), F32),
        V((R, D), BF16), V((D, R), BF16), V((4, R, 384), BF16), V((W, area, 128), F32), V((W, 4, area, 256), BF16),
        V((R, D), BF16), V((D, R), BF16), V((R, D), F32), V((R, 128), F32), V((D, R), BF16),
        V((2, R, FH), BF16), V((2, R, FH), BF16), V((R, D), F32), V((R, D), BF16), V((D, R), BF16),
        V((4, R, 384), BF16), V((80, D), F32),
        V((NC, 2, D, D), BF16), V((NC, 2, D, D), BF16), V((2, DH, D), BF16), V((2, 2, D, 384), BF16), V((2, T // 2, D), BF16),
        V((NC, D, D), BF16), V((NC, D, D), BF16), V((DH, D), BF16), V((2, D, 384), BF16), V((2, T // 2, D), BF16),
        V((5 + (dp // 16).bit_length() - 1, 16, D), F32), V((3 + X, 16, D), F32), V((4, 16, D), F32),
        pltpu.SemaphoreType.DMA((POOL,)), pltpu.SemaphoreType.DMA((copies,)), pltpu.SemaphoreType.DMA((16 + len(PIECES),)),
    ] + bufs


def call(dp, tok, seg, pos, cot, hw, mw, uw, dw, *vecs):
    R, D = tok.shape
    T = pos.shape[0]
    FH = uw.shape[1]
    S = jax.ShapeDtypeStruct
    vm = pl.BlockSpec(memory_space=pltpu.VMEM)
    hb = pl.BlockSpec(memory_space=pl.ANY)
    outs = [
        S((R, D), BF16), S((R, D), F32), S((2, D, D), BF16), S((2, D, D), BF16), S((D // 2, D), BF16),
        S((2, D, 384), BF16), S((2, T // 2, D), BF16), S((16, D), F32),
    ]
    return pl.pallas_call(
        functools.partial(kernel, dp),
        out_shape=outs,
        in_specs=[hb, vm, hb, hb, hb, hb, hb, hb] + [vm] * 7,
        out_specs=[hb] * len(outs),
        scratch_shapes=scratch(R, D, T, FH, dp),
        compiler_params=pltpu.CompilerParams(vmem_limit_bytes=VMEM_LIMIT, collective_id=1, has_side_effects=True),
    )(tok, seg, pos, cot, hw, mw, uw, dw, *vecs)


def widen(out_h, tg_h, fd_h, fu_h, fm_h, fh_h, fp_h, v, out, tg, pg_o, hg_o, gm_o, gu_o, gd_o, mb, g1, s1, ub, db, g2, s2,
          fd, fu, fm, fh, fp, tgv, outv, pg, hg, gm, gu, gd, sem, osem):
    D = fm.shape[1]
    pairs = [(fd_h, fd), (fu_h, fu), (fh_h, fh), (fm_h, fm), (fp_h, fp), (tg_h, tgv), (out_h, outv)]
    ins = [pltpu.make_async_copy(a, b, sem.at[k]) for k, (a, b) in enumerate(pairs)]
    for copy in ins:
        copy.start()
    outs = []

    def leave(src, dst):
        copy = pltpu.make_async_copy(src, dst, osem.at[len(outs)])
        copy.start()
        outs.append(copy)

    for row, o in ((9, mb), (7, g1), (8, s1), (2, db), (0, g2), (1, s2)):
        o[...] = v[row, :]
    for k in range(2):
        ub[k * D : (k + 1) * D] = v[3 + k, :]
    ins[0].wait()
    for c in range(2):
        for r in range(2):
            rows = slice(c * D + r * (D // 2), c * D + (r + 1) * (D // 2))
            gd[rows, :] = fd[c, :, r * (D // 2) : (r + 1) * (D // 2)].T.astype(F32)
        leave(gd.at[c * D : (c + 1) * D], gd_o.at[c * D : (c + 1) * D])
    ins[1].wait()
    for r in range(2):
        rows = slice(r * (D // 2), (r + 1) * (D // 2))
        for c in range(2):
            gu[rows, c * D : (c + 1) * D] = fu[c, rows, :].astype(F32)
        leave(gu.at[rows], gu_o.at[rows])
    ins[2].wait()
    for k in range(3):
        for p in range(2):
            hg[k, :, p * 128 : (p + 1) * 128] = fh[p, :, k * 128 : (k + 1) * 128].astype(F32)
        leave(hg.at[k], hg_o.at[k])
    ins[3].wait()
    gm[...] = fm[...].astype(F32)
    leave(gm, gm_o)
    ins[4].wait()
    for k in range(2):
        rows = slice(k * (D // 2), (k + 1) * (D // 2))
        pg[rows, :] = fp[k].astype(F32)
    leave(pg, pg_o)
    ins[5].wait()
    leave(tgv, tg)
    ins[6].wait()
    leave(outv, out)
    for copy in outs:
        copy.wait()


def finish(out, tg, fd, fu, fm, fh, fp, v):
    D = fm.shape[1]
    half = fm.shape[0]
    S, V = jax.ShapeDtypeStruct, pltpu.VMEM
    shapes = [(2 * half, D), (3, D, half), (half, D), (D, 2 * D), (2 * D, D)]
    hb = pl.BlockSpec(memory_space=pl.ANY)
    vm = pl.BlockSpec(memory_space=pltpu.VMEM)
    return pl.pallas_call(
        widen,
        out_shape=[S(out.shape, BF16), S(tg.shape, F32)] + [S(v, F32) for v in shapes]
        + [S((n,), F32) for n in (D, D, D, 2 * D, D, D, D)],
        in_specs=[hb] * 7 + [vm],
        out_specs=[hb] * 7 + [vm] * 7,
        scratch_shapes=[V(v.shape, BF16) for v in (fd, fu, fm, fh, fp)] + [V(tg.shape, F32), V(out.shape, BF16)] + [V(v, F32) for v in shapes]
        + [pltpu.SemaphoreType.DMA((7,)), pltpu.SemaphoreType.DMA((16,))],
        compiler_params=pltpu.CompilerParams(vmem_limit_bytes=VMEM_LIMIT),
    )(out, tg, fd, fu, fm, fh, fp, v)


def per_device(dp, tok, seg, pos, hw, mw, mb, g1, s1, uw, ub, dw, db, g2, s2, cot):
    out, tg, fd, fu, fm, fh, fp, v = call(dp, tok, seg, pos, cot, hw.transpose(1, 0, 2), mw, uw, dw, mb, g1, s1, db, g2, s2, ub)
    out, tg, pg, gh, gm, gu, gd, *vs = finish(out, tg, fd, fu, fm, fh, fp, v)
    mb, g1, s1, ub, db, g2, s2 = vs
    return (out, tg, pg, gh.transpose(1, 0, 2), gm, mb, g1, s1, gu, ub, gd, db, g2, s2)


def solution(mesh):
    rows = P(("dp", "tensor"), None)
    ins = (rows, P("dp", None), P(), P(None, None, "tensor"), P("tensor", None), P(), P(), P(), P(None, "tensor"), P("tensor"),
           P("tensor", None), P(), P(), P(), rows)
    outs = (rows, rows, P(), P(None, None, "tensor"), P("tensor", None), P(), P(), P(), P(None, "tensor"), P("tensor"),
            P("tensor", None), P(), P(), P())
    return jax.shard_map(
        functools.partial(per_device, mesh.shape["dp"]), mesh=mesh, in_specs=ins, out_specs=outs, check_vma=False
    )
```

```python
import functools
import jax
import jax.numpy as jnp
from jax import lax
from jax.experimental import pallas as pl
from jax.experimental.pallas import tpu as pltpu
from jax.sharding import PartitionSpec as P

F32, BF16 = jnp.float32, jnp.bfloat16
MESH = pl.DeviceIdType.MESH
FETCH = (
    ("wu1", "wu", 0, 256, "y"),
    ("g1", "g1", 0, 512, "e"),
    ("wu0", "wu", 256, 512, "e"),
    ("g00", "g0", 0, 256, "z"),
    ("g01", "g0", 256, 512, "x"),
    ("wm", "wm", 0, 256, "e"),
    ("wd", "wd", 0, 1024, "e"),
)
PIECES = (
    ("d0", "d0", 0, 512, 0, 256, "qab"),
    ("u0", "u0", 0, 512, 0, 256, "qab"),
    ("d1", "d0", 0, 512, 256, 512, "qz"),
    ("u1", "u0", 0, 512, 256, 512, "qab"),
    ("d2", "d1", 0, 512, 0, 256, "qz"),
    ("u2", "u1", 0, 512, 0, 256, "qab"),
    ("d3", "d1", 0, 512, 256, 512, "aqb"),
    ("u3", "u1", 0, 512, 256, 512, "aqb"),
    ("m", "m", 0, 256, 0, 512, "axby"),
    ("p", "p", 0, 256, 0, 512, "pz"),
    ("h0a", "h0", 0, 256, 0, 384, "qz"),
    ("h0b", "h0", 256, 512, 0, 384, "qz"),
    ("h1a", "h1", 0, 256, 0, 384, "yabx"),
    ("h1b", "h1", 256, 512, 0, 384, "ayxb"),
)
ORDER = (
    "g1", "wm", "enter", "g00", "g01", "qkv0", "att0", "wu0", "wd", "g1", "qkv1", "wm", "att1", "ait", "wu1", "g00", "g01", "g1",
    "wu0", "wm", "g00", "g01", "g1", "wd", "g00", "g01", "qkv2", "att2", "g1", "wu0", "wm", "qkv3", "att3", "wm", "merge", "wd",
    "up0", "wu1", "wu0", "wd", "wu1", "wu0", "up1", "wd", "down", "gd2", "d2", "gd3", "d3", "gd1", "d1", "d2", "gd0", "d0", "d3",
    "hb0", "d1", "hb1", "d0", "fb0", "gu3", "u3", "d2", "d3", "u3", "gu2", "u2", "gu1", "u1", "d1", "gm", "m", "u2", "gu0", "u0",
    "u1", "d0", "ab3", "d2", "m", "d3", "u0", "u3", "gh3", "ab1", "d0", "d1", "gh1", "h1a", "h1b", "u2", "ab0", "d2", "h1a",
    "h1b", "ab2", "u1", "m", "d3", "d0", "last", "p", "u2", "u0", "d1", "d2", "u3", "h1b", "h1a", "u1", "m", "p", "gh0", "d2",
    "d3", "d0", "gh2", "h0a", "h0b", "u0", "vec", "v", "d1", "h1a", "h1b", "h0a", "u2", "h0b", "u3", "d1", "u1", "d0", "m", "v",
    "d3", "h1b", "p", "u0", "h1a", "u2", "u3", "h0a", "d3", "u1", "m", "h1b", "d3", "h0b", "u2", "d0", "p", "u0", "h1a", "v",
    "u1", "d0", "u3", "h0a", "m", "h1b", "u2", "h1a", "h0b", "u0", "u2", "u1", "v", "p", "u3", "m", "h1b", "u1", "u3", "h0a",
    "u0", "h1a", "v", "h0b", "u0", "m", "h1b", "m", "h1a", "h0a", "h1b", "p", "h0b", "h1a", "h0a", "p", "h0b",
)
VMEM_LIMIT = 64 * 2**20 - 2**18
POOL = 32
HEAD = 64
ROWS = 256
NEG = -1000000000.0
GELU_A = 0.7978845608028654
GELU_B = GELU_A * 0.044715


def nn(a, b):
    return lax.dot_general(a, b, (((1,), (0,)), ((), ())), preferred_element_type=F32)


def nt(a, b):
    return lax.dot_general(a, b, (((1,), (1,)), ((), ())), preferred_element_type=F32)


def loop(count, body):
    lax.fori_loop(0, count, lambda i, c: (body(i), c)[1], 0)


def at(i, size):
    return pl.ds(pl.multiple_of(i * size, size), size)


def mean(v):
    return jnp.sum(v, -1, keepdims=True) * (1.0 / v.shape[-1])


class Net:
    def __init__(self, send_sem, recv_sem, dp):
        self.send_sem, self.recv_sem, self.slots, self.count = send_sem, recv_sem, [None] * POOL, 0
        i = lax.axis_index("dp")
        self.t = lax.axis_index("tensor")
        self.c = lax.rem(i, 2)
        self.x = lax.rem(i // 2, 2)
        self.z = lax.rem(i // 4, 4)
        self.core = {"dp": i + 1 - 2 * self.c}
        self.xdev = {"dp": i + 2 - 4 * self.x}
        self.ydev = {"tensor": 1 - self.t}
        self.zto = [lax.rem(self.z + s, 4) for s in range(1, 4)]
        self.zdev = [{"dp": i + 4 * (j - self.z)} for j in self.zto]
        self.zpair = {"dp": i + 4 * (1 - 2 * lax.rem(self.z, 2))}
        self.zfar = {"dp": i + 4 * (3 - 2 * self.z)}
        self.zb = self.z // 2
        self.za = lax.rem(self.z, 2) + self.zb - 2 * lax.rem(self.z, 2) * self.zb
        self.e = lax.rem(i // 2, 8)
        self.eto = [lax.rem(self.e + s, 8) for s in range(1, 8)]
        self.edev = [{"dp": i + 2 * (j - self.e)} for j in self.eto]
        self.xydev = {"dp": i + 2 - 4 * self.x, "tensor": 1 - self.t}
        self.extra = []
        step = 16
        while step < dp:
            bit = lax.rem(i // step, 2)
            self.extra.append({"dp": i + step * (1 - 2 * bit)})
            step *= 2

    def everyone(self):
        more = ([self.xydev] if any("p" in o or "q" in o for *_, o in PIECES) else []) + (self.edev if any("8" in o for *_, o in PIECES) else [self.xdev] + self.zdev)
        return [self.core, self.ydev] + more + self.extra

    def greet(self):
        barrier = pltpu.get_barrier_semaphore()
        for device in self.everyone():
            pl.semaphore_signal(barrier, inc=1, device_id=device, device_id_type=MESH)
        pl.semaphore_wait(barrier, len(self.everyone()))

    def send(self, src, dst, device):
        k = self.count
        self.count += 1
        slot = k % POOL
        if self.slots[slot] is not None:
            self.slots[slot].wait_send()
        copy = pltpu.make_async_remote_copy(
            src_ref=src, dst_ref=dst, send_sem=self.send_sem.at[slot], recv_sem=self.recv_sem.at[k],
            device_id=device, device_id_type=MESH,
        )
        copy.start()
        self.slots[slot] = copy
        return copy

    def sent(self, copy):
        for slot, other in enumerate(self.slots):
            if other is copy:
                copy.wait_send()
                self.slots[slot] = None

    def finish(self):
        for copy in self.slots:
            if copy is not None:
                copy.wait_send()


def tri(tb):
    return slice(tb * (tb + 1) // 2 * ROWS, (tb + 1) * (tb + 2) // 2 * ROWS)


def part(base, size):
    return pl.ds(pl.multiple_of(base, size), size)


def fetch_direct(net, push, oth):
    half = oth.shape[0] // 2
    r = part(net.c * half, half)
    ys = push(r)
    yield
    for y in ys:
        y.wait_recv()
    c = net.send(oth.at[r], oth.at[r], net.core)
    yield
    c.wait_recv()


def fetch_shared(net, push, oth, along):
    q = oth.shape[0] // 4
    bit, device = (net.x, net.xdev) if along == "x" else (lax.rem(net.z, 2), net.zpair)
    a = part((2 * net.c + bit) * q, q)
    b = part((2 * net.c + 1 - bit) * q, q)
    ys = push(a)
    yield
    for y in ys:
        y.wait_recv()
    x = net.send(oth.at[a], oth.at[a], device)
    c0 = net.send(oth.at[a], oth.at[a], net.core)
    yield
    x.wait_recv()
    c1 = net.send(oth.at[b], oth.at[b], net.core)
    yield
    c0.wait_recv()
    c1.wait_recv()


def fetch_plane(net, push, oth):
    q = oth.shape[0] // 8
    z = lax.rem(net.z, 2)
    start = lambda x, z: (4 * net.c + 2 * x + z) * q
    mine, by_x, by_z = start(net.x, z), start(1 - net.x, z), start(net.x, 1 - z)
    ys = push(part(mine, q))
    yield
    for y in ys:
        y.wait_recv()
    again = lambda base, size, device: net.send(oth.at[part(base, size)], oth.at[part(base, size)], device)
    x1, z1 = again(mine, q, net.xdev), again(mine, q, net.zpair)
    cores = [again(mine, q, net.core)]
    yield
    x1.wait_recv()
    z1.wait_recv()
    z2 = again(by_x, q // 2, net.zpair)
    x2 = again(by_z + q // 2, q // 2, net.xdev)
    cores += [again(by_x, q, net.core), again(by_z, q, net.core)]
    yield
    x2.wait_recv()
    z2.wait_recv()
    cores.append(again(start(1 - net.x, 1 - z), q, net.core))
    yield
    for core in cores:
        core.wait_recv()


class Ready:
    def __init__(self, *copies):
        self.copies = list(copies)

    def wait(self):
        for copy in self.copies:
            copy.wait()
        self.copies = []


def needs(rows, order, extra):
    size, halves, both, one = rows // 2, 2, rows // 2, 0
    copies = 2 + extra
    for stage in order:
        count = {"x": 2, "a": 2, "b": 2, "z": 4, "8": 8}.get(stage, 1)
        if stage in "pq":
            size, halves = size // 2, 1
            one += 3 * size
            copies += 6 if stage == "p" else 4
            copies += stage == "p"
        elif stage == "y":
            halves = 1
            one += size
            copies += 1
        else:
            size //= count
            if halves == 2:
                both += (count - 1) * size
            else:
                one += (count - 1) * size
            copies += 2 * (count - 1)
    return both, one + extra * size, copies


class Arrival:
    def __init__(self, copy):
        self.copy, self.open = copy, True

    def wait(self):
        if self.open:
            self.copy.wait_recv()
        self.open = False


def reduce(net, g, own, buf_both, buf_one, fin, order):
    rows = g.shape[1]
    oth = 1 - own
    used = {2: 0, 1: 0}
    pending = {0: [], 1: []}

    def take(k, halves=1):
        used[halves] += k
        rows = slice(used[halves] - k, used[halves])
        return buf_both.at[:, rows] if halves == 2 else buf_one.at[rows]

    def post_both(base, size, device):
        dst = take(size, 2)
        arrival = Arrival(net.send(g.at[:, part(base, size)], dst, device))
        for h in (own, oth):
            pending[h is oth].append((arrival, dst.at[h]))

    def post(h, base, size, device):
        dst = take(size)
        pending[False].append((Arrival(net.send(g.at[h, part(base, size)], dst, device)), dst))

    def settle(h, base, size, to=None):
        here = part(base, size)
        total = g[h, here, :].astype(F32)
        for arrival, dst in pending[h is oth]:
            arrival.wait()
            total = total + dst[...].astype(F32)
        pending[h is oth] = []
        if to is None:
            g[h, here, :] = total.astype(BF16)
        else:
            to[here, :] = total.astype(BF16)

    size = rows // 2
    base = net.c * size
    both = True
    post_both((1 - net.c) * size, size, net.core)
    yield
    history = []
    for stage in order:
        history.append((stage, base, size))
        if both:
            settle(oth, base, size)
        if stage == "y":
            post(oth, base, size, net.ydev)
            both = False
        elif stage in "pq":
            settle(own, base, size)
            size //= 2
            near, far = base + net.x * size, base + (1 - net.x) * size
            post(oth, far, size, net.xydev)
            post(oth, near, size, net.ydev)
            post(own, far, size, net.xdev)
            base, both = near, False
        else:
            settle(own, base, size)
            count, to, devices, place = {"x": (2, [1 - net.x], [net.xdev], net.x), "z": (4, net.zto, net.zdev, net.z),
                                         "a": (2, [1 - net.za], [net.zpair], net.za), "b": (2, [1 - net.zb], [net.zfar], net.zb),
                                         "8": (8, net.eto, net.edev, net.e)}[stage]
            size //= count
            for j, device in zip(to, devices):
                if both:
                    post_both(base + j * size, size, device)
                else:
                    post(own, base + j * size, size, device)
            base = base + place * size
        yield
    last = fin.at[own] if len(fin.shape) == 3 else fin
    settle(own, base, size, last)
    here = part(base, size)
    for device in net.extra:
        dst = take(size)
        copy = net.send(last.at[here], dst, device)
        yield
        copy.wait_recv()
        net.sent(copy)
        last[here, :] = (last[here, :].astype(F32) + dst[...].astype(F32)).astype(BF16)
    whole = [last]
    for stage, base, size in reversed(history):
        if stage == "y":
            continue
        devices = {"x": [net.xdev], "z": net.zdev, "a": [net.zpair], "b": [net.zfar], "8": net.edev, "q": [net.xdev],
                   "p": [net.xydev, net.ydev, net.xdev]}[stage]
        copies = [net.send(last.at[here], last.at[here], device) for device in devices]
        yield
        for copy in copies:
            copy.wait_recv()
        here = part(base, size)
        if stage == "p":
            whole = [fin.at[own], fin.at[oth]]
    copies = [net.send(f.at[here], f.at[here], net.core) for f in whole]
    yield
    for copy in copies:
        copy.wait_recv()


def reduce_vectors(net, vs, vr, vz):
    c = net.send(vs.at[0], vr.at[0], net.core)
    yield
    c.wait_recv()
    vs[1] = vs[0] + vr[0]
    x = net.send(vs.at[1], vr.at[1], net.xdev)
    yield
    x.wait_recv()
    vs[2] = vs[1] + vr[1]
    vz[net.z] = vs[2]
    zs = [net.send(vs.at[2], vz.at[net.z], device) for device in net.zdev]
    yield
    for z in zs:
        z.wait_recv()
    vs[3] = (vz[0] + vz[1]) + (vz[2] + vz[3])
    k = 3
    for b, device in enumerate(net.extra):
        e = net.send(vs.at[k], vr.at[3 + b], device)
        yield
        e.wait_recv()
        vs[k + 1] = vs[k] + vr[3 + b]
        k += 1
    y = net.send(vs.at[k], vr.at[2], net.ydev)
    yield
    y.wait_recv()
    vs[k + 1] = vs[k] + vr[2]
    vs[k + 1, 3:5, :] = vs[k, 3:5, :] + vr[2, 5:7, :]


REACH = 256


def span(j):
    return max(0, (j + 1) * 128 - REACH - 128), (j + 1) * 128


def strip(j):
    start = sum(span(i)[1] - span(i)[0] for i in range(j))
    return slice(start, start + span(j)[1] - span(j)[0])


def kernel(
    dp,
    tok_h, seg, pos_h, cot_h, hw, mw, uw, dw, v0, v1, v2, v3, v4, v5, v6,
    out_h, tg_h, fd_h, fu_h, fm_h, fh_h, fp_h, vg_h,
    tok, pos, cot, whp, wm, wu, wd, vec,
    ai, ait, trip, bias, probs, mix, mixt, n1, r1, nbt, hid, gp, gs, bg, bgt, dtrip, acc,
    gd, gu, gm, gh, gpos, fd, fu, fm, fh, fp, vs, vr, vz,
    send_sem, recv_sem, local_sem, *bufs,
):
    R, D = tok.shape
    T = pos.shape[0]
    W = R // T
    FH = wu.shape[2]
    C = 128
    tiles = R // ROWS
    per = T // ROWS
    lane = lax.broadcasted_iota(jnp.int32, (1, C), 1)
    nb, mg = ai, mix
    net = Net(send_sem, recv_sem, dp)
    t_id = net.t
    local = []

    def move(src, dst):
        copy = pltpu.make_async_copy(src, dst, local_sem.at[len(local)])
        copy.start()
        local.append(copy)
        return copy

    heads_in = [
        Ready(*[move(hw.at[c, :, p * C : (p + 1) * C], whp.at[0, p, :, c * C : (c + 1) * C]) for c in range(3)])
        for p in range(2)
    ]
    rows_in = Ready(move(tok_h, tok), move(pos_h, pos))
    merge_in, up_in, down_in = Ready(move(mw, wm.at[0 : D // 2])), Ready(move(uw, wu.at[0])), Ready(move(dw, wd.at[0]))
    cot_in = Ready(move(cot_h, cot))
    inward = len(local)
    net.greet()
    for k, v in enumerate((v0, v1, v2, v3, v4, v5)):
        vec[0, k : k + 1, :] = v[...].astype(F32).reshape(1, D)
    for k in range(FH // D):
        vec[0, 6 + k : 7 + k, :] = v6[k * D : (k + 1) * D].astype(F32).reshape(1, D)
    mb, g1, s1, db, g2, s2 = [vec[0, i : i + 1, :] for i in range(6)]
    vec_y = net.send(vec.at[0], vec.at[1], net.ydev)

    def head_push(p, r0):
        def push(r):
            r = pl.ds(pl.multiple_of(r.start + r0, 16), r.size)
            return [
                net.send(hw.at[c, r, p * C : (p + 1) * C], whp.at[1, p, r, c * C : (c + 1) * C], net.ydev) for c in range(3)
            ]

        return push

    def row_push(own, oth, r0):
        def push(r):
            r = pl.ds(pl.multiple_of(r.start + r0, 16), r.size)
            return [net.send(own.at[r], oth.at[r], net.ydev)]

        return push

    steps = {}
    half = D // 2
    weights = {"wm": (mw, wm.at[half : 2 * half]), "wu": (uw, wu.at[1]), "wd": (dw, wd.at[1])}
    for name, key, r0, r1_, way in FETCH:
        if key in weights:
            own, oth = weights[key]
            push, oth = row_push(own, oth, r0), oth.at[r0:r1_]
        else:
            push, oth = head_push(int(key[1]), r0), whp.at[1, int(key[1]), r0:r1_]
        if way == "y":
            steps[name] = fetch_direct(net, push, oth)
        elif way == "e":
            steps[name] = fetch_plane(net, push, oth)
        else:
            steps[name] = fetch_shared(net, push, oth, way)
    whole = {"m": (gm, fm, fm_h), "p": (gpos, fp, fp_h)}
    for k in range(2):
        whole[f"d{k}"] = (gd.at[k], fd.at[k], fd_h.at[k])
        whole[f"u{k}"] = (gu.at[k], fu.at[k], fu_h.at[k])
        whole[f"h{k}"] = (gh.at[k], fh.at[k], fh_h.at[k])
    ends = {"v": (vs.at[vs.shape[0] - 1], vg_h)}
    for (name, key, r0, r1_, c0, c1, order), buf_both, buf_one in zip(PIECES, bufs[::2], bufs[1::2]):
        g, f, f_h = whole[key]
        if key != "p":
            g, f, f_h = g.at[:, r0:r1_, c0:c1], f.at[r0:r1_, c0:c1], f_h.at[r0:r1_, c0:c1]
        steps[name] = reduce(net, g, t_id if key == "p" else 0, buf_both, buf_one, f, order)
        ends[name] = (f, f_h)
    steps["v"] = reduce_vectors(net, vs, vr, vz)
    def enter(j):
        rows = at(j, ROWS)
        x = tok[rows, :].astype(F32) + pos[at(lax.rem(j, per), ROWS), :].astype(F32)
        xb = x.astype(BF16)
        ai[rows, :] = xb

    def turn():
        for j in range(tiles):
            rows = slice(j * ROWS, (j + 1) * ROWS)
            ait[:, rows] = ai[rows, :].T

    def seg_enter():
        rows_in.wait()
        loop(tiles, enter)
        masks()

    def qkv(h, p):
        every = [slice(j * ROWS, (j + 1) * ROWS) for j in range(tiles)]
        ys = [nn(ai[rows, :], whp[h, p]).astype(BF16) for rows in every]
        for rows, y in zip(every, ys):
            trip[2 * h + p, rows, 0:C] = y[:, 0:C] * 0.125
            trip[2 * h + p, rows, C:] = y[:, C:]

    def masks():
        for w in range(W):
            row = seg[pl.ds(t_id * W + w, 1), :].astype(F32)
            col = jnp.broadcast_to(row, (C, T)).T
            for j in range(T // C):
                lo, hi = span(j)
                s_id = lax.broadcasted_iota(jnp.int32, (hi - lo, C), 0) + lo
                l_id = lax.broadcasted_iota(jnp.int32, (hi - lo, C), 1) + j * C
                ok = (col[lo:hi] == row[:, j * C : (j + 1) * C]) & (s_id <= l_id)
                bias[w, strip(j), :] = jnp.where(ok, 0.0, NEG)

    def attend(p, ws):
        zero = jnp.zeros((), BF16)
        first = lane < HEAD
        strips = range(T // C)
        cols = at(p, C)
        ss, bs, vts, ms, pts = {}, {}, {}, {}, {}
        for w in ws:
            rows = at(w, T)
            q = trip[p, rows, 0:C]
            k = trip[p, rows, C : 2 * C]
            for j in strips:
                lo, hi = span(j)
                qj = q[j * C : (j + 1) * C]
                ss[w, j] = nt(k[lo:hi], jnp.concatenate([jnp.where(first, qj, zero), jnp.where(first, zero, qj)], 0))
                bs[w, j] = bias[w, strip(j), :]
            vts[w] = trip[p, rows, 2 * C :].T
        for w in ws:
            for j in strips:
                halves = []
                for a in range(2):
                    v = ss[w, j][:, a * C : (a + 1) * C] + bs[w, j]
                    e = jnp.exp(v - jnp.max(v, 0, keepdims=True))
                    halves.append((e * (1.0 / jnp.sum(e, 0, keepdims=True))).astype(BF16))
                pts[w, j] = jnp.concatenate(halves, 1)
            for j in strips:
                lo, hi = span(j)
                m = nn(vts[w][:, lo:hi], pts[w, j])
                ms[w, j] = jnp.concatenate([m[:HEAD, :C], m[HEAD:, C:]], 0).astype(BF16)
        for w in ws:
            rows = at(w, T)
            for j in strips:
                probs[w, p, strip(j), :] = pts[w, j]
            m = jnp.concatenate([ms[w, j] for j in strips], 1)
            mixt[cols, rows] = m
            mix[rows, cols] = m.T

    def rowsum(i, v):
        acc[pl.ds(8 * i, 8), :] += jnp.sum(v.reshape(-1, 8, v.shape[-1]), 0)

    def merge():
        both = [slice(i * ROWS, (i + 1) * ROWS) for i in range(tiles)]
        xs = [
            tok[rows, :].astype(F32) + pos[(i % per) * ROWS : (i % per + 1) * ROWS, :].astype(F32) + mb for i, rows in enumerate(both)
        ]
        fs = [x + nn(mix[rows, :], wm[...]) for x, rows in zip(xs, both)]
        zs = [f - mean(f) for f in fs]
        rs = [lax.rsqrt(mean(z * z) + 1e-5) for z in zs]
        ns = [z * r for z, r in zip(zs, rs)]
        ys = [(n * g1 + s1).astype(BF16) for n in ns]
        for rows, n, r, y in zip(both, ns, rs, ys):
            n1[rows, :] = n
            r1[rows, :] = jnp.broadcast_to(r, (ROWS, 128))
            nb[rows, :] = y
            nbt[:, rows] = y.T

    def up(h):
        def body(jj):
            units = [(at(2 * jj + i, ROWS), slice(c * D // 2, (c + 1) * D // 2)) for i in range(2) for c in range(2 * FH // D)]
            xs = {i: nb[at(2 * jj + i, ROWS), :] for i in range(2)}
            ws = [wu[h, :, c * D // 2 : (c + 1) * D // 2] for c in range(2 * FH // D)]
            bs = [vec[h, 6 + c // 2 : 7 + c // 2, c % 2 * D // 2 : c % 2 * D // 2 + D // 2] for c in range(2 * FH // D)]
            n = 2 * FH // D
            vs, hs, ps = {}, [], []

            def act(v):
                v2 = v * v
                th = jnp.tanh(v * (GELU_A + GELU_B * v2))
                half = 0.5 + 0.5 * th
                hv = v * half
                hs.append(hv.astype(BF16))
                ps.append((half + hv * (1.0 - th) * (GELU_A + 3.0 * GELU_B * v2)).astype(BF16))

            for k in range(len(units) + 1):
                if k < len(units):
                    vs[k] = nn(xs[k // n], ws[k % n]) + bs[k % n]
                if k >= 1:
                    act(vs[k - 1])
            for (rows, cs), hv, pv in zip(units, hs, ps):
                hid[h, rows, cs] = hv
                gp[h, rows, cs] = pv

        loop(tiles // 2, body)

    def down(jj):
        both = [slice(i * ROWS, (i + 1) * ROWS) for i in range(tiles)]
        gvs = [cot[rows, :] for rows in both]
        fs = [n1[rows, :] * g1 + (s1 + db) + (nn(hid[0, rows, :], wd[0]) + nn(hid[1, rows, :], wd[1])) for rows in both]
        todo = []
        for rows, f, g in zip(both, fs, gvs):
            z = f - mean(f)
            r = lax.rsqrt(mean(z * z) + 1e-5)
            n2 = z * r
            g = g.astype(F32)
            e = g * g2
            d = r * (e - mean(e) - n2 * mean(e * n2))
            todo.append((rows, (n2 * g2 + s2).astype(BF16), d, d.astype(BF16), g * n2, g))
        for rows, o, d, b, _, _ in todo:
            cot[rows, :] = o
            gs[rows, :] = d
            bg[rows, :] = b
            bgt[:, rows] = b.T
        for _, _, d, _, gn, g in todo:
            rowsum(0, gn)
            rowsum(1, g)
            rowsum(2, d)

    def seg_down():
        cot_in.wait()
        down_in.wait()
        down(0)
        move(cot, out_h)

    def quarter(grad, left, k):
        n = FH // 4
        cols = slice(k * n, (k + 1) * n)
        ys = [nn(left[...], hid[h, :, cols]).astype(BF16) for h in (1, 0)]
        for h, y in zip((1, 0), ys):
            grad[k // 2, h, :, (k % 2) * n : (k % 2 + 1) * n] = y

    def hidden_back(k):
        todo = [(at(2 * k + i, ROWS), h, slice(c * D, (c + 1) * D)) for i in range(2) for h in range(2) for c in range(FH // D)]
        bs = [bg[at(2 * k + i, ROWS), :] for i in range(2)]
        dh = [nt(bs[n // (len(todo) // 2)], wd[h, cs, :]) for n, (_, h, cs) in enumerate(todo)]
        vb = [(d * gp[h, rows, cs].astype(F32)).astype(BF16) for d, (rows, h, cs) in zip(dh, todo)]
        for v, (rows, h, cs) in zip(vb, todo):
            hid[h, rows, cs] = v
        for v, (rows, h, cs) in zip(vb, todo):
            rowsum(3 + 2 * h + cs.start // D, v.astype(F32))

    def first_back(jj):
        both = [slice(i * ROWS, (i + 1) * ROWS) for i in range(tiles)]
        gg = [gs[rows, :] + (nt(hid[0, rows, :], wu[0]) + nt(hid[1, rows, :], wu[1])) for rows in both]
        nns = [n1[rows, :] for rows in both]
        rr = [r1[rows, 0:1] for rows in both]
        ds = []
        for g, n, r in zip(gg, nns, rr):
            e = g * g1
            ds.append(r * (e - mean(e) - n * mean(e * n)))
        bs = [d.astype(BF16) for d in ds]
        ms = [nt(b, wm[...]).astype(BF16) for b in bs]
        for rows, d, b, m in zip(both, ds, bs, ms):
            gs[rows, :] = d
            bg[rows, :] = b
            mg[rows, :] = m
        for g, n, d in zip(gg, nns, ds):
            rowsum(7, g * n)
            rowsum(8, g)
            rowsum(9, d)

    def grad_merge():
        for h in (1, 0):
            gm[h] = nn(mixt[h * (D // 2) : (h + 1) * (D // 2), :], bg[...]).astype(BF16)

    def vectors():
        vs[0] = jnp.zeros(vs.shape[1:], F32)
        for i in range(10):
            vs[0, i : i + 1, :] = jnp.sum(acc[8 * i : 8 * i + 8, :], 0, keepdims=True)

    def attend_back(p, ws):
        zero = jnp.zeros((), BF16)
        first = lane < HEAD
        strips = range(T // C)
        cols = at(p, C)
        both = lambda x: jnp.concatenate([jnp.where(first, x, zero), jnp.where(first, zero, x)], 0)
        cut = lambda x, j, s: x[s * C - span(j)[0] : (s + 1) * C - span(j)[0], :]
        users = [[j for j in strips if span(j)[0] <= s * C < span(j)[1]] for s in strips]
        dps, pts, dds, dvs, kts, qqs, prods, dss, dks, ms = [{} for _ in range(10)]
        for w in ws:
            rows = at(w, T)
            v = trip[p, rows, 2 * C :]
            do = mg[rows, cols]
            q = trip[p, rows, 0:C]
            for j in strips:
                dds[w, j] = both(do[j * C : (j + 1) * C])
                dps[w, j] = nt(v[span(j)[0] : span(j)[1]], dds[w, j])
                pts[w, j] = probs[w, p, strip(j), :]
                qqs[w, j] = both(q[j * C : (j + 1) * C])
            prods[w] = do.T.astype(F32) * mixt[cols, rows].astype(F32)
            kts[w] = trip[p, rows, C : 2 * C].T
        for w in ws:
            for s in strips:
                js = users[s]
                dvs[w, s] = nn(jnp.concatenate([cut(pts[w, j], j, s) for j in js], 1), jnp.concatenate([dds[w, j] for j in js], 0))
            for j in strips:
                ts = slice(j * C, (j + 1) * C)
                ds = []
                for a in range(2):
                    cs = slice(a * C, (a + 1) * C)
                    inner = jnp.sum(prods[w][a * HEAD : (a + 1) * HEAD, ts], 0, keepdims=True)
                    ds.append((pts[w, j][:, cs].astype(F32) * (dps[w, j][:, cs] - inner)).astype(BF16))
                dss[w, j] = jnp.concatenate(ds, 1)
            for j in strips:
                m = nn(kts[w][:, span(j)[0] : span(j)[1]], dss[w, j])
                ms[w, j] = (jnp.concatenate([m[:HEAD, :C], m[HEAD:, C:]], 0) * 0.125).astype(BF16)
            for s in strips:
                js = users[s]
                dks[w, s] = nn(jnp.concatenate([cut(dss[w, j], j, s) for j in js], 1), jnp.concatenate([qqs[w, j] for j in js], 0))
        for w in ws:
            rows = at(w, T)
            dtrip[p, rows, 0:C] = jnp.concatenate([ms[w, j] for j in strips], 1).T
            for s in strips:
                lanes = pl.ds(pl.multiple_of(w * T + s * C, C), C)
                dtrip[p, lanes, C : 2 * C] = dks[w, s].astype(BF16)
                dtrip[p, lanes, 2 * C :] = dvs[w, s].astype(BF16)

    def last(j):
        total = jnp.zeros((ROWS, D), F32)
        for w in range(W):
            rows = pl.ds(pl.multiple_of(w * T + j * ROWS, ROWS), ROWS)
            g = gs[rows, :]
            for p in range(4):
                g += nt(dtrip[p, rows, :], whp[p // 2, p % 2])
            gs[rows, :] = g
            total += g
        gpos[j] = total.astype(BF16)

    def seg_last():
        loop(per, last)
        move(gs, tg_h)

    assert tiles == 4

    def seg_up1():
        vec_y.wait_recv()
        up(1)

    acc[...] = jnp.zeros_like(acc)
    work = {"enter": seg_enter, "merge": lambda: (merge_in.wait(), merge()), "up0": lambda: (up_in.wait(), up(0)), "up1": seg_up1, "down": seg_down}
    work.update({"fb0": lambda: first_back(0), "ait": turn, "gm": grad_merge, "vec": vectors, "last": seg_last})
    for p in range(4):
        work[f"gd{p}"] = lambda p=p: quarter(gd, bgt, p)
        work[f"gu{p}"] = lambda p=p: quarter(gu, nbt, p)
        work[f"qkv{p}"] = lambda p=p: (heads_in[p % 2].wait(), qkv(p // 2, p % 2))
        work[f"att{p}"] = lambda p=p: attend(p, range(W))
        work[f"ab{p}"] = lambda p=p: attend_back(p, range(W))
        work[f"gh{p}"] = lambda p=p: gh.__setitem__((p % 2, p // 2), nn(ait[...], dtrip[p]).astype(BF16))
    for k in range(2):
        work[f"hb{k}"] = lambda k=k: hidden_back(k)
    for name in ORDER:
        if name in work:
            work[name]()
            continue
        try:
            next(steps[name])
        except StopIteration:
            del steps[name]
            if name in ends:
                move(*ends[name])
    for name in list(steps):
        for _ in steps[name]:
            pass
        if name in ends:
            move(*ends[name])
    assert net.count <= recv_sem.shape[0], net.count
    net.finish()
    for copy in local[inward:]:
        copy.wait()


def scratch(R, D, T, FH, dp):
    W = R // T
    V = pltpu.VMEM
    area = strip(T // 128 - 1).stop
    X = max(1, (dp // 16).bit_length() - 1)
    NC, DH = FH // D, D // 2
    extra = (dp // 16).bit_length() - 1
    bufs, copies = [], 7 + extra
    for _, _, a, b, c, d, order in PIECES:
        both, one, more = needs(b - a, order, extra)
        bufs += [V((2, both, d - c), BF16), V((max(one, 16), d - c), BF16)]
        copies += more
    for _, key, _, _, way in FETCH:
        copies += (3 if key[0] == "g" else 1) + {"y": 1, "x": 3, "z": 3, "e": 8}[way]
    assert NC == 2
    return [
        V((R, D), BF16), V((T, D), BF16), V((R, D), BF16), V((2, 2, D, 384), BF16), V((D, D), BF16), V((2, D, FH), BF16),
        V((2, FH, D), BF16), V((2, 8, D), F32),
        V((R, D), BF16), V((D, R), BF16), V((4, R, 384), BF16), V((W, area, 128), F32), V((W, 4, area, 256), BF16),
        V((R, D), BF16), V((D, R), BF16), V((R, D), F32), V((R, 128), F32), V((D, R), BF16),
        V((2, R, FH), BF16), V((2, R, FH), BF16), V((R, D), F32), V((R, D), BF16), V((D, R), BF16),
        V((4, R, 384), BF16), V((80, D), F32),
        V((NC, 2, D, D), BF16), V((NC, 2, D, D), BF16), V((2, DH, D), BF16), V((2, 2, D, 384), BF16), V((2, T // 2, D), BF16),
        V((NC, D, D), BF16), V((NC, D, D), BF16), V((DH, D), BF16), V((2, D, 384), BF16), V((2, T // 2, D), BF16),
        V((5 + (dp // 16).bit_length() - 1, 16, D), F32), V((3 + X, 16, D), F32), V((4, 16, D), F32),
        pltpu.SemaphoreType.DMA((POOL,)), pltpu.SemaphoreType.DMA((copies,)), pltpu.SemaphoreType.DMA((16 + len(PIECES),)),
    ] + bufs


def call(dp, tok, seg, pos, cot, hw, mw, uw, dw, *vecs):
    R, D = tok.shape
    T = pos.shape[0]
    FH = uw.shape[1]
    S = jax.ShapeDtypeStruct
    vm = pl.BlockSpec(memory_space=pltpu.VMEM)
    hb = pl.BlockSpec(memory_space=pl.ANY)
    outs = [
        S((R, D), BF16), S((R, D), F32), S((2, D, D), BF16), S((2, D, D), BF16), S((D // 2, D), BF16),
        S((2, D, 384), BF16), S((2, T // 2, D), BF16), S((16, D), F32),
    ]
    return pl.pallas_call(
        functools.partial(kernel, dp),
        out_shape=outs,
        in_specs=[hb, vm, hb, hb, hb, hb, hb, hb] + [vm] * 7,
        out_specs=[hb] * len(outs),
        scratch_shapes=scratch(R, D, T, FH, dp),
        compiler_params=pltpu.CompilerParams(vmem_limit_bytes=VMEM_LIMIT, collective_id=1, has_side_effects=True),
    )(tok, seg, pos, cot, hw, mw, uw, dw, *vecs)


def widen(out_h, tg_h, fd_h, fu_h, fm_h, fh_h, fp_h, v, out, tg, pg_o, hg_o, gm_o, gu_o, gd_o, mb, g1, s1, ub, db, g2, s2,
          fd, fu, fm, fh, fp, tgv, outv, pg, hg, gm, gu, gd, sem, osem):
    D = fm.shape[1]
    pairs = [(fd_h, fd), (fu_h, fu), (fh_h, fh), (fm_h, fm), (fp_h, fp), (tg_h, tgv), (out_h, outv)]
    ins = [pltpu.make_async_copy(a, b, sem.at[k]) for k, (a, b) in enumerate(pairs)]
    for copy in ins:
        copy.start()
    outs = []

    def leave(src, dst):
        copy = pltpu.make_async_copy(src, dst, osem.at[len(outs)])
        copy.start()
        outs.append(copy)

    for row, o in ((9, mb), (7, g1), (8, s1), (2, db), (0, g2), (1, s2)):
        o[...] = v[row, :]
    for k in range(2):
        ub[k * D : (k + 1) * D] = v[3 + k, :]
    ins[0].wait()
    for c in range(2):
        for r in range(2):
            rows = slice(c * D + r * (D // 2), c * D + (r + 1) * (D // 2))
            gd[rows, :] = fd[c, :, r * (D // 2) : (r + 1) * (D // 2)].T.astype(F32)
        leave(gd.at[c * D : (c + 1) * D], gd_o.at[c * D : (c + 1) * D])
    ins[1].wait()
    for r in range(2):
        rows = slice(r * (D // 2), (r + 1) * (D // 2))
        for c in range(2):
            gu[rows, c * D : (c + 1) * D] = fu[c, rows, :].astype(F32)
        leave(gu.at[rows], gu_o.at[rows])
    ins[2].wait()
    for k in range(3):
        for p in range(2):
            hg[k, :, p * 128 : (p + 1) * 128] = fh[p, :, k * 128 : (k + 1) * 128].astype(F32)
        leave(hg.at[k], hg_o.at[k])
    ins[3].wait()
    gm[...] = fm[...].astype(F32)
    leave(gm, gm_o)
    ins[4].wait()
    for k in range(2):
        rows = slice(k * (D // 2), (k + 1) * (D // 2))
        pg[rows, :] = fp[k].astype(F32)
    leave(pg, pg_o)
    ins[5].wait()
    leave(tgv, tg)
    ins[6].wait()
    leave(outv, out)
    for copy in outs:
        copy.wait()


def finish(out, tg, fd, fu, fm, fh, fp, v):
    D = fm.shape[1]
    half = fm.shape[0]
    S, V = jax.ShapeDtypeStruct, pltpu.VMEM
    shapes = [(2 * half, D), (3, D, half), (half, D), (D, 2 * D), (2 * D, D)]
    hb = pl.BlockSpec(memory_space=pl.ANY)
    vm = pl.BlockSpec(memory_space=pltpu.VMEM)
    return pl.pallas_call(
        widen,
        out_shape=[S(out.shape, BF16), S(tg.shape, F32)] + [S(v, F32) for v in shapes]
        + [S((n,), F32) for n in (D, D, D, 2 * D, D, D, D)],
        in_specs=[hb] * 7 + [vm],
        out_specs=[hb] * 7 + [vm] * 7,
        scratch_shapes=[V(v.shape, BF16) for v in (fd, fu, fm, fh, fp)] + [V(tg.shape, F32), V(out.shape, BF16)] + [V(v, F32) for v in shapes]
        + [pltpu.SemaphoreType.DMA((7,)), pltpu.SemaphoreType.DMA((16,))],
        compiler_params=pltpu.CompilerParams(vmem_limit_bytes=VMEM_LIMIT),
    )(out, tg, fd, fu, fm, fh, fp, v)


def per_device(dp, tok, seg, pos, hw, mw, mb, g1, s1, uw, ub, dw, db, g2, s2, cot):
    out, tg, fd, fu, fm, fh, fp, v = call(dp, tok, seg, pos, cot, hw.transpose(1, 0, 2), mw, uw, dw, mb, g1, s1, db, g2, s2, ub)
    out, tg, pg, gh, gm, gu, gd, *vs = finish(out, tg, fd, fu, fm, fh, fp, v)
    mb, g1, s1, ub, db, g2, s2 = vs
    return (out, tg, pg, gh.transpose(1, 0, 2), gm, mb, g1, s1, gu, ub, gd, db, g2, s2)


def solution(mesh):
    rows = P(("dp", "tensor"), None)
    ins = (rows, P("dp", None), P(), P(None, None, "tensor"), P("tensor", None), P(), P(), P(), P(None, "tensor"), P("tensor"),
           P("tensor", None), P(), P(), P(), rows)
    outs = (rows, rows, P(), P(None, None, "tensor"), P("tensor", None), P(), P(), P(), P(None, "tensor"), P("tensor"),
            P("tensor", None), P(), P(), P())
    return jax.shard_map(
        functools.partial(per_device, mesh.shape["dp"]), mesh=mesh, in_specs=ins, out_specs=outs, check_vma=False
    )
```

```python
import functools
import jax
import jax.numpy as jnp
from jax import lax
from jax.experimental import pallas as pl
from jax.experimental.pallas import tpu as pltpu
from jax.sharding import PartitionSpec as P

F32, BF16 = jnp.float32, jnp.bfloat16
MESH = pl.DeviceIdType.MESH
FETCH = (
    ("wu1", "wu", 0, 256, "y"),
    ("g1", "g1", 0, 512, "e"),
    ("wu0", "wu", 256, 512, "e"),
    ("g00", "g0", 0, 256, "z"),
    ("g01", "g0", 256, 512, "x"),
    ("wm", "wm", 0, 256, "e"),
    ("wd", "wd", 0, 1024, "e"),
)
PIECES = (
    ("d0", "d0", 0, 512, 0, 256, "qab"),
    ("u0", "u0", 0, 512, 0, 256, "qab"),
    ("d1", "d0", 0, 512, 256, 512, "qz"),
    ("u1", "u0", 0, 512, 256, 512, "qab"),
    ("d2", "d1", 0, 512, 0, 256, "qz"),
    ("u2", "u1", 0, 512, 0, 256, "qab"),
    ("d3", "d1", 0, 512, 256, 512, "aqb"),
    ("u3", "u1", 0, 512, 256, 512, "aqb"),
    ("m", "m", 0, 256, 0, 512, "axby"),
    ("p", "p", 0, 256, 0, 512, "pz"),
    ("h0a", "h0", 0, 256, 0, 384, "qz"),
    ("h0b", "h0", 256, 512, 0, 384, "qz"),
    ("h1a", "h1", 0, 256, 0, 384, "yabx"),
    ("h1b", "h1", 256, 512, 0, 384, "ayxb"),
)
ORDER = (
    "g1", "wm", "enter", "g00", "g01", "qkv0", "att0", "wu0", "wd", "g1", "qkv1", "wm", "att1", "ait", "wu1", "g00", "g01", "g1",
    "wu0", "wm", "g00", "g01", "g1", "wd", "g00", "g01", "qkv2", "att2", "g1", "wu0", "wm", "qkv3", "att3", "wm", "merge", "wd",
    "up0", "wu1", "wu0", "wd", "wu1", "wu0", "up1", "wd", "down", "gd2", "d2", "gd3", "d3", "gd1", "d1", "d2", "gd0", "d0", "d3",
    "hb0", "d1", "hb1", "d0", "fb0", "gu3", "u3", "d2", "d3", "u3", "gu2", "u2", "gu1", "u1", "d1", "gm", "m", "u2", "gu0", "u0",
    "u1", "d0", "ab3", "d2", "m", "d3", "u0", "u3", "gh3", "ab1", "d0", "d1", "gh1", "h1a", "h1b", "u2", "ab0", "d2", "h1a",
    "h1b", "ab2", "u1", "m", "d3", "d0", "last", "p", "u2", "u0", "d1", "d2", "u3", "h1b", "h1a", "u1", "m", "p", "gh0", "d2",
    "d3", "d0", "gh2", "h0a", "h0b", "u0", "vec", "v", "d1", "h1a", "h1b", "h0a", "u2", "h0b", "u3", "d1", "u1", "d0", "m", "v",
    "d3", "h1b", "p", "u0", "h1a", "u2", "u3", "h0a", "d3", "u1", "m", "h1b", "d3", "h0b", "u2", "d0", "p", "u0", "h1a", "v",
    "u1", "d0", "u3", "h0a", "m", "h1b", "u2", "h1a", "h0b", "u0", "u2", "u1", "v", "p", "u3", "m", "h1b", "u1", "u3", "h0a",
    "u0", "h1a", "v", "h0b", "u0", "m", "h1b", "m", "h1a", "h0a", "h1b", "p", "h0b", "h1a", "h0a", "p", "h0b",
)
VMEM_LIMIT = 64 * 2**20 - 2**18
POOL = 32
HEAD = 64
ROWS = 256
NEG = -1000000000.0
GELU_A = 0.7978845608028654
GELU_B = GELU_A * 0.044715


def nn(a, b):
    return lax.dot_general(a, b, (((1,), (0,)), ((), ())), preferred_element_type=F32)


def nt(a, b):
    return lax.dot_general(a, b, (((1,), (1,)), ((), ())), preferred_element_type=F32)


def loop(count, body):
    lax.fori_loop(0, count, lambda i, c: (body(i), c)[1], 0)


def at(i, size):
    return pl.ds(pl.multiple_of(i * size, size), size)


def mean(v):
    return jnp.sum(v, -1, keepdims=True) * (1.0 / v.shape[-1])


class Net:
    def __init__(self, send_sem, recv_sem, dp):
        self.send_sem, self.recv_sem, self.slots, self.count = send_sem, recv_sem, [None] * POOL, 0
        i = lax.axis_index("dp")
        self.t = lax.axis_index("tensor")
        self.c = lax.rem(i, 2)
        self.x = lax.rem(i // 2, 2)
        self.z = lax.rem(i // 4, 4)
        self.core = {"dp": i + 1 - 2 * self.c}
        self.xdev = {"dp": i + 2 - 4 * self.x}
        self.ydev = {"tensor": 1 - self.t}
        self.zto = [lax.rem(self.z + s, 4) for s in range(1, 4)]
        self.zdev = [{"dp": i + 4 * (j - self.z)} for j in self.zto]
        self.zpair = {"dp": i + 4 * (1 - 2 * lax.rem(self.z, 2))}
        self.zfar = {"dp": i + 4 * (3 - 2 * self.z)}
        self.zb = self.z // 2
        self.za = lax.rem(self.z, 2) + self.zb - 2 * lax.rem(self.z, 2) * self.zb
        self.e = lax.rem(i // 2, 8)
        self.eto = [lax.rem(self.e + s, 8) for s in range(1, 8)]
        self.edev = [{"dp": i + 2 * (j - self.e)} for j in self.eto]
        self.xydev = {"dp": i + 2 - 4 * self.x, "tensor": 1 - self.t}
        self.extra = []
        step = 16
        while step < dp:
            bit = lax.rem(i // step, 2)
            self.extra.append({"dp": i + step * (1 - 2 * bit)})
            step *= 2

    def everyone(self):
        more = ([self.xydev] if any("p" in o or "q" in o for *_, o in PIECES) else []) + (self.edev if any("8" in o for *_, o in PIECES) else [self.xdev] + self.zdev)
        return [self.core, self.ydev] + more + self.extra

    def greet(self):
        barrier = pltpu.get_barrier_semaphore()
        for device in self.everyone():
            pl.semaphore_signal(barrier, inc=1, device_id=device, device_id_type=MESH)
        pl.semaphore_wait(barrier, len(self.everyone()))

    def send(self, src, dst, device):
        k = self.count
        self.count += 1
        slot = k % POOL
        if self.slots[slot] is not None:
            self.slots[slot].wait_send()
        copy = pltpu.make_async_remote_copy(
            src_ref=src, dst_ref=dst, send_sem=self.send_sem.at[slot], recv_sem=self.recv_sem.at[k],
            device_id=device, device_id_type=MESH,
        )
        copy.start()
        self.slots[slot] = copy
        return copy

    def sent(self, copy):
        for slot, other in enumerate(self.slots):
            if other is copy:
                copy.wait_send()
                self.slots[slot] = None

    def finish(self):
        for copy in self.slots:
            if copy is not None:
                copy.wait_send()


def tri(tb):
    return slice(tb * (tb + 1) // 2 * ROWS, (tb + 1) * (tb + 2) // 2 * ROWS)


def part(base, size):
    return pl.ds(pl.multiple_of(base, size), size)


def fetch_direct(net, push, oth):
    half = oth.shape[0] // 2
    r = part(net.c * half, half)
    ys = push(r)
    yield
    for y in ys:
        y.wait_recv()
    c = net.send(oth.at[r], oth.at[r], net.core)
    yield
    c.wait_recv()


def fetch_shared(net, push, oth, along):
    q = oth.shape[0] // 4
    bit, device = (net.x, net.xdev) if along == "x" else (lax.rem(net.z, 2), net.zpair)
    a = part((2 * net.c + bit) * q, q)
    b = part((2 * net.c + 1 - bit) * q, q)
    ys = push(a)
    yield
    for y in ys:
        y.wait_recv()
    x = net.send(oth.at[a], oth.at[a], device)
    c0 = net.send(oth.at[a], oth.at[a], net.core)
    yield
    x.wait_recv()
    c1 = net.send(oth.at[b], oth.at[b], net.core)
    yield
    c0.wait_recv()
    c1.wait_recv()


def fetch_plane(net, push, oth):
    q = oth.shape[0] // 8
    z = lax.rem(net.z, 2)
    start = lambda x, z: (4 * net.c + 2 * x + z) * q
    mine, by_x, by_z = start(net.x, z), start(1 - net.x, z), start(net.x, 1 - z)
    ys = push(part(mine, q))
    yield
    for y in ys:
        y.wait_recv()
    again = lambda base, size, device: net.send(oth.at[part(base, size)], oth.at[part(base, size)], device)
    x1, z1 = again(mine, q, net.xdev), again(mine, q, net.zpair)
    cores = [again(mine, q, net.core)]
    yield
    x1.wait_recv()
    z1.wait_recv()
    z2 = again(by_x, q // 2, net.zpair)
    x2 = again(by_z + q // 2, q // 2, net.xdev)
    cores += [again(by_x, q, net.core), again(by_z, q, net.core)]
    yield
    x2.wait_recv()
    z2.wait_recv()
    cores.append(again(start(1 - net.x, 1 - z), q, net.core))
    yield
    for core in cores:
        core.wait_recv()


class Ready:
    def __init__(self, *copies):
        self.copies = list(copies)

    def wait(self):
        for copy in self.copies:
            copy.wait()
        self.copies = []


def needs(rows, order, extra):
    size, halves, both, one = rows // 2, 2, rows // 2, 0
    copies = 2 + extra
    for stage in order:
        count = {"x": 2, "a": 2, "b": 2, "z": 4, "8": 8}.get(stage, 1)
        if stage in "pq":
            size, halves = size // 2, 1
            one += 3 * size
            copies += 6 if stage == "p" else 4
            copies += stage == "p"
        elif stage == "y":
            halves = 1
            one += size
            copies += 1
        else:
            size //= count
            if halves == 2:
                both += (count - 1) * size
            else:
                one += (count - 1) * size
            copies += 2 * (count - 1)
    return both, one + extra * size, copies


class Arrival:
    def __init__(self, copy):
        self.copy, self.open = copy, True

    def wait(self):
        if self.open:
            self.copy.wait_recv()
        self.open = False


def reduce(net, g, own, buf_both, buf_one, fin, order):
    rows = g.shape[1]
    oth = 1 - own
    used = {2: 0, 1: 0}
    pending = {0: [], 1: []}

    def take(k, halves=1):
        used[halves] += k
        rows = slice(used[halves] - k, used[halves])
        return buf_both.at[:, rows] if halves == 2 else buf_one.at[rows]

    def post_both(base, size, device):
        dst = take(size, 2)
        arrival = Arrival(net.send(g.at[:, part(base, size)], dst, device))
        for h in (own, oth):
            pending[h is oth].append((arrival, dst.at[h]))

    def post(h, base, size, device):
        dst = take(size)
        pending[False].append((Arrival(net.send(g.at[h, part(base, size)], dst, device)), dst))

    def settle(h, base, size, to=None):
        here = part(base, size)
        total = g[h, here, :].astype(F32)
        for arrival, dst in pending[h is oth]:
            arrival.wait()
            total = total + dst[...].astype(F32)
        pending[h is oth] = []
        if to is None:
            g[h, here, :] = total.astype(BF16)
        else:
            to[here, :] = total.astype(BF16)

    size = rows // 2
    base = net.c * size
    both = True
    post_both((1 - net.c) * size, size, net.core)
    yield
    history = []
    for stage in order:
        history.append((stage, base, size))
        if both:
            settle(oth, base, size)
        if stage == "y":
            post(oth, base, size, net.ydev)
            both = False
        elif stage in "pq":
            settle(own, base, size)
            size //= 2
            near, far = base + net.x * size, base + (1 - net.x) * size
            post(oth, far, size, net.xydev)
            post(oth, near, size, net.ydev)
            post(own, far, size, net.xdev)
            base, both = near, False
        else:
            settle(own, base, size)
            count, to, devices, place = {"x": (2, [1 - net.x], [net.xdev], net.x), "z": (4, net.zto, net.zdev, net.z),
                                         "a": (2, [1 - net.za], [net.zpair], net.za), "b": (2, [1 - net.zb], [net.zfar], net.zb),
                                         "8": (8, net.eto, net.edev, net.e)}[stage]
            size //= count
            for j, device in zip(to, devices):
                if both:
                    post_both(base + j * size, size, device)
                else:
                    post(own, base + j * size, size, device)
            base = base + place * size
        yield
    last = fin.at[own] if len(fin.shape) == 3 else fin
    settle(own, base, size, last)
    here = part(base, size)
    for device in net.extra:
        dst = take(size)
        copy = net.send(last.at[here], dst, device)
        yield
        copy.wait_recv()
        net.sent(copy)
        last[here, :] = (last[here, :].astype(F32) + dst[...].astype(F32)).astype(BF16)
    whole = [last]
    for stage, base, size in reversed(history):
        if stage == "y":
            continue
        devices = {"x": [net.xdev], "z": net.zdev, "a": [net.zpair], "b": [net.zfar], "8": net.edev, "q": [net.xdev],
                   "p": [net.xydev, net.ydev, net.xdev]}[stage]
        copies = [net.send(last.at[here], last.at[here], device) for device in devices]
        yield
        for copy in copies:
            copy.wait_recv()
        here = part(base, size)
        if stage == "p":
            whole = [fin.at[own], fin.at[oth]]
    copies = [net.send(f.at[here], f.at[here], net.core) for f in whole]
    yield
    for copy in copies:
        copy.wait_recv()


def reduce_vectors(net, vs, vr, vz):
    c = net.send(vs.at[0], vr.at[0], net.core)
    yield
    c.wait_recv()
    vs[1] = vs[0] + vr[0]
    x = net.send(vs.at[1], vr.at[1], net.xdev)
    yield
    x.wait_recv()
    vs[2] = vs[1] + vr[1]
    vz[net.z] = vs[2]
    zs = [net.send(vs.at[2], vz.at[net.z], device) for device in net.zdev]
    yield
    for z in zs:
        z.wait_recv()
    vs[3] = (vz[0] + vz[1]) + (vz[2] + vz[3])
    k = 3
    for b, device in enumerate(net.extra):
        e = net.send(vs.at[k], vr.at[3 + b], device)
        yield
        e.wait_recv()
        vs[k + 1] = vs[k] + vr[3 + b]
        k += 1
    y = net.send(vs.at[k], vr.at[2], net.ydev)
    yield
    y.wait_recv()
    vs[k + 1] = vs[k] + vr[2]
    vs[k + 1, 3:5, :] = vs[k, 3:5, :] + vr[2, 5:7, :]


REACH = 256


def span(j):
    return max(0, (j + 1) * 128 - REACH - 128), (j + 1) * 128


def strip(j):
    start = sum(span(i)[1] - span(i)[0] for i in range(j))
    return slice(start, start + span(j)[1] - span(j)[0])


def kernel(
    dp,
    tok_h, seg, pos_h, cot_h, hw, mw, uw, dw, v0, v1, v2, v3, v4, v5, v6,
    out_h, tg_h, fd_h, fu_h, fm_h, fh_h, fp_h, vg_h,
    tok, pos, cot, whp, wm, wu, wd, vec,
    ai, ait, trip, bias, probs, mix, mixt, n1, r1, nbt, hid, gp, gs, bg, bgt, dtrip, acc,
    gd, gu, gm, gh, gpos, fd, fu, fm, fh, fp, vs, vr, vz,
    send_sem, recv_sem, local_sem, *bufs,
):
    R, D = tok.shape
    T = pos.shape[0]
    W = R // T
    FH = wu.shape[2]
    C = 128
    tiles = R // ROWS
    per = T // ROWS
    lane = lax.broadcasted_iota(jnp.int32, (1, C), 1)
    nb, mg = ai, mix
    net = Net(send_sem, recv_sem, dp)
    t_id = net.t
    local = []

    def move(src, dst):
        copy = pltpu.make_async_copy(src, dst, local_sem.at[len(local)])
        copy.start()
        local.append(copy)
        return copy

    heads_in = [
        Ready(*[move(hw.at[c, :, p * C : (p + 1) * C], whp.at[0, p, :, c * C : (c + 1) * C]) for c in range(3)])
        for p in range(2)
    ]
    rows_in = Ready(move(tok_h, tok), move(pos_h, pos))
    merge_in, up_in, down_in = Ready(move(mw, wm.at[0 : D // 2])), Ready(move(uw, wu.at[0])), Ready(move(dw, wd.at[0]))
    cot_in = Ready(move(cot_h, cot))
    inward = len(local)
    net.greet()
    for k, v in enumerate((v0, v1, v2, v3, v4, v5)):
        vec[0, k : k + 1, :] = v[...].astype(F32).reshape(1, D)
    for k in range(FH // D):
        vec[0, 6 + k : 7 + k, :] = v6[k * D : (k + 1) * D].astype(F32).reshape(1, D)
    mb, g1, s1, db, g2, s2 = [vec[0, i : i + 1, :] for i in range(6)]
    vec_y = net.send(vec.at[0], vec.at[1], net.ydev)

    def head_push(p, r0):
        def push(r):
            r = pl.ds(pl.multiple_of(r.start + r0, 16), r.size)
            return [
                net.send(hw.at[c, r, p * C : (p + 1) * C], whp.at[1, p, r, c * C : (c + 1) * C], net.ydev) for c in range(3)
            ]

        return push

    def row_push(own, oth, r0):
        def push(r):
            r = pl.ds(pl.multiple_of(r.start + r0, 16), r.size)
            return [net.send(own.at[r], oth.at[r], net.ydev)]

        return push

    steps = {}
    half = D // 2
    weights = {"wm": (mw, wm.at[half : 2 * half]), "wu": (uw, wu.at[1]), "wd": (dw, wd.at[1])}
    for name, key, r0, r1_, way in FETCH:
        if key in weights:
            own, oth = weights[key]
            push, oth = row_push(own, oth, r0), oth.at[r0:r1_]
        else:
            push, oth = head_push(int(key[1]), r0), whp.at[1, int(key[1]), r0:r1_]
        if way == "y":
            steps[name] = fetch_direct(net, push, oth)
        elif way == "e":
            steps[name] = fetch_plane(net, push, oth)
        else:
            steps[name] = fetch_shared(net, push, oth, way)
    whole = {"m": (gm, fm, fm_h), "p": (gpos, fp, fp_h)}
    for k in range(2):
        whole[f"d{k}"] = (gd.at[k], fd.at[k], fd_h.at[k])
        whole[f"u{k}"] = (gu.at[k], fu.at[k], fu_h.at[k])
        whole[f"h{k}"] = (gh.at[k], fh.at[k], fh_h.at[k])
    ends = {"v": (vs.at[vs.shape[0] - 1], vg_h)}
    for (name, key, r0, r1_, c0, c1, order), buf_both, buf_one in zip(PIECES, bufs[::2], bufs[1::2]):
        g, f, f_h = whole[key]
        if key != "p":
            g, f, f_h = g.at[:, r0:r1_, c0:c1], f.at[r0:r1_, c0:c1], f_h.at[r0:r1_, c0:c1]
        steps[name] = reduce(net, g, t_id if key == "p" else 0, buf_both, buf_one, f, order)
        ends[name] = (f, f_h)
    steps["v"] = reduce_vectors(net, vs, vr, vz)
    def enter(j):
        rows = at(j, ROWS)
        x = tok[rows, :].astype(F32) + pos[at(lax.rem(j, per), ROWS), :].astype(F32)
        xb = x.astype(BF16)
        ai[rows, :] = xb

    def turn():
        for j in range(tiles):
            rows = slice(j * ROWS, (j + 1) * ROWS)
            ait[:, rows] = ai[rows, :].T

    def seg_enter():
        rows_in.wait()
        loop(tiles, enter)
        masks()

    def qkv(h, p):
        every = [slice(j * ROWS, (j + 1) * ROWS) for j in range(tiles)]
        ys = [nn(ai[rows, :], whp[h, p]).astype(BF16) for rows in every]
        for rows, y in zip(every, ys):
            trip[2 * h + p, rows, 0:C] = y[:, 0:C] * 0.125
            trip[2 * h + p, rows, C:] = y[:, C:]

    def masks():
        for w in range(W):
            row = seg[pl.ds(t_id * W + w, 1), :].astype(F32)
            col = jnp.broadcast_to(row, (C, T)).T
            for j in range(T // C):
                lo, hi = span(j)
                s_id = lax.broadcasted_iota(jnp.int32, (hi - lo, C), 0) + lo
                l_id = lax.broadcasted_iota(jnp.int32, (hi - lo, C), 1) + j * C
                ok = (col[lo:hi] == row[:, j * C : (j + 1) * C]) & (s_id <= l_id)
                bias[w, strip(j), :] = jnp.where(ok, 0.0, NEG)

    def attend(p, ws):
        zero = jnp.zeros((), BF16)
        first = lane < HEAD
        strips = range(T // C)
        cols = at(p, C)
        ss, bs, vts, ms, pts = {}, {}, {}, {}, {}
        for w in ws:
            rows = at(w, T)
            q = trip[p, rows, 0:C]
            k = trip[p, rows, C : 2 * C]
            for j in strips:
                lo, hi = span(j)
                qj = q[j * C : (j + 1) * C]
                ss[w, j] = nt(k[lo:hi], jnp.concatenate([jnp.where(first, qj, zero), jnp.where(first, zero, qj)], 0))
                bs[w, j] = bias[w, strip(j), :]
            vts[w] = trip[p, rows, 2 * C :].T
        for w in ws:
            for j in strips:
                halves = []
                for a in range(2):
                    v = ss[w, j][:, a * C : (a + 1) * C] + bs[w, j]
                    e = jnp.exp(v - jnp.max(v, 0, keepdims=True))
                    halves.append((e * (1.0 / jnp.sum(e, 0, keepdims=True))).astype(BF16))
                pts[w, j] = jnp.concatenate(halves, 1)
            for j in strips:
                lo, hi = span(j)
                m = nn(vts[w][:, lo:hi], pts[w, j])
                ms[w, j] = jnp.concatenate([m[:HEAD, :C], m[HEAD:, C:]], 0).astype(BF16)
        for w in ws:
            rows = at(w, T)
            for j in strips:
                probs[w, p, strip(j), :] = pts[w, j]
            m = jnp.concatenate([ms[w, j] for j in strips], 1)
            mixt[cols, rows] = m
            mix[rows, cols] = m.T

    def rowsum(i, v):
        acc[pl.ds(8 * i, 8), :] += jnp.sum(v.reshape(-1, 8, v.shape[-1]), 0)

    def merge():
        both = [slice(i * ROWS, (i + 1) * ROWS) for i in range(tiles)]
        xs = [
            tok[rows, :].astype(F32) + pos[(i % per) * ROWS : (i % per + 1) * ROWS, :].astype(F32) + mb for i, rows in enumerate(both)
        ]
        fs = [x + nn(mix[rows, :], wm[...]) for x, rows in zip(xs, both)]
        zs = [f - mean(f) for f in fs]
        rs = [lax.rsqrt(mean(z * z) + 1e-5) for z in zs]
        ns = [z * r for z, r in zip(zs, rs)]
        ys = [(n * g1 + s1).astype(BF16) for n in ns]
        for rows, n, r, y in zip(both, ns, rs, ys):
            n1[rows, :] = n
            r1[rows, :] = jnp.broadcast_to(r, (ROWS, 128))
            nb[rows, :] = y
            nbt[:, rows] = y.T

    def up(h):
        def body(jj):
            units = [(at(1 * jj + i, ROWS), slice(c * D // 2, (c + 1) * D // 2)) for i in range(1) for c in range(2 * FH // D)]
            xs = {i: nb[at(1 * jj + i, ROWS), :] for i in range(1)}
            ws = [wu[h, :, c * D // 2 : (c + 1) * D // 2] for c in range(2 * FH // D)]
            bs = [vec[h, 6 + c // 2 : 7 + c // 2, c % 2 * D // 2 : c % 2 * D // 2 + D // 2] for c in range(2 * FH // D)]
            n = 2 * FH // D
            vs, hs, ps = {}, [], []

            def act(v):
                v2 = v * v
                th = jnp.tanh(v * (GELU_A + GELU_B * v2))
                half = 0.5 + 0.5 * th
                hv = v * half
                hs.append(hv.astype(BF16))
                ps.append((half + hv * (1.0 - th) * (GELU_A + 3.0 * GELU_B * v2)).astype(BF16))

            for k in range(len(units) + 1):
                if k < len(units):
                    vs[k] = nn(xs[k // n], ws[k % n]) + bs[k % n]
                if k >= 1:
                    act(vs[k - 1])
            for (rows, cs), hv, pv in zip(units, hs, ps):
                hid[h, rows, cs] = hv
                gp[h, rows, cs] = pv

        loop(tiles, body)

    def down(jj):
        both = [at(2 * jj + i, ROWS) for i in range(2)]
        gvs = [cot[rows, :] for rows in both]
        fs = [n1[rows, :] * g1 + (s1 + db) + (nn(hid[0, rows, :], wd[0]) + nn(hid[1, rows, :], wd[1])) for rows in both]
        todo = []
        for rows, f, g in zip(both, fs, gvs):
            z = f - mean(f)
            r = lax.rsqrt(mean(z * z) + 1e-5)
            n2 = z * r
            g = g.astype(F32)
            e = g * g2
            d = r * (e - mean(e) - n2 * mean(e * n2))
            todo.append((rows, (n2 * g2 + s2).astype(BF16), d, d.astype(BF16), g * n2, g))
        for rows, o, d, b, _, _ in todo:
            cot[rows, :] = o
            gs[rows, :] = d
            bg[rows, :] = b
            bgt[:, rows] = b.T
        for _, _, d, _, gn, g in todo:
            rowsum(0, gn)
            rowsum(1, g)
            rowsum(2, d)

    def seg_down():
        cot_in.wait()
        down_in.wait()
        loop(tiles // 2, down)
        move(cot, out_h)

    def quarter(grad, left, k):
        n = FH // 4
        cols = slice(k * n, (k + 1) * n)
        ys = [nn(left[...], hid[h, :, cols]).astype(BF16) for h in (1, 0)]
        for h, y in zip((1, 0), ys):
            grad[k // 2, h, :, (k % 2) * n : (k % 2 + 1) * n] = y

    def hidden_back(k):
        todo = [(at(2 * k + i, ROWS), h, slice(c * D, (c + 1) * D)) for i in range(2) for h in range(2) for c in range(FH // D)]
        bs = [bg[at(2 * k + i, ROWS), :] for i in range(2)]
        dh = [nt(bs[n // (len(todo) // 2)], wd[h, cs, :]) for n, (_, h, cs) in enumerate(todo)]
        vb = [(d * gp[h, rows, cs].astype(F32)).astype(BF16) for d, (rows, h, cs) in zip(dh, todo)]
        for v, (rows, h, cs) in zip(vb, todo):
            hid[h, rows, cs] = v
        for v, (rows, h, cs) in zip(vb, todo):
            rowsum(3 + 2 * h + cs.start // D, v.astype(F32))

    def first_back(jj):
        both = [slice(i * ROWS, (i + 1) * ROWS) for i in range(tiles)]
        gg = [gs[rows, :] + (nt(hid[0, rows, :], wu[0]) + nt(hid[1, rows, :], wu[1])) for rows in both]
        nns = [n1[rows, :] for rows in both]
        rr = [r1[rows, 0:1] for rows in both]
        ds = []
        for g, n, r in zip(gg, nns, rr):
            e = g * g1
            ds.append(r * (e - mean(e) - n * mean(e * n)))
        bs = [d.astype(BF16) for d in ds]
        ms = [nt(b, wm[...]).astype(BF16) for b in bs]
        for rows, d, b, m in zip(both, ds, bs, ms):
            gs[rows, :] = d
            bg[rows, :] = b
            mg[rows, :] = m
        for g, n, d in zip(gg, nns, ds):
            rowsum(7, g * n)
            rowsum(8, g)
            rowsum(9, d)

    def grad_merge():
        for h in (1, 0):
            gm[h] = nn(mixt[h * (D // 2) : (h + 1) * (D // 2), :], bg[...]).astype(BF16)

    def vectors():
        vs[0] = jnp.zeros(vs.shape[1:], F32)
        for i in range(10):
            vs[0, i : i + 1, :] = jnp.sum(acc[8 * i : 8 * i + 8, :], 0, keepdims=True)

    def attend_back(p, ws):
        zero = jnp.zeros((), BF16)
        first = lane < HEAD
        strips = range(T // C)
        cols = at(p, C)
        both = lambda x: jnp.concatenate([jnp.where(first, x, zero), jnp.where(first, zero, x)], 0)
        cut = lambda x, j, s: x[s * C - span(j)[0] : (s + 1) * C - span(j)[0], :]
        users = [[j for j in strips if span(j)[0] <= s * C < span(j)[1]] for s in strips]
        dps, pts, dds, dvs, kts, qqs, prods, dss, dks, ms = [{} for _ in range(10)]
        for w in ws:
            rows = at(w, T)
            v = trip[p, rows, 2 * C :]
            do = mg[rows, cols]
            q = trip[p, rows, 0:C]
            for j in strips:
                dds[w, j] = both(do[j * C : (j + 1) * C])
                dps[w, j] = nt(v[span(j)[0] : span(j)[1]], dds[w, j])
                pts[w, j] = probs[w, p, strip(j), :]
                qqs[w, j] = both(q[j * C : (j + 1) * C])
            prods[w] = do.T.astype(F32) * mixt[cols, rows].astype(F32)
            kts[w] = trip[p, rows, C : 2 * C].T
        for w in ws:
            for s in strips:
                js = users[s]
                dvs[w, s] = nn(jnp.concatenate([cut(pts[w, j], j, s) for j in js], 1), jnp.concatenate([dds[w, j] for j in js], 0))
            for j in strips:
                ts = slice(j * C, (j + 1) * C)
                ds = []
                for a in range(2):
                    cs = slice(a * C, (a + 1) * C)
                    inner = jnp.sum(prods[w][a * HEAD : (a + 1) * HEAD, ts], 0, keepdims=True)
                    ds.append((pts[w, j][:, cs].astype(F32) * (dps[w, j][:, cs] - inner)).astype(BF16))
                dss[w, j] = jnp.concatenate(ds, 1)
            for j in strips:
                m = nn(kts[w][:, span(j)[0] : span(j)[1]], dss[w, j])
                ms[w, j] = (jnp.concatenate([m[:HEAD, :C], m[HEAD:, C:]], 0) * 0.125).astype(BF16)
            for s in strips:
                js = users[s]
                dks[w, s] = nn(jnp.concatenate([cut(dss[w, j], j, s) for j in js], 1), jnp.concatenate([qqs[w, j] for j in js], 0))
        for w in ws:
            rows = at(w, T)
            dtrip[p, rows, 0:C] = jnp.concatenate([ms[w, j] for j in strips], 1).T
            for s in strips:
                lanes = pl.ds(pl.multiple_of(w * T + s * C, C), C)
                dtrip[p, lanes, C : 2 * C] = dks[w, s].astype(BF16)
                dtrip[p, lanes, 2 * C :] = dvs[w, s].astype(BF16)

    def last(j):
        total = jnp.zeros((ROWS, D), F32)
        for w in range(W):
            rows = pl.ds(pl.multiple_of(w * T + j * ROWS, ROWS), ROWS)
            g = gs[rows, :]
            for p in range(4):
                g += nt(dtrip[p, rows, :], whp[p // 2, p % 2])
            gs[rows, :] = g
            total += g
        gpos[j] = total.astype(BF16)

    def seg_last():
        loop(per, last)
        move(gs, tg_h)

    assert tiles == 4

    def seg_up1():
        vec_y.wait_recv()
        up(1)

    acc[...] = jnp.zeros_like(acc)
    work = {"enter": seg_enter, "merge": lambda: (merge_in.wait(), merge()), "up0": lambda: (up_in.wait(), up(0)), "up1": seg_up1, "down": seg_down}
    work.update({"fb0": lambda: first_back(0), "ait": turn, "gm": grad_merge, "vec": vectors, "last": seg_last})
    for p in range(4):
        work[f"gd{p}"] = lambda p=p: quarter(gd, bgt, p)
        work[f"gu{p}"] = lambda p=p: quarter(gu, nbt, p)
        work[f"qkv{p}"] = lambda p=p: (heads_in[p % 2].wait(), qkv(p // 2, p % 2))
        work[f"att{p}"] = lambda p=p: attend(p, range(W))
        work[f"ab{p}"] = lambda p=p: attend_back(p, range(W))
        work[f"gh{p}"] = lambda p=p: gh.__setitem__((p % 2, p // 2), nn(ait[...], dtrip[p]).astype(BF16))
    for k in range(2):
        work[f"hb{k}"] = lambda k=k: hidden_back(k)
    for name in ORDER:
        if name in work:
            work[name]()
            continue
        try:
            next(steps[name])
        except StopIteration:
            del steps[name]
            if name in ends:
                move(*ends[name])
    for name in list(steps):
        for _ in steps[name]:
            pass
        if name in ends:
            move(*ends[name])
    assert net.count <= recv_sem.shape[0], net.count
    net.finish()
    for copy in local[inward:]:
        copy.wait()


def scratch(R, D, T, FH, dp):
    W = R // T
    V = pltpu.VMEM
    area = strip(T // 128 - 1).stop
    X = max(1, (dp // 16).bit_length() - 1)
    NC, DH = FH // D, D // 2
    extra = (dp // 16).bit_length() - 1
    bufs, copies = [], 7 + extra
    for _, _, a, b, c, d, order in PIECES:
        both, one, more = needs(b - a, order, extra)
        bufs += [V((2, both, d - c), BF16), V((max(one, 16), d - c), BF16)]
        copies += more
    for _, key, _, _, way in FETCH:
        copies += (3 if key[0] == "g" else 1) + {"y": 1, "x": 3, "z": 3, "e": 8}[way]
    assert NC == 2
    return [
        V((R, D), BF16), V((T, D), BF16), V((R, D), BF16), V((2, 2, D, 384), BF16), V((D, D), BF16), V((2, D, FH), BF16),
        V((2, FH, D), BF16), V((2, 8, D), F32),
        V((R, D), BF16), V((D, R), BF16), V((4, R, 384), BF16), V((W, area, 128), F32), V((W, 4, area, 256), BF16),
        V((R, D), BF16), V((D, R), BF16), V((R, D), F32), V((R, 128), F32), V((D, R), BF16),
        V((2, R, FH), BF16), V((2, R, FH), BF16), V((R, D), F32), V((R, D), BF16), V((D, R), BF16),
        V((4, R, 384), BF16), V((80, D), F32),
        V((NC, 2, D, D), BF16), V((NC, 2, D, D), BF16), V((2, DH, D), BF16), V((2, 2, D, 384), BF16), V((2, T // 2, D), BF16),
        V((NC, D, D), BF16), V((NC, D, D), BF16), V((DH, D), BF16), V((2, D, 384), BF16), V((2, T // 2, D), BF16),
        V((5 + (dp // 16).bit_length() - 1, 16, D), F32), V((3 + X, 16, D), F32), V((4, 16, D), F32),
        pltpu.SemaphoreType.DMA((POOL,)), pltpu.SemaphoreType.DMA((copies,)), pltpu.SemaphoreType.DMA((16 + len(PIECES),)),
    ] + bufs


def call(dp, tok, seg, pos, cot, hw, mw, uw, dw, *vecs):
    R, D = tok.shape
    T = pos.shape[0]
    FH = uw.shape[1]
    S = jax.ShapeDtypeStruct
    vm = pl.BlockSpec(memory_space=pltpu.VMEM)
    hb = pl.BlockSpec(memory_space=pl.ANY)
    outs = [
        S((R, D), BF16), S((R, D), F32), S((2, D, D), BF16), S((2, D, D), BF16), S((D // 2, D), BF16),
        S((2, D, 384), BF16), S((2, T // 2, D), BF16), S((16, D), F32),
    ]
    return pl.pallas_call(
        functools.partial(kernel, dp),
        out_shape=outs,
        in_specs=[hb, vm, hb, hb, hb, hb, hb, hb] + [vm] * 7,
        out_specs=[hb] * len(outs),
        scratch_shapes=scratch(R, D, T, FH, dp),
        compiler_params=pltpu.CompilerParams(vmem_limit_bytes=VMEM_LIMIT, collective_id=1, has_side_effects=True),
    )(tok, seg, pos, cot, hw, mw, uw, dw, *vecs)


def widen(out_h, tg_h, fd_h, fu_h, fm_h, fh_h, fp_h, v, out, tg, pg_o, hg_o, gm_o, gu_o, gd_o, mb, g1, s1, ub, db, g2, s2,
          fd, fu, fm, fh, fp, tgv, outv, pg, hg, gm, gu, gd, sem, osem):
    D = fm.shape[1]
    pairs = [(fd_h, fd), (fu_h, fu), (fh_h, fh), (fm_h, fm), (fp_h, fp), (tg_h, tgv), (out_h, outv)]
    ins = [pltpu.make_async_copy(a, b, sem.at[k]) for k, (a, b) in enumerate(pairs)]
    for copy in ins:
        copy.start()
    outs = []

    def leave(src, dst):
        copy = pltpu.make_async_copy(src, dst, osem.at[len(outs)])
        copy.start()
        outs.append(copy)

    for row, o in ((9, mb), (7, g1), (8, s1), (2, db), (0, g2), (1, s2)):
        o[...] = v[row, :]
    for k in range(2):
        ub[k * D : (k + 1) * D] = v[3 + k, :]
    ins[0].wait()
    for c in range(2):
        for r in range(2):
            rows = slice(c * D + r * (D // 2), c * D + (r + 1) * (D // 2))
            gd[rows, :] = fd[c, :, r * (D // 2) : (r + 1) * (D // 2)].T.astype(F32)
        leave(gd.at[c * D : (c + 1) * D], gd_o.at[c * D : (c + 1) * D])
    ins[1].wait()
    for r in range(2):
        rows = slice(r * (D // 2), (r + 1) * (D // 2))
        for c in range(2):
            gu[rows, c * D : (c + 1) * D] = fu[c, rows, :].astype(F32)
        leave(gu.at[rows], gu_o.at[rows])
    ins[2].wait()
    for k in range(3):
        for p in range(2):
            hg[k, :, p * 128 : (p + 1) * 128] = fh[p, :, k * 128 : (k + 1) * 128].astype(F32)
        leave(hg.at[k], hg_o.at[k])
    ins[3].wait()
    gm[...] = fm[...].astype(F32)
    leave(gm, gm_o)
    ins[4].wait()
    for k in range(2):
        rows = slice(k * (D // 2), (k + 1) * (D // 2))
        pg[rows, :] = fp[k].astype(F32)
    leave(pg, pg_o)
    ins[5].wait()
    leave(tgv, tg)
    ins[6].wait()
    leave(outv, out)
    for copy in outs:
        copy.wait()


def finish(out, tg, fd, fu, fm, fh, fp, v):
    D = fm.shape[1]
    half = fm.shape[0]
    S, V = jax.ShapeDtypeStruct, pltpu.VMEM
    shapes = [(2 * half, D), (3, D, half), (half, D), (D, 2 * D), (2 * D, D)]
    hb = pl.BlockSpec(memory_space=pl.ANY)
    vm = pl.BlockSpec(memory_space=pltpu.VMEM)
    return pl.pallas_call(
        widen,
        out_shape=[S(out.shape, BF16), S(tg.shape, F32)] + [S(v, F32) for v in shapes]
        + [S((n,), F32) for n in (D, D, D, 2 * D, D, D, D)],
        in_specs=[hb] * 7 + [vm],
        out_specs=[hb] * 7 + [vm] * 7,
        scratch_shapes=[V(v.shape, BF16) for v in (fd, fu, fm, fh, fp)] + [V(tg.shape, F32), V(out.shape, BF16)] + [V(v, F32) for v in shapes]
        + [pltpu.SemaphoreType.DMA((7,)), pltpu.SemaphoreType.DMA((16,))],
        compiler_params=pltpu.CompilerParams(vmem_limit_bytes=VMEM_LIMIT),
    )(out, tg, fd, fu, fm, fh, fp, v)


def per_device(dp, tok, seg, pos, hw, mw, mb, g1, s1, uw, ub, dw, db, g2, s2, cot):
    out, tg, fd, fu, fm, fh, fp, v = call(dp, tok, seg, pos, cot, hw.transpose(1, 0, 2), mw, uw, dw, mb, g1, s1, db, g2, s2, ub)
    out, tg, pg, gh, gm, gu, gd, *vs = finish(out, tg, fd, fu, fm, fh, fp, v)
    mb, g1, s1, ub, db, g2, s2 = vs
    return (out, tg, pg, gh.transpose(1, 0, 2), gm, mb, g1, s1, gu, ub, gd, db, g2, s2)


def solution(mesh):
    rows = P(("dp", "tensor"), None)
    ins = (rows, P("dp", None), P(), P(None, None, "tensor"), P("tensor", None), P(), P(), P(), P(None, "tensor"), P("tensor"),
           P("tensor", None), P(), P(), P(), rows)
    outs = (rows, rows, P(), P(None, None, "tensor"), P("tensor", None), P(), P(), P(), P(None, "tensor"), P("tensor"),
            P("tensor", None), P(), P(), P())
    return jax.shard_map(
        functools.partial(per_device, mesh.shape["dp"]), mesh=mesh, in_specs=ins, out_specs=outs, check_vma=False
    )
```
